32 devices in a mesh: dp: 16 (over z, y, core), mp: 2 (over x).
Axes of the slice: x: 2, y: 2, z: 4, core: 2. Of those that a mesh axis runs over, the one named last changes fastest.
Arguments:
- tokens: bfloat16 [32, 1024, 768], P('dp', 'mp'), may hold values from -6 to 6
- memory: bfloat16 [32, 1024, 768], P('dp', 'mp'), may hold values from -6 to 6
- doc_lengths: int32 [32, 3], P('dp'), may hold values from 1 to 895, as said below
- mem_lengths: int32 [32], P('dp'), may hold values from 513 to 1024
- norm_gains: float32 [3, 768], replicated, may hold values from 0.1 to 1.9
- rel_table: float32 [32, 12], replicated, may hold values from -4 to 4
- self_proj: bfloat16 [3, 768, 768], P(None, 'dp', 'mp'), may hold values from -0.109375 to 0.109375
- self_out: bfloat16 [768, 768], P('mp', 'dp'), may hold values from -1.75 to 1.75
- cross_proj: bfloat16 [3, 768, 768], P(None, 'dp', 'mp'), may hold values from -0.109375 to 0.109375
- cross_out: bfloat16 [768, 768], P('mp', 'dp'), may hold values from -1.75 to 1.75
- ffn_proj: bfloat16 [2, 768, 2048], P(None, 'dp', 'mp'), may hold values from -0.21875 to 0.21875
- ffn_out: bfloat16 [2048, 768], P('mp', 'dp'), may hold values from -0.125 to 0.125
- cotangent: bfloat16 [32, 1024, 768], P('dp', 'mp'), may hold values from -6 to 6
Outputs:
- output: float32 [32, 1024, 768], P('dp', 'mp')
- grad_tokens: float32 [32, 1024, 768], P('dp', 'mp')
- grad_memory: float32 [32, 1024, 768], P('dp', 'mp')
- grad_gains: float32 [3, 768], replicated
- bias_table_gradient: float32 [32, 12], replicated
- grad_self_proj: float32 [3, 768, 768], P(None, 'dp', 'mp')
- grad_self_out: float32 [768, 768], P('mp', 'dp')
- grad_cross_proj: float32 [3, 768, 768], P(None, 'dp', 'mp')
- grad_cross_out: float32 [768, 768], P('mp', 'dp')
- grad_ffn_proj: float32 [2, 768, 2048], P(None, 'dp', 'mp')
- grad_ffn_out: float32 [2048, 768], P('mp', 'dp')
The draws below stay inside these ranges and needn't reach their ends.
Inputs may be any that keep to these rules, and one draw needn't show every extreme that they name: `doc_lengths`: each row holds three documents in this order followed by one or more padding slots; the second document covers slots 1024 // 4 to 767.
All inputs are finite; a program needn't handle non-finite values.
Results may differ from the reference program's by a relative error of at most 0.028.
The reference program's roundings to bfloat16 on the way count: a program that leaves them out, or rounds other values in their place, can miss the bound.
Values may be sent and summed in bfloat16 or wider, within the bound.
No kernel may reach another device: no remote copies, remote signals or barrier semaphores. Data moves between devices by JAX's collectives and lax.ppermute only.
A program may use at most 512 MiB of HBM per device.

```python
import jax
import jax.numpy as jnp
import numpy as np
from jax import lax

D = 768
HEADS = 12
DH = 64
FF = 2048
NB = 32
REACH = 128
ROW = 1024
MEM = 1024
INNER = 768
BATCH = 32


def draw_doc_lengths(key, part):
    key = jax.random.fold_in(key, 7)
    first_key, second_key, third_key = jax.random.split(key, 3)
    first_end = jax.random.randint(first_key, (BATCH,), 1, ROW // 4 + 1)
    second_end = jax.random.randint(second_key, (BATCH,), 3 * ROW // 4, 7 * ROW // 8 + 1)
    first_end = first_end.at[0].set(1)
    second_end = second_end.at[0].set(7 * ROW // 8)
    third_end = jax.random.randint(third_key, (BATCH,), second_end + 1, ROW)
    return jnp.stack([first_end, second_end - first_end, third_end - second_end], axis=-1).astype(jnp.int32)


def with_ends(entries, rng, smallest, high):
    place = [jax.random.randint(jax.random.fold_in(rng, axis), (), 0, length) for axis, length in enumerate(entries.shape)]
    main_axis = entries.shape.index(max(entries.shape))
    next_to = place[:main_axis] + [(place[main_axis] + 1) % entries.shape[main_axis]] + place[main_axis + 1:]
    return entries.at[tuple(place)].set(smallest).at[tuple(next_to)].set(high)


def block_levels(key, extent, cuts, low, top_value):
    level = 1.0
    for axis_at, shards_of in cuts:
        draws = jax.random.uniform(jax.random.fold_in(jax.random.fold_in(key, 6), axis_at), (shards_of,), jnp.float32, low / len(cuts), top_value / len(cuts))
        level = level * jnp.repeat(jnp.exp(draws), extent[axis_at] // shards_of).reshape((-1,) + (1,) * (len(extent) - 1 - axis_at))
    return level


def bell_draw(key, shape, scale, limit, pieces=(), kind=jnp.bfloat16):
    factor_of = block_levels(key, shape, pieces, -0.22, 0.18) if pieces else 1.0
    values = jax.random.normal(key, shape, jnp.float32) * scale * factor_of
    return jnp.minimum(jnp.maximum(values, -limit), limit).astype(kind)


def setup_inputs(seed: int = 0) -> dict:
    keys = jax.random.split(jax.random.key(seed), 14)
    tokens = bell_draw(keys[0], (BATCH, ROW, D), 1.0, 6.0, ((0, 16), (1, 2)))
    memory = bell_draw(keys[1], (BATCH, MEM, D), 1.0, 6.0, ((0, 16), (1, 2)))
    doc_lengths = draw_doc_lengths(jax.random.fold_in(keys[13], 71), 0)
    mem_lengths = with_ends(jax.random.randint(keys[3], (BATCH,), MEM // 2 + 1, MEM + 1), jax.random.fold_in(keys[3], 1), MEM // 2 + 1, MEM).astype(jnp.int32)
    norm_gains = jnp.clip(1.0 + 0.18 * jax.random.normal(keys[4], (3, D), jnp.float32), 0.1, 1.9)
    rel_table = bell_draw(keys[5], (NB, HEADS), 1.0, 4.0, (), jnp.float32)
    self_proj = bell_draw(keys[6], (3, D, INNER), (4 * D) ** -0.5, 0.109375, ((1, 16), (2, 2)))
    self_out = bell_draw(keys[7], (INNER, D), (max(INNER // 64, 4)) ** -0.5, 1.75, ((0, 2), (1, 16)))
    cross_proj = bell_draw(keys[8], (3, D, INNER), (4 * D) ** -0.5, 0.109375, ((1, 16), (2, 2)))
    cross_out = bell_draw(keys[9], (INNER, D), (max(INNER // 64, 4)) ** -0.5, 1.75, ((0, 2), (1, 16)))
    ffn_proj = bell_draw(keys[10], (2, D, FF), D ** -0.5, 0.21875, ((1, 16), (2, 2)))
    ffn_out = bell_draw(keys[11], (FF, D), FF ** -0.5, 0.125, ((0, 2), (1, 16)))
    cotangent = bell_draw(keys[12], (BATCH, ROW, D), 1.0, 6.0, ((0, 16), (1, 2)))
    return {"tokens": tokens, "memory": memory, "doc_lengths": doc_lengths, "mem_lengths": mem_lengths, "norm_gains": norm_gains, "rel_table": rel_table, "self_proj": self_proj, "self_out": self_out, "cross_proj": cross_proj, "cross_out": cross_out, "ffn_proj": ffn_proj, "ffn_out": ffn_out, "cotangent": cotangent}


epsilon = 1e-06
masked_score = -1000000000.0

@jax.custom_vjp
def low(v):
    return lax.optimization_barrier(v.astype(jnp.bfloat16)).astype(jnp.float32)

@jax.custom_vjp
def low_back(v):
    return v

def low_keep(v):
    return (low(v), None)

def low_pass(kept, grad):
    return (grad,)

def back_keep(v):
    return (v, None)

def back_low(kept, grad):
    return (low(grad),)
low.defvjp(low_keep, low_pass)
low_back.defvjp(back_keep, back_low)

def bucket_table(length, buckets, reach):
    offsets = np.arange(length)
    exact_part = buckets // 2
    scaled = np.log(np.maximum(offsets, 1) / exact_part) / np.log(reach / exact_part) * (buckets - exact_part)
    far_bucket = np.minimum(exact_part + np.floor(scaled).astype(np.int64), buckets - 1)
    return np.where(offsets < exact_part, offsets, far_bucket).astype(np.int32)

def segment_ids(doc_lengths, length):
    bounds = jnp.cumsum(doc_lengths, axis=-1)
    slots = jnp.arange(length, dtype=jnp.int32)
    return lax.optimization_barrier(jnp.sum((slots[None, :, None] >= bounds[:, None, :]).astype(jnp.int32), axis=-1))

def high_dot(left, right):
    return jnp.dot(left, right, precision=lax.Precision.HIGHEST)

def rms_norm(values, gain):
    return values * lax.rsqrt(lax.optimization_barrier(jnp.mean(values * values, axis=-1, keepdims=True)) + epsilon) * gain

def attention(query_matrix, key_rows, value_rows, extra, mask):
    query_heads = query_matrix.reshape(query_matrix.shape[0], -1, DH)
    key_heads = key_rows.reshape(key_rows.shape[0], -1, DH)
    value_heads = value_rows.reshape(value_rows.shape[0], -1, DH)
    scores = jnp.einsum('qhe,khe->hqk', query_heads, key_heads, precision=lax.Precision.HIGHEST)
    scores = low_back(scores + extra)
    scores = jnp.where(mask[None], scores, masked_score)
    probs = low(jax.nn.softmax(scores, axis=-1))
    mixed = jnp.einsum('hqk,khe->qhe', probs, value_heads, precision=lax.Precision.HIGHEST)
    return low(low_back(mixed.reshape(query_matrix.shape[0], -1)))

def reference(tokens, memory, doc_lengths, mem_lengths, norm_gains, rel_table, self_proj, self_out, cross_proj, cross_out, ffn_proj, ffn_out, cotangent):
    segments = segment_ids(doc_lengths, ROW)
    padding = segments == doc_lengths.shape[-1]
    mem_valid = jnp.arange(MEM, dtype=jnp.int32)[None, :] < mem_lengths[:, None]
    bucket_dist = jnp.asarray(bucket_table(ROW, NB, REACH))
    key_slots = jnp.arange(ROW, dtype=jnp.int32)
    offsets = jnp.maximum(key_slots[:, None] - key_slots[None, :], 0).astype(jnp.int32)
    causal = key_slots[None, :] <= key_slots[:, None]
    onehot_dist = (bucket_dist[:, None] == jnp.arange(NB, dtype=jnp.int32)[None, :]).astype(jnp.float32)

    def forward(tokens_f, memory_f, gains, table, proj_self, out_self, proj_cross, out_cross, proj_ffn, out_ffn):
        dist_heads = high_dot(onehot_dist, table).T
        bias = jnp.take(dist_heads, offsets, axis=1)

        def one_row(row_args):
            resid_in, memory_row, segment_row, pad_row, valid_row = row_args
            normed_one = low(rms_norm(resid_in, gains[0]))
            query = low(low_back(high_dot(normed_one, proj_self[0])))
            key_rows = low(low_back(high_dot(normed_one, proj_self[1])))
            value_rows = low(low_back(high_dot(normed_one, proj_self[2])))
            self_mask = (segment_row[:, None] == segment_row[None, :]) & causal
            mixed_self = attention(query, key_rows, value_rows, bias, self_mask)
            resid_two = resid_in + low_back(high_dot(mixed_self, out_self))
            normed_two = low(rms_norm(resid_two, gains[1]))
            cross_query = low(low_back(high_dot(normed_two, proj_cross[0])))
            cross_key = low(low_back(high_dot(memory_row, proj_cross[1])))
            cross_value = low(low_back(high_dot(memory_row, proj_cross[2])))
            cross_mask = jnp.broadcast_to(valid_row[None, :], (ROW, MEM))
            mixed_cross = attention(cross_query, cross_key, cross_value, 0.0, cross_mask)
            resid_three = resid_two + low_back(high_dot(mixed_cross, out_cross))
            normed_three = low(rms_norm(resid_three, gains[2]))
            gate = low_back(high_dot(normed_three, proj_ffn[0]))
            upward = low_back(high_dot(normed_three, proj_ffn[1]))
            hidden = low(jax.nn.gelu(gate, approximate=True) * upward)
            resid_four = resid_three + low_back(high_dot(hidden, out_ffn))
            return jnp.where(pad_row[:, None], 0.0, resid_four)
        return lax.map(jax.checkpoint(one_row), (tokens_f, memory_f, segments, padding, mem_valid))
    float_args = tuple((array.astype(jnp.float32) for array in (tokens, memory, norm_gains, rel_table, self_proj, self_out, cross_proj, cross_out, ffn_proj, ffn_out)))
    output, pullback = jax.vjp(forward, *float_args)
    grads = pullback(cotangent.astype(jnp.float32))
    return (output, grads[0], grads[1], grads[2], grads[3], grads[4], grads[5], grads[6], grads[7], grads[8], grads[9])
```

```python
import functools
import jax
import jax.numpy as jnp
import numpy as np
from jax import lax
from jax.experimental import pallas as pl
from jax.experimental.pallas import tpu as pltpu
from jax.sharding import PartitionSpec as P

DH = 64
NB = 32
REACH = 128
ROW = 1024
LANES = 128
QB = 256
masked_score = -1000000000.0
BF = jnp.bfloat16
F32 = jnp.float32
VMEM_LIMIT = 56 * 1024 * 1024


def dot_t(a, b):
    return lax.dot_general(a, b, (((1,), (1,)), ((), ())), preferred_element_type=F32)


def dot_n(a, b):
    return lax.dot_general(a, b, (((1,), (0,)), ((), ())), preferred_element_type=F32)


def dot_tn(a, b):
    return lax.dot_general(a, b, (((0,), (0,)), ((), ())), preferred_element_type=F32)


def split_three(x):
    top = x.astype(BF)
    rest = x - top.astype(F32)
    mid = rest.astype(BF)
    low = (rest - mid.astype(F32)).astype(BF)
    return top.astype(F32), mid.astype(F32), low.astype(F32)


def place_three(x, slot, other):
    top, mid, low = split_three(x)
    return jnp.where(slot == 4, top, jnp.where(slot == 5, mid, jnp.where(slot == 6, low, other)))


def lane_slots(shape):
    lane = lax.broadcasted_iota(jnp.int32, shape, 1)
    return lane, lane % DH


def make_extras(bounds_ref, causal, extra_q, extra_k):
    shape = extra_q.shape
    _, slot = lane_slots(shape)
    rows = lax.broadcasted_iota(jnp.int32, shape, 0)
    if causal:
        first = bounds_ref[0]
        second = first + bounds_ref[1]
        third = second + bounds_ref[2]
        seg = (
            (rows >= first).astype(jnp.int32)
            + (rows >= second).astype(jnp.int32)
            + (rows >= third).astype(jnp.int32)
        )
        own = jnp.where(slot == seg, 1.0, 0.0)
        barred = jnp.where((slot < 4) & (slot != seg), masked_score, 0.0)
    else:
        own = jnp.where(slot == 0, 1.0, 0.0)
        barred = jnp.where((slot == 0) & (rows >= bounds_ref[0]), masked_score, 0.0)
    extra_q[...] = jnp.where(slot == 7, 1.0, own).astype(BF)
    extra_k[...] = jnp.where((slot >= 4) & (slot <= 6), 1.0, barred).astype(BF)


def band_square(band_ref, head):
    wide = jnp.broadcast_to(band_ref[head : head + 1, :], (LANES, 3 * LANES))
    rolled = pltpu.roll(wide, 0, 1, stride=1, stride_axis=0)
    return rolled[:, LANES : 2 * LANES], rolled[:, :LANES]


def forward_kernel(causal, bounds_ref, band_ref, q_ref, k_ref, v_ref, o_ref, qa_ref, extra_q, extra_k):
    length = q_ref.shape[0]

    @pl.when(pl.program_id(0) == 0)
    def _():
        make_extras(bounds_ref, causal, extra_q, extra_k)

    lane, slot = lane_slots((QB, LANES))
    full_lane, _ = lane_slots((length, LANES))
    values = v_ref[...]
    kept = []
    for head in range(2):
        mine = (full_lane < DH) == (head == 0)
        mine_block = (lane < DH) == (head == 0)
        keys = jnp.where(mine, k_ref[...], extra_k[...])
        if causal:
            near, side = band_square(band_ref, head)
            near_only = jnp.full((LANES, LANES), masked_score, F32)
        for block in range(length // QB):
            first = block * QB
            count = first + QB if causal else length
            queries = jnp.where(mine_block, q_ref[first : first + QB, :], extra_q[first : first + QB, :])
            scores = dot_t(queries, keys[:count])
            if causal:
                corner = jnp.concatenate([side, jnp.zeros((LANES, LANES), F32)], axis=0)
                left = jnp.concatenate([near, side], axis=0)
                right = jnp.concatenate([near_only, near], axis=0)
                pieces = []
                if block > 0:
                    if first > LANES:
                        pieces.append(scores[:, : first - LANES])
                    pieces.append(scores[:, first - LANES : first] + corner)
                pieces.append(scores[:, first : first + LANES] + left)
                pieces.append(scores[:, first + LANES :] + right)
                scores = jnp.concatenate(pieces, axis=1)
            top = jnp.max(scores, axis=1, keepdims=True)
            terms = jnp.exp(scores - top)
            total = jnp.sum(terms, axis=1, keepdims=True)
            probs = (terms * (1.0 / total)).astype(BF)
            mixed = dot_n(probs, values[:count])
            if head == 0:
                kept.append(mixed)
            else:
                o_ref[first : first + QB, :] = jnp.where(lane < DH, kept[block], mixed).astype(BF)
            minus_log = -(top + jnp.log(total))
            spare = place_three(minus_log, slot, queries.astype(F32))
            qa_ref[head, first : first + QB, :] = jnp.where(mine_block, queries, spare.astype(BF))


def backward_kernel(causal, bounds_ref, band_ref, qa_ref, k_ref, v_ref, g_ref, o_ref,
                    grad_ref, bias_ref, extra_q, extra_k, dk_acc, dv_acc, near_acc, side_acc):
    length = k_ref.shape[0]

    @pl.when(pl.program_id(0) == 0)
    def _():
        make_extras(bounds_ref, causal, extra_q, extra_k)

    lane, slot = lane_slots((QB, LANES))
    full_lane, full_slot = lane_slots((length, LANES))
    spare_v = jnp.where((full_slot >= 4) & (full_slot <= 6), 1.0, 0.0).astype(BF)
    for head in range(2):
        mine = (full_lane < DH) == (head == 0)
        mine_block = (lane < DH) == (head == 0)
        keys = jnp.where(mine, k_ref[...], extra_k[...])
        values = jnp.where(mine, v_ref[...], spare_v)
        if causal:
            near, side = band_square(band_ref, head)
            near, side = near.T, side.T
            near_only = jnp.full((LANES, LANES), masked_score, F32)
            near_acc[...] = jnp.zeros_like(near_acc)
            side_acc[...] = jnp.zeros_like(side_acc)
        dk_acc[...] = jnp.zeros_like(dk_acc)
        dv_acc[...] = jnp.zeros_like(dv_acc)
        for block in range(length // QB):
            first = block * QB
            count = first + QB if causal else length
            span = slice(first, first + QB)
            queries = qa_ref[head, span, :]
            upstream = g_ref[span, :]
            inner = jnp.sum(
                jnp.where(mine_block, upstream.astype(F32) * o_ref[span, :].astype(F32), 0.0), axis=1, keepdims=True
            )
            spare = place_three(-inner, slot, jnp.zeros((QB, LANES), F32))
            grads = jnp.where(mine_block, upstream, spare.astype(BF))
            scores = dot_t(keys[:count], queries)
            if causal:
                corner = jnp.concatenate([side, jnp.zeros((LANES, LANES), F32)], axis=1)
                upper = jnp.concatenate([near, side], axis=1)
                lower = jnp.concatenate([near_only, near], axis=1)
                pieces = []
                if block > 0:
                    if first > LANES:
                        pieces.append(scores[: first - LANES])
                    pieces.append(scores[first - LANES : first] + corner)
                pieces.append(scores[first : first + LANES] + upper)
                pieces.append(scores[first + LANES :] + lower)
                scores = jnp.concatenate(pieces, axis=0)
            probs = jnp.exp(scores)
            lifted = dot_t(values[:count], grads)
            score_grads = (probs * lifted).astype(BF)
            dv_acc[:count, :] += dot_n(probs.astype(BF), grads)
            dk_acc[:count, :] += dot_n(score_grads, queries)
            dq = dot_tn(score_grads, keys[:count])
            if causal:
                near_acc[...] += score_grads[first : first + LANES, :LANES].astype(F32)
                near_acc[...] += score_grads[first + LANES :, LANES:].astype(F32)
                side_acc[...] += score_grads[first : first + LANES, LANES:].astype(F32)
                if block > 0:
                    side_acc[...] += score_grads[first - LANES : first, :LANES].astype(F32)
            if head == 0:
                grad_ref[0, span, :] = dq.astype(BF)
            else:
                grad_ref[0, span, :] = jnp.where(lane < DH, grad_ref[0, span, :], dq.astype(BF))
        if head == 0:
            grad_ref[1] = dk_acc[...].astype(BF)
            grad_ref[2] = dv_acc[...].astype(BF)
        else:
            grad_ref[1] = jnp.where(full_lane < DH, grad_ref[1], dk_acc[...].astype(BF))
            grad_ref[2] = jnp.where(full_lane < DH, grad_ref[2], dv_acc[...].astype(BF))
        if causal:
            square = jnp.concatenate([side_acc[...], near_acc[...]], axis=0)
            wide = jnp.concatenate([square, jnp.zeros((2 * LANES, 2 * LANES), F32)], axis=1)
            half = LANES
            while half:
                wide = wide[:half] + pltpu.roll(wide[half:], 3 * LANES - half, 1)
                half //= 2
            diag = wide[:, 2 * LANES :]
            ones_column = jnp.where((full_lane % DH == 7) & ~mine, dk_acc[...], 0.0)
            whole = jnp.sum(ones_column, axis=0, keepdims=True)
            bias_ref[0, head : head + 1, :] = diag
            bias_ref[0, 2 + head : 3 + head, :] = whole


def attention_forward(causal, bounds, band, q, k, v, cols):
    rows = q[0].shape[0]
    pairs = cols // LANES

    def spec(offset):
        return pl.BlockSpec((rows, LANES), lambda p: (0, p + offset))

    n = rows * rows * pairs * 2
    return pl.pallas_call(
        functools.partial(forward_kernel, causal),
        grid=(pairs,),
        in_specs=[
            pl.BlockSpec(memory_space=pltpu.SMEM),
            pl.BlockSpec((None, 2, 3 * LANES), lambda p: (p, 0, 0)),
            spec(q[1]), spec(k[1]), spec(v[1]),
        ],
        out_specs=[
            pl.BlockSpec((rows, LANES), lambda p: (0, p)),
            pl.BlockSpec((2, rows, LANES), lambda p: (p, 0, 0)),
        ],
        out_shape=[
            jax.ShapeDtypeStruct((rows, cols), BF),
            jax.ShapeDtypeStruct((2 * pairs, rows, LANES), BF),
        ],
        scratch_shapes=[pltpu.VMEM((rows, LANES), BF), pltpu.VMEM((rows, LANES), BF)],
        compiler_params=pltpu.CompilerParams(vmem_limit_bytes=VMEM_LIMIT, dimension_semantics=("arbitrary",)),
        cost_estimate=pl.CostEstimate(flops=n * 256 * 4 // (2 if causal else 1), bytes_accessed=rows * cols * 16, transcendentals=n),
        name="attention_forward",
    )(bounds, band, q[0], k[0], v[0])


def attention_backward(causal, bounds, band, qa, k, v, g, o, cols):
    rows = qa.shape[1]
    pairs = cols // LANES

    def spec(offset):
        return pl.BlockSpec((rows, LANES), lambda p: (0, p + offset))

    n = rows * rows * pairs * 2
    return pl.pallas_call(
        functools.partial(backward_kernel, causal),
        grid=(pairs,),
        in_specs=[
            pl.BlockSpec(memory_space=pltpu.SMEM),
            pl.BlockSpec((None, 2, 3 * LANES), lambda p: (p, 0, 0)),
            pl.BlockSpec((2, rows, LANES), lambda p: (p, 0, 0)),
            spec(k[1]), spec(v[1]), spec(0), spec(0),
        ],
        out_specs=[
            pl.BlockSpec((3, rows, LANES), lambda p: (0, 0, p)),
            pl.BlockSpec((1, 8, LANES), lambda p: (p, 0, 0)),
        ],
        out_shape=[
            jax.ShapeDtypeStruct((3, rows, cols), BF),
            jax.ShapeDtypeStruct((pairs, 8, LANES), F32),
        ],
        scratch_shapes=[
            pltpu.VMEM((rows, LANES), BF), pltpu.VMEM((rows, LANES), BF),
            pltpu.VMEM((rows, LANES), F32), pltpu.VMEM((rows, LANES), F32),
            pltpu.VMEM((LANES, LANES), F32), pltpu.VMEM((LANES, LANES), F32),
        ],
        compiler_params=pltpu.CompilerParams(vmem_limit_bytes=VMEM_LIMIT, dimension_semantics=("arbitrary",)),
        cost_estimate=pl.CostEstimate(flops=n * 256 * 10 // (2 if causal else 1), bytes_accessed=rows * cols * 20, transcendentals=n),
        name="attention_backward",
    )(bounds, band, qa, k[0], v[0], g, o)


def bucket_table(length, buckets, reach):
    offsets = np.arange(length)
    exact_part = buckets // 2
    scaled = np.log(np.maximum(offsets, 1) / exact_part) / np.log(reach / exact_part) * (buckets - exact_part)
    far_bucket = np.minimum(exact_part + np.floor(scaled).astype(np.int64), buckets - 1)
    return np.where(offsets < exact_part, offsets, far_bucket).astype(np.int32)


def bias_band(rel_table):
    distance = LANES - np.arange(3 * LANES)
    buckets = bucket_table(LANES + 1, NB, REACH)
    onehot = np.zeros((3 * LANES, NB), np.float32)
    shift = np.zeros((3 * LANES,), np.float32)
    for at, far in enumerate(distance):
        if 0 <= far < LANES:
            onehot[at, buckets[far]] = 1.0
        elif -LANES < far < 0:
            shift[at] = masked_score
    relative = rel_table - rel_table[NB - 1 :]
    band = jnp.dot(jnp.asarray(onehot), relative, precision=lax.Precision.HIGHEST) + shift[:, None]
    return band.T.reshape(-1, 2, 3 * LANES)


def table_gradient(sums):
    buckets = bucket_table(LANES, NB, REACH)
    near = (buckets[:, None] == np.arange(NB)[None, :]) & (buckets[:, None] < NB - 1)
    diag = sums[:, 0:2].reshape(-1, LANES)
    whole = jnp.sum(sums[:, 2:4].reshape(-1, LANES), axis=-1)
    table = jnp.dot(diag, jnp.asarray(near.astype(np.float32)), precision=lax.Precision.HIGHEST)
    last = whole - jnp.sum(table, axis=-1)
    table = table + last[:, None] * jnp.asarray((np.arange(NB) == NB - 1).astype(np.float32))
    return table.T


epsilon = 1e-06


def norm_forward(values, gain):
    inverse = lax.rsqrt(jnp.mean(values * values, axis=-1, keepdims=True) + epsilon)
    return (values * inverse * gain).astype(BF), inverse


def norm_backward(values, inverse, gain, upstream):
    weighted = upstream * gain
    inner_mean = jnp.mean(weighted * values, axis=-1, keepdims=True)
    grad_values = inverse * weighted - values * inverse * inverse * inverse * inner_mean
    return grad_values, jnp.sum(upstream * values * inverse, axis=0)


def mm(a, b, dims, kind=F32):
    return lax.dot_general(a, b, ((dims[0], dims[1]), ((), ())), preferred_element_type=F32).astype(kind)


def nn(a, b, kind=F32):
    return mm(a, b, ((1,), (0,)), kind)


def nt(a, b, kind=F32):
    return mm(a, b, ((1,), (1,)), kind)


def tn(a, b, kind=F32):
    return mm(a, b, ((0,), (0,)), kind)


def whole_row(pair_rows, me, size):
    kept = lax.dynamic_index_in_dim(pair_rows, me, 0, False)
    sent = lax.dynamic_index_in_dim(pair_rows, 1 - me, 0, False)
    came = lax.ppermute(sent, "mp", [(0, 1), (1, 0)])
    return jnp.where(me == 0, jnp.concatenate([kept, came]), jnp.concatenate([came, kept]))


def row_halves(row, me):
    halves = row.reshape(2, row.shape[0] // 2, row.shape[1])
    kept = lax.dynamic_index_in_dim(halves, me, 0, False)
    sent = lax.dynamic_index_in_dim(halves, 1 - me, 0, False)
    came = lax.ppermute(sent.astype(BF), "mp", [(0, 1), (1, 0)]).astype(F32)
    return jnp.where(me == 0, jnp.stack([kept, came]), jnp.stack([came, kept]))


def gather_weights(shard):
    n, rows, cols = shard.shape
    pieces = lax.all_gather(shard, ("dp", "mp"), axis=0)
    dp = lax.axis_size("dp")
    mp = lax.axis_size("mp")
    pieces = pieces.reshape(dp, mp, n, rows, cols).transpose(2, 0, 3, 1, 4)
    return pieces.reshape(n, dp * rows, mp * cols)


def scatter_grads(grads):
    dp = lax.axis_size("dp")
    mp = lax.axis_size("mp")
    n, rows, cols = grads.shape
    pieces = grads.astype(BF).reshape(n, dp, rows // dp, mp, cols // mp).transpose(1, 3, 0, 2, 4)
    pieces = pieces.reshape(dp * mp, n, rows // dp, cols // mp)
    return lax.psum_scatter(pieces, ("dp", "mp"), scatter_dimension=0, tiled=True)[0].astype(F32)


def per_device(
    tokens,
    memory,
    doc_lengths,
    mem_lengths,
    norm_gains,
    rel_table,
    self_proj,
    self_out,
    cross_proj,
    cross_out,
    ffn_proj,
    ffn_out,
    cotangent,
):
    me = lax.axis_index("mp")
    width = tokens.shape[2]
    docs = lax.dynamic_index_in_dim(doc_lengths, me, 0, False)
    mem_length = lax.dynamic_slice_in_dim(mem_lengths, me, 1, 0)
    band = bias_band(rel_table)

    w_self = gather_weights(self_proj)
    w_mid = gather_weights(jnp.concatenate([self_out.T[None], cross_proj, cross_out.T[None]]))
    w_ffn = gather_weights(jnp.concatenate([ffn_proj, ffn_out.T[None]]))

    resid_in = whole_row(tokens, me, None).astype(F32)
    memory_row = whole_row(memory, me, None)
    cot_row = whole_row(cotangent, me, None)
    padding = (jnp.arange(ROW, dtype=jnp.int32) >= jnp.sum(docs))[:, None]

    normed_one, inverse_one = norm_forward(resid_in, norm_gains[0])
    qkv = jnp.concatenate([nn(normed_one, w_self[s], BF) for s in range(3)], axis=1)
    mixed_self, qa_self = attention_forward(True, docs, band, (qkv, 0), (qkv, 6), (qkv, 12), width)
    resid_two = resid_in + nt(mixed_self, w_mid[0])
    normed_two, inverse_two = norm_forward(resid_two, norm_gains[1])
    query_cross = nn(normed_two, w_mid[1], BF)
    key_cross = nn(memory_row, w_mid[2], BF)
    value_cross = nn(memory_row, w_mid[3], BF)
    mixed_cross, qa_cross = attention_forward(
        False, mem_length, band, (query_cross, 0), (key_cross, 0), (value_cross, 0), width
    )
    resid_three = resid_two + nt(mixed_cross, w_mid[4])
    normed_three, inverse_three = norm_forward(resid_three, norm_gains[2])
    gate = nn(normed_three, w_ffn[0])
    up = nn(normed_three, w_ffn[1])
    activated, gelu_pull = jax.vjp(lambda x: jax.nn.gelu(x, approximate=True), gate)
    hidden = (activated * up).astype(BF)
    output = jnp.where(padding, 0.0, resid_three + nt(hidden, w_ffn[2]))
    output = row_halves(output, me)

    grad_four = jnp.where(padding, 0.0, cot_row.astype(F32))
    branch = grad_four.astype(BF)
    grad_ffn_out = tn(branch, hidden, BF)
    grad_hidden = nn(branch, w_ffn[2])
    grad_gate = gelu_pull(grad_hidden * up)[0].astype(BF)
    grad_up = (grad_hidden * activated).astype(BF)
    ffn_grads = scatter_grads(
        jnp.stack([tn(normed_three, grad_gate, BF), tn(normed_three, grad_up, BF), grad_ffn_out])
    )
    upstream = nt(grad_gate, w_ffn[0]) + nt(grad_up, w_ffn[1])
    grad_resid, gain_three = norm_backward(resid_three, inverse_three, norm_gains[2], upstream)
    grad_three = grad_four + grad_resid

    branch = grad_three.astype(BF)
    grad_cross_out = tn(branch, mixed_cross, BF)
    grad_mixed = nn(branch, w_mid[4], BF)
    grads_cross, _ = attention_backward(
        False, mem_length, band, qa_cross, (key_cross, 0), (value_cross, 0), grad_mixed, mixed_cross, width
    )
    grad_memory = row_halves(nt(grads_cross[1], w_mid[2]) + nt(grads_cross[2], w_mid[3]), me)
    upstream = nt(grads_cross[0], w_mid[1])
    grad_resid, gain_two = norm_backward(resid_two, inverse_two, norm_gains[1], upstream)
    grad_two = grad_three + grad_resid

    branch = grad_two.astype(BF)
    grad_self_out = tn(branch, mixed_self, BF)
    mid_grads = scatter_grads(
        jnp.stack(
            [
                grad_self_out,
                tn(normed_two, grads_cross[0], BF),
                tn(memory_row, grads_cross[1], BF),
                tn(memory_row, grads_cross[2], BF),
                grad_cross_out,
            ]
        )
    )
    grad_mixed = nn(branch, w_mid[0], BF)
    grads_self, sums = attention_backward(
        True, docs, band, qa_self, (qkv, 6), (qkv, 12), grad_mixed, mixed_self, width
    )
    self_grads = scatter_grads(jnp.stack([tn(normed_one, grads_self[s], BF) for s in range(3)]))
    upstream = sum(nt(grads_self[s], w_self[s]) for s in range(3))
    grad_resid, gain_one = norm_backward(resid_in, inverse_one, norm_gains[0], upstream)
    grad_tokens = row_halves(grad_two + grad_resid, me)
    grad_gains, table = lax.psum(
        (jnp.stack([gain_one, gain_two, gain_three]), table_gradient(sums)), ("dp", "mp")
    )
    return (
        output,
        grad_tokens,
        grad_memory,
        grad_gains,
        table,
        self_grads,
        mid_grads[0].T,
        mid_grads[1:4],
        mid_grads[4].T,
        ffn_grads[:2],
        ffn_grads[2].T,
    )


def solution(mesh):
    rows = P("dp", "mp", None)
    proj = P(None, "dp", "mp")
    out = P("mp", "dp")
    return jax.shard_map(
        per_device,
        mesh=mesh,
        in_specs=(rows, rows, P("dp", None), P("dp"), P(), P(), proj, out, proj, out, proj, out, rows),
        out_specs=(rows, rows, rows, P(), P(), proj, out, proj, out, proj, out),
        check_vma=False,
    )
```

```python
import functools
import jax
import jax.numpy as jnp
import numpy as np
from jax import lax
from jax.experimental import pallas as pl
from jax.experimental.pallas import tpu as pltpu
from jax.sharding import PartitionSpec as P

DH = 64
NB = 32
REACH = 128
ROW = 1024
LANES = 128
QB = 256
masked_score = -1000000000.0
BF = jnp.bfloat16
F32 = jnp.float32
VMEM_LIMIT = 56 * 1024 * 1024


def dot_t(a, b):
    return lax.dot_general(a, b, (((1,), (1,)), ((), ())), preferred_element_type=F32)


def dot_n(a, b):
    return lax.dot_general(a, b, (((1,), (0,)), ((), ())), preferred_element_type=F32)


def dot_tn(a, b):
    return lax.dot_general(a, b, (((0,), (0,)), ((), ())), preferred_element_type=F32)


def split_three(x):
    top = x.astype(BF)
    rest = x - top.astype(F32)
    mid = rest.astype(BF)
    low = (rest - mid.astype(F32)).astype(BF)
    return top.astype(F32), mid.astype(F32), low.astype(F32)


def place_three(x, slot, other):
    top, mid, low = split_three(x)
    return jnp.where(slot == 4, top, jnp.where(slot == 5, mid, jnp.where(slot == 6, low, other)))


def lane_slots(shape):
    lane = lax.broadcasted_iota(jnp.int32, shape, 1)
    return lane, lane % DH


def make_extras(bounds_ref, causal, extra_q, extra_k):
    shape = extra_q.shape
    _, slot = lane_slots(shape)
    rows = lax.broadcasted_iota(jnp.int32, shape, 0)
    if causal:
        first = bounds_ref[0]
        second = first + bounds_ref[1]
        third = second + bounds_ref[2]
        seg = (
            (rows >= first).astype(jnp.int32)
            + (rows >= second).astype(jnp.int32)
            + (rows >= third).astype(jnp.int32)
        )
        own = jnp.where(slot == seg, 1.0, 0.0)
        barred = jnp.where((slot < 4) & (slot != seg), masked_score, 0.0)
    else:
        own = jnp.where(slot == 0, 1.0, 0.0)
        barred = jnp.where((slot == 0) & (rows >= bounds_ref[0]), masked_score, 0.0)
    extra_q[...] = jnp.where(slot == 7, 1.0, own).astype(BF)
    extra_k[...] = jnp.where((slot >= 4) & (slot <= 6), 1.0, barred).astype(BF)


def band_square(band_ref, head):
    wide = jnp.broadcast_to(band_ref[head : head + 1, :], (LANES, 3 * LANES))
    rolled = pltpu.roll(wide, 0, 1, stride=1, stride_axis=0)
    return rolled[:, LANES : 2 * LANES], rolled[:, :LANES]


def forward_kernel(causal, bounds_ref, band_ref, q_ref, k_ref, v_ref, o_ref, qa_ref, extra_q, extra_k):
    length = q_ref.shape[0]

    @pl.when(pl.program_id(0) == 0)
    def _():
        make_extras(bounds_ref, causal, extra_q, extra_k)

    lane, slot = lane_slots((QB, LANES))
    full_lane, _ = lane_slots((length, LANES))
    values = v_ref[...]
    kept = []
    for head in range(2):
        mine = (full_lane < DH) == (head == 0)
        mine_block = (lane < DH) == (head == 0)
        keys = jnp.where(mine, k_ref[...], extra_k[...])
        if causal:
            near, side = band_square(band_ref, head)
            near_only = jnp.full((LANES, LANES), masked_score, F32)
        for block in range(length // QB):
            first = block * QB
            count = first + QB if causal else length
            queries = jnp.where(mine_block, q_ref[first : first + QB, :], extra_q[first : first + QB, :])
            scores = dot_t(queries, keys[:count])
            if causal:
                corner = jnp.concatenate([side, jnp.zeros((LANES, LANES), F32)], axis=0)
                left = jnp.concatenate([near, side], axis=0)
                right = jnp.concatenate([near_only, near], axis=0)
                pieces = []
                if block > 0:
                    if first > LANES:
                        pieces.append(scores[:, : first - LANES])
                    pieces.append(scores[:, first - LANES : first] + corner)
                pieces.append(scores[:, first : first + LANES] + left)
                pieces.append(scores[:, first + LANES :] + right)
                scores = jnp.concatenate(pieces, axis=1)
            top = jnp.max(scores, axis=1, keepdims=True)
            terms = jnp.exp(scores - top)
            total = jnp.sum(terms, axis=1, keepdims=True)
            probs = (terms * (1.0 / total)).astype(BF)
            mixed = dot_n(probs, values[:count])
            if head == 0:
                kept.append(mixed)
            else:
                o_ref[first : first + QB, :] = jnp.where(lane < DH, kept[block], mixed).astype(BF)
            minus_log = -(top + jnp.log(total))
            spare = place_three(minus_log, slot, queries.astype(F32))
            qa_ref[head, first : first + QB, :] = jnp.where(mine_block, queries, spare.astype(BF))


def backward_kernel(causal, extra, bounds_ref, band_ref, qa_ref, k_ref, v_ref, g_ref, o_ref, *rest):
    grad_ref, bias_ref, extra_q, extra_k, dk_acc, dv_acc, near_acc, side_acc = rest[extra:]
    length = k_ref.shape[0]

    @pl.when(pl.program_id(0) == 0)
    def _():
        make_extras(bounds_ref, causal, extra_q, extra_k)

    lane, slot = lane_slots((QB, LANES))
    full_lane, full_slot = lane_slots((length, LANES))
    spare_v = jnp.where((full_slot >= 4) & (full_slot <= 6), 1.0, 0.0).astype(BF)
    for head in range(2):
        mine = (full_lane < DH) == (head == 0)
        mine_block = (lane < DH) == (head == 0)
        keys = jnp.where(mine, k_ref[...], extra_k[...])
        values = jnp.where(mine, v_ref[...], spare_v)
        if causal:
            near, side = band_square(band_ref, head)
            near, side = near.T, side.T
            near_only = jnp.full((LANES, LANES), masked_score, F32)
            near_acc[...] = jnp.zeros_like(near_acc)
            side_acc[...] = jnp.zeros_like(side_acc)
        dk_acc[...] = jnp.zeros_like(dk_acc)
        dv_acc[...] = jnp.zeros_like(dv_acc)
        for block in range(length // QB):
            first = block * QB
            count = first + QB if causal else length
            span = slice(first, first + QB)
            queries = qa_ref[head, span, :]
            upstream = g_ref[span, :]
            inner = jnp.sum(
                jnp.where(mine_block, upstream.astype(F32) * o_ref[span, :].astype(F32), 0.0), axis=1, keepdims=True
            )
            spare = place_three(-inner, slot, jnp.zeros((QB, LANES), F32))
            grads = jnp.where(mine_block, upstream, spare.astype(BF))
            scores = dot_t(keys[:count], queries)
            if causal:
                corner = jnp.concatenate([side, jnp.zeros((LANES, LANES), F32)], axis=1)
                upper = jnp.concatenate([near, side], axis=1)
                lower = jnp.concatenate([near_only, near], axis=1)
                pieces = []
                if block > 0:
                    if first > LANES:
                        pieces.append(scores[: first - LANES])
                    pieces.append(scores[first - LANES : first] + corner)
                pieces.append(scores[first : first + LANES] + upper)
                pieces.append(scores[first + LANES :] + lower)
                scores = jnp.concatenate(pieces, axis=0)
            probs = jnp.exp(scores)
            lifted = dot_t(values[:count], grads)
            score_grads = (probs * lifted).astype(BF)
            dv_acc[:count, :] += dot_n(probs.astype(BF), grads)
            dk_acc[:count, :] += dot_n(score_grads, queries)
            dq = dot_tn(score_grads, keys[:count])
            if causal:
                near_acc[...] += score_grads[first : first + LANES, :LANES].astype(F32)
                near_acc[...] += score_grads[first + LANES :, LANES:].astype(F32)
                side_acc[...] += score_grads[first : first + LANES, LANES:].astype(F32)
                if block > 0:
                    side_acc[...] += score_grads[first - LANES : first, :LANES].astype(F32)
            if head == 0:
                grad_ref[0, span, :] = dq.astype(BF)
            else:
                grad_ref[0, span, :] = jnp.where(lane < DH, grad_ref[0, span, :], dq.astype(BF))
        if head == 0:
            grad_ref[1] = dk_acc[...].astype(BF)
            grad_ref[2] = dv_acc[...].astype(BF)
        else:
            grad_ref[1] = jnp.where(full_lane < DH, grad_ref[1], dk_acc[...].astype(BF))
            grad_ref[2] = jnp.where(full_lane < DH, grad_ref[2], dv_acc[...].astype(BF))
        if causal:
            square = jnp.concatenate([side_acc[...], near_acc[...]], axis=0)
            wide = jnp.concatenate([square, jnp.zeros((2 * LANES, 2 * LANES), F32)], axis=1)
            half = LANES
            while half:
                wide = wide[:half] + pltpu.roll(wide[half:], 3 * LANES - half, 1)
                half //= 2
            diag = wide[:, 2 * LANES :]
            ones_column = jnp.where((full_lane % DH == 7) & ~mine, dk_acc[...], 0.0)
            whole = jnp.sum(ones_column, axis=0, keepdims=True)
            bias_ref[0, head : head + 1, :] = diag
            bias_ref[0, 2 + head : 3 + head, :] = whole


def attention_forward(causal, bounds, band, q, k, v, cols):
    rows = q[0].shape[0]
    pairs = cols // LANES

    def spec(offset):
        return pl.BlockSpec((rows, LANES), lambda p: (0, p + offset))

    n = rows * rows * pairs * 2
    return pl.pallas_call(
        functools.partial(forward_kernel, causal),
        grid=(pairs,),
        in_specs=[
            pl.BlockSpec(memory_space=pltpu.SMEM),
            pl.BlockSpec((None, 2, 3 * LANES), lambda p: (p, 0, 0)),
            spec(q[1]), spec(k[1]), spec(v[1]),
        ],
        out_specs=[
            pl.BlockSpec((rows, LANES), lambda p: (0, p)),
            pl.BlockSpec((2, rows, LANES), lambda p: (p, 0, 0)),
        ],
        out_shape=[
            jax.ShapeDtypeStruct((rows, cols), BF),
            jax.ShapeDtypeStruct((2 * pairs, rows, LANES), BF),
        ],
        scratch_shapes=[pltpu.VMEM((rows, LANES), BF), pltpu.VMEM((rows, LANES), BF)],
        compiler_params=pltpu.CompilerParams(vmem_limit_bytes=VMEM_LIMIT, dimension_semantics=("arbitrary",)),
        cost_estimate=pl.CostEstimate(flops=n * 256 * 4 // (2 if causal else 1), bytes_accessed=rows * cols * 16, transcendentals=n),
        name="attention_forward",
    )(bounds, band, q[0], k[0], v[0])


def attention_backward(causal, bounds, band, qa, k, v, g, o, cols, start=0, stop=None, into=None):
    rows = qa.shape[1]
    pairs = (cols // LANES if stop is None else stop) - start

    def spec(offset):
        return pl.BlockSpec((rows, LANES), lambda p: (0, p + offset + start))

    n = rows * rows * pairs * 2
    shape = jax.ShapeDtypeStruct((3, rows, cols), BF)
    extra = [] if into is None else [into]
    return pl.pallas_call(
        functools.partial(backward_kernel, causal, len(extra)),
        grid=(pairs,),
        in_specs=[
            pl.BlockSpec(memory_space=pltpu.SMEM),
            pl.BlockSpec((None, 2, 3 * LANES), lambda p: (p + start, 0, 0)),
            pl.BlockSpec((2, rows, LANES), lambda p: (p + start, 0, 0)),
            spec(k[1]), spec(v[1]), spec(0), spec(0),
        ] + [pl.BlockSpec(memory_space=pl.ANY)] * len(extra),
        out_specs=[
            pl.BlockSpec((3, rows, LANES), lambda p: (0, 0, p + start)),
            pl.BlockSpec((1, 8, LANES), lambda p: (p, 0, 0)),
        ],
        out_shape=[shape, jax.ShapeDtypeStruct((pairs, 8, LANES), F32)],
        input_output_aliases={7: 0} if extra else {},
        scratch_shapes=[
            pltpu.VMEM((rows, LANES), BF), pltpu.VMEM((rows, LANES), BF),
            pltpu.VMEM((rows, LANES), F32), pltpu.VMEM((rows, LANES), F32),
            pltpu.VMEM((LANES, LANES), F32), pltpu.VMEM((LANES, LANES), F32),
        ],
        compiler_params=pltpu.CompilerParams(vmem_limit_bytes=VMEM_LIMIT, dimension_semantics=("arbitrary",)),
        cost_estimate=pl.CostEstimate(flops=n * 256 * 10 // (2 if causal else 1), bytes_accessed=rows * cols * 20, transcendentals=n),
        name="attention_backward",
    )(bounds, band, qa, k[0], v[0], g, o, *extra)


def bucket_table(length, buckets, reach):
    offsets = np.arange(length)
    exact_part = buckets // 2
    scaled = np.log(np.maximum(offsets, 1) / exact_part) / np.log(reach / exact_part) * (buckets - exact_part)
    far_bucket = np.minimum(exact_part + np.floor(scaled).astype(np.int64), buckets - 1)
    return np.where(offsets < exact_part, offsets, far_bucket).astype(np.int32)


def bias_band(rel_table):
    distance = LANES - np.arange(3 * LANES)
    buckets = bucket_table(LANES + 1, NB, REACH)
    onehot = np.zeros((3 * LANES, NB), np.float32)
    shift = np.zeros((3 * LANES,), np.float32)
    for at, far in enumerate(distance):
        if 0 <= far < LANES:
            onehot[at, buckets[far]] = 1.0
        elif -LANES < far < 0:
            shift[at] = masked_score
    relative = rel_table - rel_table[NB - 1 :]
    band = jnp.dot(jnp.asarray(onehot), relative, precision=lax.Precision.HIGHEST) + shift[:, None]
    return band.T.reshape(-1, 2, 3 * LANES)


def table_gradient(sums):
    buckets = bucket_table(LANES, NB, REACH)
    near = (buckets[:, None] == np.arange(NB)[None, :]) & (buckets[:, None] < NB - 1)
    diag = sums[:, 0:2].reshape(-1, LANES)
    whole = jnp.sum(sums[:, 2:4].reshape(-1, LANES), axis=-1)
    table = jnp.dot(diag, jnp.asarray(near.astype(np.float32)), precision=lax.Precision.HIGHEST)
    last = whole - jnp.sum(table, axis=-1)
    table = table + last[:, None] * jnp.asarray((np.arange(NB) == NB - 1).astype(np.float32))
    return table.T

epsilon = 1e-06
TB = 256


def rms(values, gain):
    inverse = lax.rsqrt(jnp.mean(values * values, axis=-1, keepdims=True) + epsilon)
    return (values * inverse * gain).astype(BF), inverse


def rms_back(values, inverse, gain, upstream):
    weighted = upstream * gain
    inner_mean = jnp.mean(weighted * values, axis=-1, keepdims=True)
    grad_values = inverse * weighted - values * (inverse * inverse * inverse * inner_mean)
    return grad_values, jnp.sum(upstream * values * inverse, axis=0, keepdims=True)


def params():
    return pltpu.CompilerParams(vmem_limit_bytes=VMEM_LIMIT, dimension_semantics=("arbitrary",))


def held(shape):
    zeros = (0,) * len(shape)
    return pl.BlockSpec(shape, lambda s: zeros, pipeline_mode=pl.Buffered(1))


def tokens_block(*lead):
    zeros = (0,) * len(lead)

    def spec(blocks, width):
        return pl.BlockSpec(lead + (TB, width), lambda s: zeros + (jnp.minimum(s, blocks - 1), 0))

    return spec


def cost(flops, moved):
    return pl.CostEstimate(flops=flops, bytes_accessed=moved, transcendentals=0)


def piece_places():
    return [(y, x, z0, c) for c in range(2) for z0 in range(2) for y in range(2) for x in range(2)]


def relative_copies(ids_ref, pieces, place, sem):
    mine = ids_ref[0]
    count, rows, _ = pieces[0].shape[1:]

    def copy(flip):
        for piece, (y, x, z0, c) in zip(pieces, piece_places()):
            for z1 in range(2):
                block = jnp.bitwise_xor(mine, 8 * z1 + 4 * z0 + 2 * y + c)
                span = pl.ds(pl.multiple_of(block * rows, 16), rows)
                for n in range(count):
                    pltpu.make_async_copy(piece.at[z1, n], place(n, span, x ^ flip), sem).start()

    @pl.when(ids_ref[1] == 0)
    def _():
        copy(0)

    @pl.when(ids_ref[1] == 1)
    def _():
        copy(1)


def natural_place(w_ref, cols):
    return lambda n, span, x: w_ref.at[n, span, x * cols : (x + 1) * cols]


def plain_copies(w_in, w_ref, sem):
    dp, mp, count, rows, cols = w_in.shape
    for block in range(dp):
        for x in range(mp):
            for n in range(count):
                target = w_ref.at[n, block * rows : (block + 1) * rows, x * cols : (x + 1) * cols]
                pltpu.make_async_copy(w_in.at[block, x, n], target, sem).start()


def project_kernel(pieces, ids_ref, gain_ref, x_ref, *refs):
    w_in = refs[:pieces]
    normed_ref, out_ref, w_ref, sem = refs[pieces:]

    @pl.when(pl.program_id(0) == 0)
    def _():
        if pieces == 1:
            whole = pltpu.make_async_copy(w_in[0], w_ref, sem)
            whole.start()
        else:
            relative_copies(ids_ref, w_in, natural_place(w_ref, w_in[0].shape[-1]), sem)
        pltpu.make_async_copy(w_ref, w_ref, sem).wait()

    normed, _ = rms(x_ref[...].astype(F32), gain_ref[...])
    normed_ref[...] = normed
    width = x_ref.shape[1]
    for s in range(3):
        out_ref[:, s * width : (s + 1) * width] = dot_n(normed, w_ref[s]).astype(BF)


def project(ids, gain, x, pieces):
    rows, width = x.shape
    blocks = rows // TB
    spec = tokens_block()
    full = (3, width, width)
    shape = jax.ShapeDtypeStruct
    return pl.pallas_call(
        functools.partial(project_kernel, len(pieces)),
        grid=(blocks,),
        in_specs=[pl.BlockSpec(memory_space=pltpu.SMEM), held((1, width)), spec(blocks, width)]
        + [pl.BlockSpec(memory_space=pl.ANY)] * len(pieces),
        out_specs=[spec(blocks, width), spec(blocks, 3 * width), held(full)],
        out_shape=[shape((rows, width), BF), shape((rows, 3 * width), BF), shape(full, BF)],
        scratch_shapes=[pltpu.SemaphoreType.DMA],
        compiler_params=params(),
        cost_estimate=cost(6 * rows * width * width, 10 * rows * width + 6 * width * width),
        name="project",
    )(ids, gain, x, *pieces)


def middle_kernel(gain_ref, x_ref, mixed_ref, memory_ref, w_in, resid_ref, normed_ref, q_ref, k_ref, v_ref, w_ref, sem):
    @pl.when(pl.program_id(0) == 0)
    def _():
        if len(w_in.shape) == 3:
            pltpu.make_async_copy(w_in, w_ref, sem).start()
        else:
            plain_copies(w_in, w_ref, sem)
        pltpu.make_async_copy(w_ref, w_ref, sem).wait()

    resid = x_ref[...].astype(F32) + dot_t(mixed_ref[...], w_ref[0])
    resid_ref[...] = resid
    normed, _ = rms(resid, gain_ref[...])
    normed_ref[...] = normed
    q_ref[...] = dot_n(normed, w_ref[1]).astype(BF)
    memory = memory_ref[...]
    k_ref[...] = dot_n(memory, w_ref[2]).astype(BF)
    v_ref[...] = dot_n(memory, w_ref[3]).astype(BF)


def middle(gain, x, mixed, memory, w):
    rows, width = x.shape
    blocks = rows // TB
    spec = tokens_block()(blocks, width)
    full = (5, width, width)
    return pl.pallas_call(
        middle_kernel,
        grid=(blocks,),
        in_specs=[held((1, width)), spec, spec, spec, pl.BlockSpec(memory_space=pl.ANY)],
        out_specs=[spec] * 5 + [held(full)],
        out_shape=[jax.ShapeDtypeStruct((rows, width), F32)] + [jax.ShapeDtypeStruct((rows, width), BF)] * 4
        + [jax.ShapeDtypeStruct(full, BF)],
        scratch_shapes=[pltpu.SemaphoreType.DMA],
        compiler_params=params(),
        cost_estimate=cost(8 * rows * width * width, 20 * rows * width + 10 * width * width),
        name="middle",
    )(gain, x, mixed, memory, w)


def feed_kernel(blocks, pieces, ids_ref, docs_ref, gain_ref, resid_ref, mixed_ref, cot_ref, wo_ref, *refs):
    w_in = refs[:pieces]
    (out_ref, out_low_ref, grad_ref, gmix_ref, gain_grad_ref, wgrad_ref,
     w_ref, normed_t, branch_t, hidden_s, gate_s, up_s, sem) = refs[pieces:]
    step = pl.program_id(0)
    width = resid_ref.shape[1]

    def weight(which, x):
        return w_ref[x, which]

    @pl.when(step == 0)
    def _():
        if pieces == 1:
            pltpu.make_async_copy(w_in[0], w_ref, sem).start()
        else:
            relative_copies(ids_ref, w_in, lambda n, span, x: w_ref.at[x, n, span], sem)
        gain_grad_ref[...] = jnp.zeros_like(gain_grad_ref)
        pltpu.make_async_copy(w_ref, w_ref, sem).wait()

    @pl.when(step < blocks)
    def _():
        first = pl.multiple_of(step * TB, TB)
        span = pl.ds(first, TB)
        resid = resid_ref[...] + dot_t(mixed_ref[...], wo_ref[...])
        normed, inverse = rms(resid, gain_ref[...])
        slots = first + lax.broadcasted_iota(jnp.int32, (TB, 1), 0)
        padding = slots >= docs_ref[0] + docs_ref[1] + docs_ref[2]
        grad_four = jnp.where(padding, 0.0, cot_ref[...].astype(F32))
        branch = grad_four.astype(BF)
        normed_t[:, span] = normed.T
        branch_t[:, span] = branch.T
        total = resid
        upstream = jnp.zeros((TB, width), F32)
        for x in range(2):
            gate = dot_n(normed, weight(0, x))
            up = dot_n(normed, weight(1, x))
            lifted = dot_n(branch, weight(2, x))
            square = gate * gate
            inner = jnp.tanh(gate * (0.7978845608028654 + 0.035677408136300125 * square))
            half_up = 0.5 + 0.5 * inner
            activated = gate * half_up
            slope = half_up + (0.5 * gate) * (1.0 - inner * inner) * (
                0.7978845608028654 + 0.10703222440890037 * square
            )
            hidden = (activated * up).astype(BF)
            gate_grad = (lifted * up * slope).astype(BF)
            up_grad = (lifted * activated).astype(BF)
            hidden_s[x, span, :] = hidden
            gate_s[x, span, :] = gate_grad
            up_s[x, span, :] = up_grad
            total = total + dot_t(hidden, weight(2, x))
            upstream = upstream + dot_t(gate_grad, weight(0, x)) + dot_t(up_grad, weight(1, x))
        output = jnp.where(padding, 0.0, total)
        out_ref[...] = output
        out_low_ref[...] = output.astype(BF)
        grad_resid, gain_grad = rms_back(resid, inverse, gain_ref[...], upstream)
        grad = grad_four + grad_resid
        grad_ref[...] = grad
        grad_low = grad.astype(BF)
        gain_grad_ref[...] += gain_grad
        gmix_ref[...] = dot_n(grad_low, wo_ref[...]).astype(BF)

    for which, (left, right) in enumerate(((normed_t, gate_s), (normed_t, up_s), (branch_t, hidden_s))):
        for x in range(2):

            @pl.when(step == blocks + 2 * which + x)
            def _():
                wgrad = dot_n(left[...], right[x]).astype(BF)
                wgrad_ref[...] = wgrad.reshape(wgrad_ref.shape)


def feed(ids, docs, gain, resid, mixed, cot, wo, pieces, parts):
    rows, width = resid.shape
    half = pieces[0].shape[-1]
    depth = width // parts
    blocks = rows // TB
    spec = tokens_block()(blocks, width)
    shape = jax.ShapeDtypeStruct

    def wgrad_at(s):
        at = jnp.maximum(s - blocks, 0)
        return (0, at % 2, at // 2, 0, 0)

    return pl.pallas_call(
        functools.partial(feed_kernel, blocks, len(pieces)),
        grid=(blocks + 6,),
        in_specs=[
            pl.BlockSpec(memory_space=pltpu.SMEM), pl.BlockSpec(memory_space=pltpu.SMEM),
            held((1, width)), spec, spec, spec, held(wo.shape),
        ] + [pl.BlockSpec(memory_space=pl.ANY)] * len(pieces),
        out_specs=[spec, spec, spec, spec, held((1, width)), pl.BlockSpec((parts, None, None, depth, half), wgrad_at)],
        out_shape=[
            shape((rows, width), F32),
            shape((rows, width), BF),
            shape((rows, width), F32),
            shape((rows, width), BF),
            shape((1, width), F32),
            shape((parts, 2, 3, depth, half), BF),
        ],
        scratch_shapes=[pltpu.VMEM((2, 3, width, half), BF)] + [pltpu.VMEM((width, rows), BF)] * 2
        + [pltpu.VMEM((2, rows, half), BF)] * 3 + [pltpu.SemaphoreType.DMA],
        compiler_params=params(),
        cost_estimate=cost(36 * rows * width * half, 24 * rows * width + 24 * width * half),
        name="feed",
    )(ids, docs, gain, resid, mixed, cot, wo, *pieces)


def pack_blocks(ids_ref, full_ref, keep_ref, send_ref):
    mine = ids_ref[0]
    x_at = ids_ref[1]
    n, rows, cols = keep_ref.shape[-3:]

    def copy(flip):
        for target, part in ((keep_ref, 0), (send_ref, 1)):
            for y in range(2):
                for z0 in range(2):
                    for z1 in range(2):
                        block = jnp.bitwise_xor(mine, 8 * z1 + 4 * z0 + 2 * y + part)
                        span = pl.ds(pl.multiple_of(block * rows, 16), rows)
                        for x in range(2):
                            first = cols * (x ^ flip)
                            target[y, x, z0, z1] = full_ref[:, span, first : first + cols]

    @pl.when(x_at == 0)
    def _():
        copy(0)

    @pl.when(x_at == 1)
    def _():
        copy(1)


def packed_shapes(n, width):
    return jax.ShapeDtypeStruct((2, 2, 2, 2, n, width // 16, width // 2), BF)


def cross_back_kernel(blocks, packed, ids_ref, gain_ref, d_ref, resid_ref, normed_ref, memory_ref, grad_ref,
                      mixed_cross_ref, mixed_self_ref, w_ref, *outs):
    (grad_two_ref, gmix_ref, gmem_ref, gmem_low_ref, gain_grad_ref) = outs[:5]
    rest = outs[5:]
    if packed:
        keep_ref, send_ref, full = rest[0], rest[1], rest[-1]
        rest = rest[2:-1]
    else:
        full = rest[0]
        rest = rest[1:]
    lefts, rights = rest
    step = pl.program_id(0)

    @pl.when(step == 0)
    def _():
        gain_grad_ref[...] = jnp.zeros_like(gain_grad_ref)

    @pl.when(step < blocks)
    def _():
        span = pl.ds(pl.multiple_of(step * TB, TB), TB)
        resid = resid_ref[...]
        inverse = lax.rsqrt(jnp.mean(resid * resid, axis=-1, keepdims=True) + epsilon)
        grad_resid, gain_grad = rms_back(resid, inverse, gain_ref[...], dot_t(d_ref[0], w_ref[1]))
        gain_grad_ref[...] += gain_grad
        grad_three = grad_ref[...]
        grad_two = grad_three + grad_resid
        grad_two_ref[...] = grad_two
        branch = grad_two.astype(BF)
        gmix_ref[...] = dot_n(branch, w_ref[0]).astype(BF)
        gmem = dot_t(d_ref[1], w_ref[2]) + dot_t(d_ref[2], w_ref[3])
        gmem_ref[...] = gmem
        gmem_low_ref[...] = gmem.astype(BF)
        lefts[0, :, span] = branch.T
        lefts[1, :, span] = normed_ref[...].T
        lefts[2, :, span] = memory_ref[...].T
        lefts[3, :, span] = grad_three.astype(BF).T
        rights[0, span, :] = mixed_self_ref[...]
        rights[1, span, :] = d_ref[0]
        rights[2, span, :] = d_ref[1]
        rights[3, span, :] = d_ref[2]
        rights[4, span, :] = mixed_cross_ref[...]

    for n, left in enumerate((0, 1, 2, 2, 3)):

        @pl.when(step == blocks + n)
        def _():
            full[n] = dot_n(lefts[left], rights[n]).astype(BF)

    if packed:

        @pl.when(step == blocks + 4)
        def _():
            pack_blocks(ids_ref, full, keep_ref, send_ref)


def cross_back(packed, ids, gain, d, resid, normed, memory, grad, mixed_cross, mixed_self, w):
    rows, width = resid.shape
    blocks = rows // TB
    spec = tokens_block()(blocks, width)
    shape = jax.ShapeDtypeStruct
    full = shape((5, width, width), BF)
    if packed:
        extra = [packed_shapes(5, width)] * 2
        scratch = [pltpu.VMEM(full.shape, BF)]
    else:
        extra = [full]
        scratch = []
    return pl.pallas_call(
        functools.partial(cross_back_kernel, blocks, packed),
        grid=(blocks + 5,),
        in_specs=[
            pl.BlockSpec(memory_space=pltpu.SMEM), held((1, width)), tokens_block(3)(blocks, width),
            spec, spec, spec, spec, spec, spec, held(w.shape),
        ],
        out_specs=[spec, spec, spec, spec, held((1, width))] + [held(e.shape) for e in extra],
        out_shape=[shape((rows, width), F32), shape((rows, width), BF), shape((rows, width), F32),
                   shape((rows, width), BF), shape((1, width), F32)] + extra,
        scratch_shapes=[pltpu.VMEM((4, width, rows), BF), pltpu.VMEM((5, rows, width), BF)] + scratch,
        compiler_params=params(),
        cost_estimate=cost(18 * rows * width * width, 36 * rows * width + 20 * width * width),
        name="cross_back",
    )(ids, gain, d, resid, normed, memory, grad, mixed_cross, mixed_self, w)


def self_weights_kernel(packed, ids_ref, d_ref, normed_ref, *rest):
    if packed:
        keep_ref, send_ref, left, full = rest
    else:
        full, left = rest
    step = pl.program_id(0)

    @pl.when(step == 0)
    def _():
        left[...] = normed_ref[...].T

    full[step] = dot_n(left[...], d_ref[...]).astype(BF)
    if packed:

        @pl.when(step == 2)
        def _():
            pack_blocks(ids_ref, full, keep_ref, send_ref)


def self_weights(packed, ids, d, normed):
    rows, width = normed.shape
    full = jax.ShapeDtypeStruct((3, width, width), BF)
    if packed:
        outs = [packed_shapes(3, width)] * 2
        scratch = [pltpu.VMEM(full.shape, BF)]
    else:
        outs = [full]
        scratch = []
    return pl.pallas_call(
        functools.partial(self_weights_kernel, packed),
        grid=(3,),
        in_specs=[
            pl.BlockSpec(memory_space=pltpu.SMEM),
            pl.BlockSpec((None, rows, width), lambda s: (s, 0, 0)),
            held((rows, width)),
        ],
        out_specs=[held(o.shape) for o in outs],
        out_shape=outs,
        scratch_shapes=[pltpu.VMEM((width, rows), BF)] + scratch,
        compiler_params=params(),
        cost_estimate=cost(6 * rows * width * width, 8 * rows * width + 6 * width * width),
        name="self_weights",
    )(ids, d, normed)


def self_back_kernel(gain_ref, d_ref, x_ref, grad_ref, w_ref, out_ref, low_ref, gain_grad_ref):
    @pl.when(pl.program_id(0) == 0)
    def _():
        gain_grad_ref[...] = jnp.zeros_like(gain_grad_ref)

    values = x_ref[...].astype(F32)
    inverse = lax.rsqrt(jnp.mean(values * values, axis=-1, keepdims=True) + epsilon)
    upstream = dot_t(d_ref[0], w_ref[0]) + dot_t(d_ref[1], w_ref[1]) + dot_t(d_ref[2], w_ref[2])
    grad_values, gain_grad = rms_back(values, inverse, gain_ref[...], upstream)
    gain_grad_ref[...] += gain_grad
    grad = grad_ref[...] + grad_values
    out_ref[...] = grad
    low_ref[...] = grad.astype(BF)


def self_back(gain, d, x, grad, w):
    rows, width = x.shape
    blocks = rows // TB
    spec = tokens_block()(blocks, width)
    shape = jax.ShapeDtypeStruct
    return pl.pallas_call(
        self_back_kernel,
        grid=(blocks,),
        in_specs=[held((1, width)), tokens_block(3)(blocks, width), spec, spec, held(w.shape)],
        out_specs=[spec, spec, held((1, width))],
        out_shape=[shape((rows, width), F32), shape((rows, width), BF), shape((1, width), F32)],
        compiler_params=params(),
        cost_estimate=cost(6 * rows * width * width, 20 * rows * width + 6 * width * width),
        name="self_back",
    )(gain, d, x, grad, w)


def flip_bit(values, bit):
    size = lax.axis_size("dp")
    return lax.ppermute(values, "dp", [(i, i ^ (1 << bit)) for i in range(size)])


def flip_mp(values):
    return lax.ppermute(values, "mp", [(0, 1), (1, 0)])


def after(values, *others):
    return lax.optimization_barrier((values, others))[0]


class Gather:
    def __init__(self, shard):
        self.shard = shard

    def first(self):
        self.state = (flip_bit(self.shard, 3),)

    def second(self):
        self.low = jnp.stack([self.shard, self.state[0]])
        self.state = (flip_bit(self.low, 2),)

    def third(self):
        (high,) = self.state
        self.near = (self.low, high)
        self.state = (flip_mp(self.low), flip_bit(high, 1), flip_bit(self.low, 0), flip_bit(high, 0))

    def fourth(self):
        low, high = self.near
        low_x, high_y, low_c, high_c = self.state
        self.near = (low, low_x, high, high_y, low_c, high_c)
        self.state = (
            flip_bit(low, 1), flip_bit(low_x, 1), flip_mp(high), flip_mp(high_y),
            flip_bit(low_x, 0), flip_bit(high_y, 0),
        )

    def pieces(self):
        low, low_x, high, high_y, low_c, high_c = self.near
        low_y, low_xy, high_x, high_xy, low_x_c, high_y_c = self.state
        return [
            low, low_x, low_y, low_xy, high, high_x, high_y, high_xy,
            low_c, low_x_c, flip_bit(low_y, 0), flip_bit(low_xy, 0),
            high_c, flip_bit(high_x, 0), high_y_c, flip_bit(high_xy, 0),
        ]


class Scatter:
    def __init__(self, keep, send):
        self.keep = keep
        self.send = send

    def own(self, y, x, z0):
        return self.keep[y, x, z0].astype(F32) + self.came[y, x, z0].astype(F32)

    def first(self):
        self.state = (flip_bit(self.send, 0),)

    def second(self):
        (self.came,) = self.state

        def both(*parts):
            return jnp.stack([p.astype(BF) for p in parts])

        self.state = (
            flip_bit(both(self.own(1, 0, 0), self.own(1, 1, 0)), 1),
            flip_mp(both(self.own(0, 1, 1), self.own(1, 1, 1))),
        )

    def third(self):
        low_y, high_x = self.state
        self.kept = (low_y, high_x)
        self.state = (
            flip_mp((self.own(0, 1, 0) + low_y[1].astype(F32)).astype(BF)),
            flip_bit((self.own(1, 0, 1) + high_x[1].astype(F32)).astype(BF), 1),
        )

    def fourth(self):
        low_y, high_x = self.kept
        low_x, high_y = self.state
        high = self.own(0, 0, 1) + high_x[0].astype(F32) + high_y.astype(F32)
        self.kept = self.own(0, 0, 0) + low_y[0].astype(F32) + low_x.astype(F32)
        self.state = (flip_bit(high.astype(BF), 2),)

    def fifth(self):
        self.kept = self.kept + self.state[0].astype(F32)
        self.state = (flip_bit(self.kept[1].astype(BF), 3),)

    def total(self):
        return self.kept[0] + self.state[0].astype(F32)


def hold(value, *steps):
    value, states = lax.optimization_barrier((value, [s.state for s in steps]))
    for step, state in zip(steps, states):
        step.state = state
    return value


def gather_plain(shard):
    pieces = lax.all_gather(shard, ("dp", "mp"), axis=0)
    return pieces.reshape((lax.axis_size("dp"), lax.axis_size("mp")) + shard.shape)


def gather_whole(shard):
    n, rows, cols = shard.shape
    pieces = gather_plain(shard)
    dp, mp = pieces.shape[:2]
    return pieces.transpose(2, 0, 3, 1, 4).reshape(n, dp * rows, mp * cols)


def scatter_plain(pieces):
    flat = pieces.reshape((-1,) + pieces.shape[2:])
    return lax.psum_scatter(flat, ("dp", "mp"), scatter_dimension=0, tiled=True)[0].astype(F32)


def scatter_whole(grads):
    dp = lax.axis_size("dp")
    mp = lax.axis_size("mp")
    n, rows, cols = grads.shape
    return scatter_plain(grads.reshape(n, dp, rows // dp, mp, cols // mp).transpose(1, 3, 0, 2, 4))


class Sum:
    def __init__(self, values):
        self.held = values
        self.state = None

    def flip(self, bit):
        if self.state is not None:
            self.held = self.held + self.state
        self.state = flip_bit(self.held, bit)

    @property
    def values(self):
        return self.held if self.state is None else self.held + self.state


class Swap:
    def __init__(self, sent):
        self.state = flip_mp(sent)


def other_row(pair_rows, me):
    return lax.dynamic_index_in_dim(pair_rows, 1 - me, 0, False)


def whole_row(pair_rows, swap, me):
    kept = lax.dynamic_index_in_dim(pair_rows, me, 0, False)
    came = swap.state
    return jnp.where(me == 0, jnp.concatenate([kept, came]), jnp.concatenate([came, kept]))


def other_half(low, me):
    half = low.shape[0] // 2
    return lax.dynamic_slice_in_dim(low, (1 - me) * half, half, 0)


def row_halves(row, swap, me):
    half = row.shape[0] // 2
    kept = lax.dynamic_slice_in_dim(row, me * half, half, 0)
    came = swap.state.astype(F32)
    return jnp.where(me == 0, jnp.stack([kept, came]), jnp.stack([came, kept]))


def per_device(
    tokens,
    memory,
    doc_lengths,
    mem_lengths,
    norm_gains,
    rel_table,
    self_proj,
    self_out,
    cross_proj,
    cross_out,
    ffn_proj,
    ffn_out,
    cotangent,
):
    me = lax.axis_index("mp")
    dp = lax.axis_size("dp")
    width = tokens.shape[2]
    packed = dp == 16 and lax.axis_size("mp") == 2
    ids = jnp.stack([lax.axis_index("dp"), me]).astype(jnp.int32)
    docs = lax.dynamic_index_in_dim(doc_lengths, me, 0, False)
    mem_length = lax.dynamic_slice_in_dim(mem_lengths, me, 1, 0)
    band = bias_band(rel_table)
    gains = [norm_gains[i : i + 1] for i in range(3)]

    shard_mid = jnp.concatenate([self_out.T[None], cross_proj, cross_out.T[None]])
    shard_ffn = jnp.concatenate([ffn_proj, ffn_out.T[None]])
    token_swap = Swap(other_row(tokens, me))
    if packed:
        w_mid = gather_plain(shard_mid)
        w_one = Gather(self_proj)
        w_one.first()
        w_one.second()
        hold((), w_one, token_swap)
        w_one.third()
        hold((), w_one)
        w_one.fourth()
        hold((), w_one)
        w_self = w_one.pieces()
        w_self, shard_ffn, memory, cotangent = lax.optimization_barrier((w_self, shard_ffn, memory, cotangent))
        w_two = Gather(shard_ffn)
        w_two.first()
    else:
        w_self = [gather_whole(self_proj)]
        w_mid = gather_whole(shard_mid)
        w_ffn = gather_whole(shard_ffn)
        w_ffn = [w_ffn.reshape(3, width, 2, -1).transpose(2, 0, 1, 3)]
    memory_swap = Swap(other_row(memory, me))
    x = whole_row(tokens, token_swap, me)
    normed_one, qkv, w_self = project(ids, gains[0], x, w_self)
    if packed:
        qkv = hold(qkv, w_two, memory_swap)
        w_two.second()
    cot_swap = Swap(other_row(cotangent, me))
    mixed_self, qa_self = attention_forward(True, docs, band, (qkv, 0), (qkv, 6), (qkv, 12), width)
    if packed:
        mixed_self = hold(mixed_self, w_two, cot_swap)
        w_two.third()
    memory_row = whole_row(memory, memory_swap, me)
    resid_two, normed_two, q_cross, k_cross, v_cross, w_mid = middle(gains[1], x, mixed_self, memory_row, w_mid)
    if packed:
        q_cross = hold(q_cross, w_two)
        w_two.fourth()
    mixed_cross, qa_cross = attention_forward(
        False, mem_length, band, (q_cross, 0), (k_cross, 0), (v_cross, 0), width
    )
    if packed:
        mixed_cross = hold(mixed_cross, w_two)
        w_ffn = w_two.pieces()
    cot_row = whole_row(cotangent, cot_swap, me)
    output, output_low, grad_three, grad_mixed, gain_three, ffn_grads = feed(
        ids, docs, gains[2], resid_two, mixed_cross, cot_row, w_mid[4], w_ffn, dp if packed else 1
    )
    output_swap = Swap(other_half(output_low, me))
    if packed:
        ffn_grads = scatter_plain(ffn_grads)
    else:
        ffn_grads = scatter_whole(ffn_grads[0].transpose(1, 2, 0, 3).reshape(3, width, -1))
    grads_cross, _ = attention_backward(
        False, mem_length, band, qa_cross, (k_cross, 0), (v_cross, 0), grad_mixed, mixed_cross, width
    )
    grads_cross = hold(grads_cross, output_swap)
    grad_two, grad_mixed, gmem, gmem_low, gain_two, *mid_grads = cross_back(
        packed, ids, gains[1], grads_cross, resid_two, normed_two, memory_row, grad_three, mixed_cross, mixed_self, w_mid
    )
    memory_swap = Swap(other_half(gmem_low, me))
    if packed:
        mid = Scatter(*mid_grads)
        mid.first()
    pairs = width // LANES
    grads_self, sums = attention_backward(
        True, docs, band, qa_self, (qkv, 6), (qkv, 12), grad_mixed, mixed_self, width, 0, pairs // 2
    )
    if packed:
        grads_self = hold(grads_self, mid, memory_swap)
        mid.second()
    grads_self, more_sums = attention_backward(
        True, docs, band, qa_self, (qkv, 6), (qkv, 12), grad_mixed, mixed_self, width, pairs // 2, pairs, grads_self
    )
    sums = jnp.concatenate([sums, more_sums])
    table = table_gradient(sums).reshape(1, -1)
    if packed:
        grads_self, table = hold((grads_self, table), mid)
        mid.third()
    self_grads = self_weights(packed, ids, grads_self, normed_one)
    if packed:
        self_grads = hold(self_grads, mid)
        mid.fourth()
        last = Scatter(*self_grads)
        last.first()
    grad_x, grad_x_low, gain_one = self_back(gains[0], grads_self, x, grad_two, w_self)
    if packed:
        grad_x_low, gain_one = hold((grad_x_low, gain_one), mid, last)
        mid.fifth()
        last.second()
    token_swap = Swap(other_half(grad_x_low, me))
    pad = width - table.shape[1]
    small = Sum(jnp.concatenate([gain_one, gain_two, gain_three, jnp.pad(table, ((0, 0), (0, pad)))]))
    if packed:
        small.flip(0)
        hold((), mid, last, small)
        last.third()
        small.flip(1)
        hold((), last, small)
        last.fourth()
        small.flip(2)
        hold((), last, small)
        last.fifth()
        small.flip(3)
        hold((), last, small)
        mid_grads = mid.total()
        self_grads = last.total()
        small = small.values + flip_mp(small.values)
    else:
        mid_grads = scatter_whole(mid_grads[0])
        self_grads = scatter_whole(self_grads[0])
        small = lax.psum(small.values, ("dp", "mp"))
    output = row_halves(output, output_swap, me)
    grad_memory = row_halves(gmem, memory_swap, me)
    grad_tokens = row_halves(grad_x, token_swap, me)
    return (
        output,
        grad_tokens,
        grad_memory,
        small[:3],
        small[3, : NB * rel_table.shape[1]].reshape(rel_table.shape),
        self_grads,
        mid_grads[0].T,
        mid_grads[1:4],
        mid_grads[4].T,
        ffn_grads[:2],
        ffn_grads[2].T,
    )


def solution(mesh):
    rows = P("dp", "mp", None)
    proj = P(None, "dp", "mp")
    out = P("mp", "dp")
    return jax.shard_map(
        per_device,
        mesh=mesh,
        in_specs=(rows, rows, P("dp", None), P("dp"), P(), P(), proj, out, proj, out, proj, out, rows),
        out_specs=(rows, rows, rows, P(), P(), proj, out, proj, out, proj, out),
        check_vma=False,
    )
```

```python
import functools
import jax
import jax.numpy as jnp
import numpy as np
from jax import lax
from jax.experimental import pallas as pl
from jax.experimental.pallas import tpu as pltpu
from jax.sharding import PartitionSpec as P

DH = 64
NB = 32
REACH = 128
ROW = 1024
LANES = 128
QB = 256
masked_score = -1000000000.0
BF = jnp.bfloat16
F32 = jnp.float32
FORWARD_MB = 56
BACKWARD_MB = 56
PROJECT_MB = 56
MIDDLE_MB = 56
FEED_MB = 60
CROSS_BACK_MB = 56
WEIGHTS_MB = 56
SELF_BACK_MB = 56


def params(megabytes):
    return pltpu.CompilerParams(vmem_limit_bytes=megabytes * 1024 * 1024, dimension_semantics=("arbitrary",))


def dot_t(a, b):
    return lax.dot_general(a, b, (((1,), (1,)), ((), ())), preferred_element_type=F32)


def dot_n(a, b):
    return lax.dot_general(a, b, (((1,), (0,)), ((), ())), preferred_element_type=F32)


def dot_tn(a, b):
    return lax.dot_general(a, b, (((0,), (0,)), ((), ())), preferred_element_type=F32)


def split_three(x):
    top = x.astype(BF)
    rest = x - top.astype(F32)
    mid = rest.astype(BF)
    low = (rest - mid.astype(F32)).astype(BF)
    return top.astype(F32), mid.astype(F32), low.astype(F32)


def place_three(x, slot, other):
    top, mid, low = split_three(x)
    return jnp.where(slot == 4, top, jnp.where(slot == 5, mid, jnp.where(slot == 6, low, other)))


def lane_slots(shape):
    lane = lax.broadcasted_iota(jnp.int32, shape, 1)
    return lane, lane % DH


def make_extras(ids_ref, bounds_ref, causal, extra_q, extra_k):
    me = ids_ref[1]
    shape = extra_q.shape
    _, slot = lane_slots(shape)
    rows = lax.broadcasted_iota(jnp.int32, shape, 0)
    if causal:
        first = bounds_ref[me, 0]
        second = first + bounds_ref[me, 1]
        third = second + bounds_ref[me, 2]
        seg = (
            (rows >= first).astype(jnp.int32)
            + (rows >= second).astype(jnp.int32)
            + (rows >= third).astype(jnp.int32)
        )
        own = jnp.where(slot == seg, 1.0, 0.0)
        barred = jnp.where((slot < 4) & (slot != seg), masked_score, 0.0)
    else:
        own = jnp.where(slot == 0, 1.0, 0.0)
        barred = jnp.where((slot == 0) & (rows >= bounds_ref[me]), masked_score, 0.0)
    extra_q[...] = jnp.where(slot == 7, 1.0, own).astype(BF)
    extra_k[...] = jnp.where((slot >= 4) & (slot <= 6), 1.0, barred).astype(BF)


def band_square(band_ref, head):
    wide = jnp.broadcast_to(band_ref[head : head + 1, :], (LANES, 3 * LANES))
    rolled = pltpu.roll(wide, 0, 1, stride=1, stride_axis=0)
    return rolled[:, LANES : 2 * LANES], rolled[:, :LANES]


def add_band(scores, first, near, side):
    above = jnp.full((LANES, LANES), masked_score, F32)
    corner = jnp.concatenate([side, jnp.zeros((LANES, LANES), F32)], axis=0)
    left = jnp.concatenate([near, side], axis=0)
    right = jnp.concatenate([above, near], axis=0)
    pieces = []
    if first > 0:
        pieces.append(scores[:, : first - LANES])
        pieces.append(scores[:, first - LANES : first] + corner)
    pieces.append(scores[:, first : first + LANES] + left)
    pieces.append(scores[:, first + LANES :] + right)
    return jnp.concatenate(pieces, axis=1)


def forward_kernel(causal, extra, ids_ref, bounds_ref, band_ref, q_ref, k_ref, v_ref, *rest):
    o_ref, qa_ref, extra_q, extra_k = rest[extra:]
    length = q_ref.shape[0]

    @pl.when(pl.program_id(0) == 0)
    def _():
        make_extras(ids_ref, bounds_ref, causal, extra_q, extra_k)

    lane, slot = lane_slots((QB, LANES))
    full_lane, full_slot = lane_slots((length, LANES))
    ones = jnp.where(full_slot == 0, 1.0, 0.0).astype(BF)
    keys, values, bands = [], [], []
    for head in range(2):
        mine = (full_lane < DH) == (head == 0)
        keys.append(jnp.where(mine, k_ref[...], extra_k[...]))
        values.append(jnp.where(mine, v_ref[...], ones))
        if causal:
            bands.append(band_square(band_ref, head))

    def scores_of(block, head):
        first = block * QB
        count = first + QB if causal else length
        mine_block = (lane < DH) == (head == 0)
        queries = jnp.where(mine_block, q_ref[first : first + QB, :], extra_q[first : first + QB, :])
        return queries, dot_t(queries, keys[head][:count])

    todo = [(block, head) for block in range(length // QB) for head in range(2)]
    ahead = [scores_of(*item) for item in todo[:2]]
    for at, (block, head) in enumerate(todo):
        first = block * QB
        span = slice(first, first + QB)
        queries, scores = ahead.pop(0)
        if at + 2 < len(todo):
            ahead.append(scores_of(*todo[at + 2]))
        if causal:
            scores = add_band(scores, first, *bands[head])
        top = jnp.max(scores, axis=1, keepdims=True)
        weights = jnp.exp(scores - top).astype(BF)
        mixed = dot_n(weights, values[head][: weights.shape[1]])
        spare_column = DH if head == 0 else 0
        total = mixed[:, spare_column : spare_column + 1]
        mixed = mixed * (1.0 / total)
        if head == 0:
            kept = mixed
        else:
            o_ref[span, :] = jnp.where(lane < DH, kept, mixed).astype(BF)
        spare = place_three(-(top + jnp.log(total)), slot, queries.astype(F32))
        qa_ref[head, span, :] = jnp.where((lane < DH) == (head == 0), queries, spare.astype(BF))


def backward_kernel(causal, packed, extra, ids_ref, bounds_ref, band_ref, qa_ref, k_ref, v_ref, g_ref, o_ref, *rest):
    if causal:
        rest = rest[:2] + rest[2 + extra :]
        near_ref, normed_ref, grad_ref, bias_ref = rest[:4]
        wgrads = rest[4:-7]
        extra_q, extra_k, dk_acc, dv_acc, near_acc, side_acc, left = rest[-7:]
    else:
        grad_ref, extra_q, extra_k, dk_acc, dv_acc = rest[-5:]
    length = k_ref.shape[0]

    @pl.when(pl.program_id(0) == 0)
    def _():
        make_extras(ids_ref, bounds_ref, causal, extra_q, extra_k)
        if causal:
            put_turned(packed, ids_ref, left, slice(None), normed_ref[...])

    if causal:
        bias_ref[...] = jnp.zeros_like(bias_ref)

    lane, slot = lane_slots((QB, LANES))
    full_lane, full_slot = lane_slots((length, LANES))
    spare_v = jnp.where((full_slot >= 4) & (full_slot <= 6), 1.0, 0.0).astype(BF)
    for head in range(2):
        mine = (full_lane < DH) == (head == 0)
        mine_block = (lane < DH) == (head == 0)
        keys = jnp.where(mine, k_ref[...], extra_k[...])
        values = jnp.where(mine, v_ref[...], spare_v)
        if causal:
            near, side = band_square(band_ref, head)
            near, side = near.T, side.T
            near_only = jnp.full((LANES, LANES), masked_score, F32)
            near_acc[...] = jnp.zeros_like(near_acc)
            side_acc[...] = jnp.zeros_like(side_acc)
        dk_acc[...] = jnp.zeros_like(dk_acc)
        dv_acc[...] = jnp.zeros_like(dv_acc)
        for block in range(length // QB):
            first = block * QB
            count = first + QB if causal else length
            span = slice(first, first + QB)
            queries = qa_ref[head, span, :]
            upstream = g_ref[span, :]
            inner = jnp.sum(
                jnp.where(mine_block, upstream.astype(F32) * o_ref[span, :].astype(F32), 0.0), axis=1, keepdims=True
            )
            spare = place_three(-inner, slot, jnp.zeros((QB, LANES), F32))
            grads = jnp.where(mine_block, upstream, spare.astype(BF))
            scores = dot_t(keys[:count], queries)
            if causal:
                corner = jnp.concatenate([side, jnp.zeros((LANES, LANES), F32)], axis=1)
                upper = jnp.concatenate([near, side], axis=1)
                lower = jnp.concatenate([near_only, near], axis=1)
                pieces = []
                if block > 0:
                    if first > LANES:
                        pieces.append(scores[: first - LANES])
                    pieces.append(scores[first - LANES : first] + corner)
                pieces.append(scores[first : first + LANES] + upper)
                pieces.append(scores[first + LANES :] + lower)
                scores = jnp.concatenate(pieces, axis=0)
            probs = jnp.exp(scores)
            lifted = dot_t(values[:count], grads)
            score_grads = (probs * lifted).astype(BF)
            dv_acc[:count, :] += dot_n(probs.astype(BF), grads)
            dk_acc[:count, :] += dot_n(score_grads, queries)
            dq = dot_tn(score_grads, keys[:count])
            if causal:
                near_acc[...] += score_grads[first : first + LANES, :LANES].astype(F32)
                near_acc[...] += score_grads[first + LANES :, LANES:].astype(F32)
                side_acc[...] += score_grads[first : first + LANES, LANES:].astype(F32)
                if block > 0:
                    side_acc[...] += score_grads[first - LANES : first, :LANES].astype(F32)
            if head == 0:
                grad_ref[0, span, :] = dq.astype(BF)
            else:
                grad_ref[0, span, :] = jnp.where(lane < DH, grad_ref[0, span, :], dq.astype(BF))
        if head == 0:
            grad_ref[1] = dk_acc[...].astype(BF)
            grad_ref[2] = dv_acc[...].astype(BF)
        else:
            grad_ref[1] = jnp.where(full_lane < DH, grad_ref[1], dk_acc[...].astype(BF))
            grad_ref[2] = jnp.where(full_lane < DH, grad_ref[2], dv_acc[...].astype(BF))
        if causal:
            square = jnp.concatenate([side_acc[...], near_acc[...]], axis=0)
            wide = jnp.concatenate([square, jnp.zeros((2 * LANES, 2 * LANES), F32)], axis=1)
            half = LANES
            while half:
                wide = wide[:half] + pltpu.roll(wide[half:], 3 * LANES - half, 1)
                half //= 2
            diag = wide[:, 2 * LANES :]
            ones_column = jnp.where((full_lane % DH == 7) & ~mine, dk_acc[...], 0.0)
            whole = jnp.sum(ones_column, axis=0, keepdims=True)
            table = lax.dot_general(
                diag, near_ref[...], (((1,), (0,)), ((), ())),
                precision=lax.Precision.HIGHEST, preferred_element_type=F32,
            )
            last = jnp.sum(whole, axis=1, keepdims=True) - jnp.sum(table, axis=1, keepdims=True)
            at_last = lax.broadcasted_iota(jnp.int32, table.shape, 1) == NB - 1
            bias_ref[0, head : head + 1, :] = jnp.where(at_last, last, table)
    if causal:
        right = jnp.concatenate([grad_ref[n] for n in range(3)], axis=1)
        grads = dot_n(left[...], right).astype(BF)
        middle_row = grads.shape[0] // 2
        for n in range(3):
            part = grads[:, n * LANES : (n + 1) * LANES]
            if packed:
                shape = wgrads[0].shape[:3] + wgrads[0].shape[4:]
                wgrads[0][:, :, :, n] = part[:middle_row].reshape(shape)
                wgrads[1][:, :, :, n] = part[middle_row:].reshape(shape)
            else:
                wgrads[0][n] = part


def attention_forward(causal, ids, bounds, band, q, k, v, cols, start=0, stop=None, into=()):
    rows = q[0].shape[0]
    pairs = (cols // LANES if stop is None else stop) - start

    def spec(offset):
        return pl.BlockSpec((rows, LANES), lambda p, ids: (0, p + offset + start))

    n = rows * rows * pairs * 2
    return call(
        functools.partial(forward_kernel, causal, len(into)), "attention_forward", FORWARD_MB, pairs,
        [
            pl.BlockSpec(memory_space=pltpu.SMEM),
            pl.BlockSpec((None, 2, 3 * LANES), lambda p, ids: (p + start, 0, 0)),
            spec(q[1]), spec(k[1]), spec(v[1]),
        ] + [anywhere()] * len(into),
        [
            (spec(0), (rows, cols), BF),
            (pl.BlockSpec((2, rows, LANES), lambda p, ids: (p + start, 0, 0)), (2 * cols // LANES, rows, LANES), BF),
        ],
        [pltpu.VMEM((rows, LANES), BF)] * 2,
        n * 256 * 4 // (2 if causal else 1), rows * cols * 16,
        {6: 0, 7: 1} if into else {},
    )(ids, bounds, band, q[0], k[0], v[0], *into)


def cross_backward(ids, bounds, band, qa, k, v, g, o, start, stop, into=()):
    rows, cols = g.shape

    def spec(offset):
        return pl.BlockSpec((rows, LANES), lambda p, ids: (0, p + start + offset))

    n = rows * rows * (stop - start) * 2
    return call(
        functools.partial(backward_kernel, False, False, 0), "cross_backward", BACKWARD_MB, stop - start,
        [
            pl.BlockSpec(memory_space=pltpu.SMEM),
            pl.BlockSpec((None, 2, 3 * LANES), lambda p, ids: (p + start, 0, 0)),
            pl.BlockSpec((2, rows, LANES), lambda p, ids: (p + start, 0, 0)),
            spec(k[1]), spec(v[1]), spec(0), spec(0),
        ] + [anywhere()] * len(into),
        [(pl.BlockSpec((3, rows, LANES), lambda p, ids: (0, 0, p + start)), (3, rows, cols), BF)],
        [pltpu.VMEM((rows, LANES), BF)] * 2 + [pltpu.VMEM((rows, LANES), F32)] * 2,
        n * 256 * 10, rows * cols * 20,
        {8: 0} if into else {},
    )(ids, bounds, band, qa, k[0], v[0], g, o, *into)[0]


def self_backward(side, packed, ids, bounds, band, qa, k, v, g, o, normed, start=0, stop=None, into=()):
    rows, cols = g.shape
    pairs = cols // LANES // 2
    stop = pairs if stop is None else stop
    depth = normed.shape[1] >> BITS

    def at(p, ids):
        return p + start + pairs * jnp.bitwise_xor(ids[1], side)

    def spec(offset):
        return pl.BlockSpec((rows, LANES), lambda p, ids: (0, at(p, ids) + offset))

    n = rows * rows * (stop - start) * 2
    if packed:
        block = pl.BlockSpec((2, 2, 2, 3, depth, LANES), lambda p, ids: (0, 0, 0, 0, 0, p + start))
        wgrads = [(block, (2, 2, 2, 3, depth, cols // 2), BF)] * 2
    else:
        block = pl.BlockSpec((3, normed.shape[1], LANES), lambda p, ids: (0, 0, p + start))
        wgrads = [(block, (3, normed.shape[1], cols // 2), BF)]
    return call(
        functools.partial(backward_kernel, True, packed, len(into)), "self_backward", BACKWARD_MB, stop - start,
        [
            pl.BlockSpec(memory_space=pltpu.SMEM),
            pl.BlockSpec((None, 2, 3 * LANES), lambda p, ids: (at(p, ids), 0, 0)),
            pl.BlockSpec((2, rows, LANES), lambda p, ids: (at(p, ids), 0, 0)),
            spec(k[1]), spec(v[1]), spec(0), spec(0),
            held((LANES, LANES)), held(normed.shape),
        ] + [anywhere()] * len(into),
        [
            (pl.BlockSpec((3, rows, LANES), lambda p, ids: (0, 0, p + start)), (3, rows, cols // 2), BF),
            (pl.BlockSpec((1, 8, LANES), lambda p, ids: (at(p, ids), 0, 0)), (2 * pairs, 8, LANES), F32),
        ] + wgrads,
        [pltpu.VMEM((rows, LANES), BF)] * 2 + [pltpu.VMEM((rows, LANES), F32)] * 2
        + [pltpu.VMEM((LANES, LANES), F32)] * 2 + [pltpu.VMEM((normed.shape[1], rows), BF)],
        n * 256 * 8, rows * cols * 20,
        {10 + i: i for i in range(len(into))},
    )(ids, bounds, band, qa, k[0], v[0], g, o, jnp.asarray(near_buckets()), normed, *into)


def near_buckets():
    buckets = bucket_table(LANES, NB, REACH)
    columns = np.arange(LANES)[None, :]
    return ((buckets[:, None] == columns) & (columns < NB - 1)).astype(np.float32)


def bucket_table(length, buckets, reach):
    offsets = np.arange(length)
    exact_part = buckets // 2
    scaled = np.log(np.maximum(offsets, 1) / exact_part) / np.log(reach / exact_part) * (buckets - exact_part)
    far_bucket = np.minimum(exact_part + np.floor(scaled).astype(np.int64), buckets - 1)
    return np.where(offsets < exact_part, offsets, far_bucket).astype(np.int32)


def bias_band(rel_table):
    distance = LANES - np.arange(3 * LANES)
    buckets = bucket_table(LANES + 1, NB, REACH)
    onehot = np.zeros((3 * LANES, NB), np.float32)
    shift = np.zeros((3 * LANES,), np.float32)
    for at, far in enumerate(distance):
        if 0 <= far < LANES:
            onehot[at, buckets[far]] = 1.0
        elif -LANES < far < 0:
            shift[at] = masked_score
    relative = rel_table - rel_table[NB - 1 :]
    band = jnp.dot(jnp.asarray(onehot), relative, precision=lax.Precision.HIGHEST) + shift[:, None]
    return band.T.reshape(-1, 2, 3 * LANES)


epsilon = 1e-06
TB = 256
BITS = 4


def rms(values, gain):
    inverse = lax.rsqrt(jnp.mean(values * values, axis=-1, keepdims=True) + epsilon)
    return (values * inverse * gain).astype(BF), inverse


def rms_back(values, inverse, gain, upstream):
    weighted = upstream * gain
    inner_mean = jnp.mean(weighted * values, axis=-1, keepdims=True)
    grad_values = inverse * weighted - values * (inverse * inverse * inverse * inner_mean)
    return grad_values, jnp.sum(upstream * values * inverse, axis=0, keepdims=True)


def cost(flops, moved):
    return pl.CostEstimate(flops=flops, bytes_accessed=moved, transcendentals=0)


def turn(s, ids, blocks):
    return ((1 - ids[1]) * (blocks // 2) + jnp.minimum(s, blocks - 1)) % blocks


def row_spec(blocks, width, *lead):
    zeros = (0,) * len(lead)
    return pl.BlockSpec(lead + (TB, width), lambda s, ids: zeros + (turn(s, ids, blocks), 0))


def kept_spec(blocks, width):
    half = blocks // 2
    return pl.BlockSpec((None, TB, width), lambda s, ids: (ids[1], jnp.clip(s - half, 0, half - 1), 0))


def own_spec(blocks, width):
    half = blocks // 2
    return pl.BlockSpec((TB, width), lambda s, ids: (jnp.clip(s - half, 0, half - 1), 0))


def other_spec(blocks, width):
    return pl.BlockSpec((TB, width), lambda s, ids: (jnp.minimum(s, blocks // 2 - 1), 0))


def held(shape):
    zeros = (0,) * len(shape)
    return pl.BlockSpec(shape, lambda s, ids: zeros, pipeline_mode=pl.Buffered(1))


def anywhere():
    return pl.BlockSpec(memory_space=pl.ANY)


def call(kernel, name, megabytes, grid, in_specs, outs, scratch, flops, moved, aliases=None):
    return pl.pallas_call(
        kernel,
        grid_spec=pltpu.PrefetchScalarGridSpec(
            num_scalar_prefetch=1,
            grid=(grid,),
            in_specs=in_specs,
            out_specs=[o[0] for o in outs],
            scratch_shapes=scratch,
        ),
        out_shape=[jax.ShapeDtypeStruct(o[1], o[2]) for o in outs],
        input_output_aliases=aliases or {},
        compiler_params=params(megabytes),
        cost_estimate=cost(flops, moved),
        name=name,
    )


def chosen(step, blocks, came_ref, kept_ref):
    return jnp.where(step < blocks // 2, came_ref[...], kept_ref[...])


def share(step, blocks, values, own_ref, other_ref):
    @pl.when(step < blocks // 2)
    def _():
        other_ref[...] = values.astype(BF)

    @pl.when(step >= blocks // 2)
    def _():
        own_ref[...] = values


def gather_table():
    near = [((0, 0, 0),), ((0, 1, 0),), ((1, 0, 0), (1, 1, 0)), ((0, 0, 1),), ((1, 0, 1),), ((0, 1, 1), (1, 1, 1))]
    table = []
    for c in range(2):
        for places in near:
            entries = []
            for at, (y, x, z0) in enumerate(places):
                for z1 in range(2):
                    entries.append(((at, z1) if len(places) > 1 else (z1,), (y, x, z0, z1, c), 0))
            table.append(entries)
    return table


def wide_table():
    pairs = [(a, b) for a in range(2) for b in range(2)]
    table = []
    for c in range(2):
        for y in range(2):
            table.append([((z0, z1, x), (y, x, z0, z1, c), 0) for x in range(2) for z0, z1 in pairs])
    for c in range(2):
        for z0 in range(2):
            table.append([((z1, y, x), (y, x, z0, z1, c), 1) for x in range(2) for z1, y in pairs])
    return table


def copy_pieces(ids_ref, pieces, table, place, w_ref, sem):
    if len(pieces) == 1:
        pltpu.make_async_copy(pieces[0], w_ref, sem).start()
    else:
        mine = ids_ref[2]
        rows = pieces[0].shape[-2]

        def copy(flip):
            for piece, entries in zip(pieces, table):
                for at, (y, x, z0, z1, c), part in entries:
                    block = jnp.bitwise_xor(mine, 8 * z1 + 4 * z0 + 2 * y + c)
                    span = pl.ds(pl.multiple_of(block * rows, 16), rows)
                    pltpu.make_async_copy(piece.at[at], place(span, x ^ flip, part), sem).start()

        @pl.when(ids_ref[1] == 0)
        def _():
            copy(0)

        @pl.when(ids_ref[1] == 1)
        def _():
            copy(1)

    pltpu.make_async_copy(w_ref, w_ref, sem).wait()


def natural_place(w_ref, cols):
    return lambda span, x, part: w_ref.at[:, span, x * cols : (x + 1) * cols]


def put_turned(packed, ids_ref, target, span, values):
    turned = values.T
    if not packed:
        target[:, span] = turned
        return
    depth = turned.shape[0] >> BITS
    for block in range(1 << BITS):
        reverse = int(format(block, "04b")[::-1], 2)
        at = jnp.bitwise_xor(ids_ref[0], reverse) * depth
        target[pl.ds(pl.multiple_of(at, 16), depth), span] = turned[block * depth : (block + 1) * depth]


def put_grads(packed, ids_ref, n, grads, outs):
    if not packed:
        outs[0][n] = grads
        return
    keep_ref, send_ref = outs
    rows, cols = keep_ref.shape[-2:]
    middle = grads.shape[0] // 2

    def store(flip):
        for x in range(2):
            first = cols * (x ^ flip)
            for target, part in ((keep_ref, grads[:middle]), (send_ref, grads[middle:])):
                block = part[:, first : first + cols].reshape(2, 2, 2, rows, cols)
                target[:, x, :, :, n] = block

    @pl.when(ids_ref[1] == 0)
    def _():
        store(0)

    @pl.when(ids_ref[1] == 1)
    def _():
        store(1)


def grads_out(packed, n, width):
    if not packed:
        shape = (n, width, width)
        return [(held(shape), shape, BF)]
    shape = (2, 2, 2, 2, n, width >> BITS, width // 2)
    return [(held(shape), shape, BF)] * 2


def project_kernel(blocks, pieces, ids_ref, gain_ref, came_ref, kept_ref, *refs):
    w_in = refs[:pieces]
    normed_ref, out_ref, w_ref, sem = refs[pieces:]
    step = pl.program_id(0)

    @pl.when(step == 0)
    def _():
        copy_pieces(ids_ref, w_in, gather_table(), natural_place(w_ref, w_in[0].shape[-1]), w_ref, sem)

    normed, _ = rms(chosen(step, blocks, came_ref, kept_ref).astype(F32), gain_ref[0:1, :])
    normed_ref[...] = normed
    width = normed.shape[1]
    for s in range(3):
        out_ref[:, s * width : (s + 1) * width] = dot_n(normed, w_ref[s]).astype(BF)


def project(ids, gain, came, kept, pieces):
    _, half, width = kept.shape
    rows = 2 * half
    blocks = rows // TB
    full = (3, width, width)
    return call(
        functools.partial(project_kernel, blocks, len(pieces)), "project", PROJECT_MB, blocks,
        [held((3, width)), other_spec(blocks, width), kept_spec(blocks, width)] + [anywhere()] * len(pieces),
        [
            (row_spec(blocks, width), (rows, width), BF),
            (row_spec(blocks, 3 * width), (rows, 3 * width), BF),
            (held(full), full, BF),
        ],
        [pltpu.SemaphoreType.DMA],
        6 * rows * width * width, 10 * rows * width + 6 * width * width,
    )(ids, gain, came, kept, *pieces)


def middle_kernel(blocks, pieces, ids_ref, gain_ref, came_ref, kept_ref, mixed_ref, mem_came_ref, mem_kept_ref, *refs):
    w_in = refs[:pieces]
    resid_ref, normed_ref, q_ref, k_ref, v_ref, w_ref, sem = refs[pieces:]
    step = pl.program_id(0)

    @pl.when(step == 0)
    def _():
        copy_pieces(ids_ref, w_in, gather_table(), natural_place(w_ref, w_in[0].shape[-1]), w_ref, sem)

    resid = chosen(step, blocks, came_ref, kept_ref).astype(F32) + dot_t(mixed_ref[...], w_ref[0])
    resid_ref[...] = resid
    normed, _ = rms(resid, gain_ref[1:2, :])
    normed_ref[...] = normed
    q_ref[...] = dot_n(normed, w_ref[1]).astype(BF)
    memory = chosen(step, blocks, mem_came_ref, mem_kept_ref)
    k_ref[...] = dot_n(memory, w_ref[2]).astype(BF)
    v_ref[...] = dot_n(memory, w_ref[3]).astype(BF)


def middle(ids, gain, came, kept, mixed, mem_came, mem_kept, pieces):
    rows, width = mixed.shape
    blocks = rows // TB
    full = (5, width, width)
    spec = row_spec(blocks, width)
    pair = [other_spec(blocks, width), kept_spec(blocks, width)]
    return call(
        functools.partial(middle_kernel, blocks, len(pieces)), "middle", MIDDLE_MB, blocks,
        [held((3, width))] + pair + [spec] + pair + [anywhere()] * len(pieces),
        [(spec, (rows, width), F32)] + [(spec, (rows, width), BF)] * 4 + [(held(full), full, BF)],
        [pltpu.SemaphoreType.DMA],
        8 * rows * width * width, 20 * rows * width + 10 * width * width,
    )(ids, gain, came, kept, mixed, mem_came, mem_kept, *pieces)


def feed_kernel(blocks, pieces, packed, ids_ref, docs_ref, gain_ref, resid_ref, mixed_ref, cot_came_ref, cot_kept_ref,
                wo_ref, *refs):
    w_in = refs[:pieces]
    refs = refs[pieces:]
    own_ref, other_ref, grad_ref, gmix_ref, gain_grad_ref = refs[:5]
    wgrads = refs[5:-7]
    w_ref, normed_t, branch_t, hidden_s, gate_s, up_s, sem = refs[-7:]
    step = pl.program_id(0)
    me = ids_ref[1]
    width = resid_ref.shape[1]

    def weight(which, x):
        return w_ref[x, which]

    @pl.when(step == 0)
    def _():
        cols = w_in[0].shape[-1]
        copy_pieces(
            ids_ref, w_in, wide_table(),
            lambda span, x, part: w_ref.at[x, :, span, cols * part : cols if part == 0 else None], w_ref, sem,
        )
        gain_grad_ref[...] = jnp.zeros_like(gain_grad_ref)

    @pl.when(step < blocks)
    def _():
        first = pl.multiple_of(turn(step, ids_ref, blocks) * TB, TB)
        span = pl.ds(first, TB)
        resid = resid_ref[...] + dot_t(mixed_ref[...], wo_ref[...])
        normed, inverse = rms(resid, gain_ref[2:3, :])
        slots = first + lax.broadcasted_iota(jnp.int32, (TB, 1), 0)
        padding = slots >= docs_ref[me, 0] + docs_ref[me, 1] + docs_ref[me, 2]
        grad_four = jnp.where(padding, 0.0, chosen(step, blocks, cot_came_ref, cot_kept_ref).astype(F32))
        branch = grad_four.astype(BF)
        put_turned(packed, ids_ref, normed_t, span, normed)
        put_turned(packed, ids_ref, branch_t, span, branch)
        total = resid
        upstream = jnp.zeros((TB, width), F32)
        for x in range(2):
            gate = dot_n(normed, weight(0, x))
            up = dot_n(normed, weight(1, x))
            lifted = dot_n(branch, weight(2, x))
            square = gate * gate
            inner = jnp.tanh(gate * (0.7978845608028654 + 0.035677408136300125 * square))
            half_up = 0.5 + 0.5 * inner
            activated = gate * half_up
            slope = half_up + (0.5 * gate) * (1.0 - inner * inner) * (
                0.7978845608028654 + 0.10703222440890037 * square
            )
            hidden = (activated * up).astype(BF)
            gate_grad = (lifted * up * slope).astype(BF)
            up_grad = (lifted * activated).astype(BF)
            hidden_s[x, span, :] = hidden
            gate_s[x, span, :] = gate_grad
            up_s[x, span, :] = up_grad
            total = total + dot_t(hidden, weight(2, x))
            upstream = upstream + dot_t(gate_grad, weight(0, x)) + dot_t(up_grad, weight(1, x))
        share(step, blocks, jnp.where(padding, 0.0, total), own_ref, other_ref)
        grad_resid, gain_grad = rms_back(resid, inverse, gain_ref[2:3, :], upstream)
        grad = grad_four + grad_resid
        grad_ref[...] = grad
        gain_grad_ref[...] += gain_grad
        gmix_ref[...] = dot_n(grad.astype(BF), wo_ref[...]).astype(BF)

    for which, (left, right) in enumerate(((normed_t, gate_s), (normed_t, up_s), (branch_t, hidden_s))):
        for x in range(2):

            @pl.when(step == blocks + 2 * which + x)
            def _():
                if packed:
                    grads = dot_n(left[...], right[jnp.bitwise_xor(x, me)]).astype(BF)
                    middle_row = grads.shape[0] // 2
                    wgrads[0][...] = grads[:middle_row].reshape(wgrads[0].shape)
                    wgrads[1][...] = grads[middle_row:].reshape(wgrads[1].shape)
                else:
                    wgrads[0][...] = dot_n(left[...], right[x]).astype(BF)


def feed(packed, ids, docs, gain, resid, mixed, cot_came, cot_kept, w_mid, pieces):
    rows, width = resid.shape
    half = pieces[0].shape[-1] if len(pieces) == 1 else pieces[0].shape[-1] + pieces[-1].shape[-1]
    blocks = rows // TB
    spec = row_spec(blocks, width)

    def at(s):
        late = jnp.maximum(s - blocks, 0)
        return late // 2, late % 2

    if packed:
        depth = width >> BITS
        block = pl.BlockSpec((2, None, 2, 2, None, depth, half), lambda s, ids: (0, at(s)[1], 0, 0, at(s)[0], 0, 0))
        wgrads = [(block, (2, 2, 2, 2, 3, depth, half), BF)] * 2
    else:
        block = pl.BlockSpec((None, None, width, half), lambda s, ids: (at(s)[1], at(s)[0], 0, 0))
        wgrads = [(block, (2, 3, width, half), BF)]
    return call(
        functools.partial(feed_kernel, blocks, len(pieces), packed), "feed", FEED_MB, blocks + 6,
        [pl.BlockSpec(memory_space=pltpu.SMEM), held((3, width)), spec, spec, other_spec(blocks, width),
         kept_spec(blocks, width),
         pl.BlockSpec((None, width, width), lambda s, ids: (4, 0, 0), pipeline_mode=pl.Buffered(1))]
        + [anywhere()] * len(pieces),
        [
            (own_spec(blocks, width), (rows // 2, width), F32),
            (other_spec(blocks, width), (rows // 2, width), BF),
            (spec, (rows, width), F32),
            (spec, (rows, width), BF),
            (held((1, width)), (1, width), F32),
        ] + wgrads,
        [pltpu.VMEM((2, 3, width, half), BF)] + [pltpu.VMEM((width, rows), BF)] * 2
        + [pltpu.VMEM((2, rows, half), BF)] * 3 + [pltpu.SemaphoreType.DMA],
        36 * rows * width * half, 24 * rows * width + 24 * width * half,
    )(ids, docs, gain, resid, mixed, cot_came, cot_kept, w_mid, *pieces)


def cross_back_kernel(blocks, packed, ids_ref, gain_ref, d_ref, resid_ref, normed_ref, mem_came_ref, mem_kept_ref,
                      grad_ref, mixed_cross_ref, mixed_self_ref, w_ref, *outs):
    grad_two_ref, gmix_ref, gmem_own_ref, gmem_other_ref, gain_grad_ref = outs[:5]
    wgrads = outs[5:-2]
    lefts, rights = outs[-2:]
    step = pl.program_id(0)

    @pl.when(step == 0)
    def _():
        gain_grad_ref[...] = jnp.zeros_like(gain_grad_ref)

    @pl.when(step < blocks)
    def _():
        span = pl.ds(pl.multiple_of(turn(step, ids_ref, blocks) * TB, TB), TB)
        resid = resid_ref[...]
        inverse = lax.rsqrt(jnp.mean(resid * resid, axis=-1, keepdims=True) + epsilon)
        grad_resid, gain_grad = rms_back(resid, inverse, gain_ref[1:2, :], dot_t(d_ref[0], w_ref[1]))
        gain_grad_ref[...] += gain_grad
        grad_three = grad_ref[...]
        grad_two = grad_three + grad_resid
        grad_two_ref[...] = grad_two
        branch = grad_two.astype(BF)
        gmix_ref[...] = dot_n(branch, w_ref[0]).astype(BF)
        gmem = dot_t(d_ref[1], w_ref[2]) + dot_t(d_ref[2], w_ref[3])
        share(step, blocks, gmem, gmem_own_ref, gmem_other_ref)
        memory = chosen(step, blocks, mem_came_ref, mem_kept_ref)
        for n, values in enumerate((branch, normed_ref[...], memory, grad_three.astype(BF))):
            put_turned(packed, ids_ref, lefts.at[n], span, values)
        rights[0, span, :] = mixed_self_ref[...]
        rights[1, span, :] = d_ref[0]
        rights[2, span, :] = d_ref[1]
        rights[3, span, :] = d_ref[2]
        rights[4, span, :] = mixed_cross_ref[...]

    for n, left in enumerate((0, 1, 2, 2, 3)):

        @pl.when(step == blocks + n)
        def _():
            put_grads(packed, ids_ref, n, dot_n(lefts[left], rights[n]).astype(BF), wgrads)


def cross_back(packed, ids, gain, d, resid, normed, mem_came, mem_kept, grad, mixed_cross, mixed_self, w):
    rows, width = resid.shape
    blocks = rows // TB
    spec = row_spec(blocks, width)
    return call(
        functools.partial(cross_back_kernel, blocks, packed), "cross_back", CROSS_BACK_MB, blocks + 5,
        [held((3, width)), row_spec(blocks, width, 3), spec, spec, other_spec(blocks, width), kept_spec(blocks, width),
         spec, spec, spec, held(w.shape)],
        [
            (spec, (rows, width), F32),
            (spec, (rows, width), BF),
            (own_spec(blocks, width), (rows // 2, width), F32),
            (other_spec(blocks, width), (rows // 2, width), BF),
            (held((1, width)), (1, width), F32),
        ] + grads_out(packed, 5, width),
        [pltpu.VMEM((4, width, rows), BF), pltpu.VMEM((5, rows, width), BF)],
        18 * rows * width * width, 36 * rows * width + 20 * width * width,
    )(ids, gain, d, resid, normed, mem_came, mem_kept, grad, mixed_cross, mixed_self, w)


def self_back_kernel(blocks, ids_ref, gain_ref, ours_ref, theirs_ref, came_ref, kept_ref, grad_ref, w_ref,
                     own_ref, other_ref, gain_grad_ref):
    step = pl.program_id(0)

    @pl.when(step == 0)
    def _():
        gain_grad_ref[...] = jnp.zeros_like(gain_grad_ref)

    values = chosen(step, blocks, came_ref, kept_ref).astype(F32)
    inverse = lax.rsqrt(jnp.mean(values * values, axis=-1, keepdims=True) + epsilon)
    upstream = jnp.zeros(values.shape, F32)
    for n in range(3):
        ours, theirs = ours_ref[n], theirs_ref[n]
        first = jnp.where(ids_ref[1] == 0, ours, theirs)
        second = jnp.where(ids_ref[1] == 0, theirs, ours)
        upstream = upstream + dot_t(jnp.concatenate([first, second], axis=1), w_ref[n])
    grad_values, gain_grad = rms_back(values, inverse, gain_ref[0:1, :], upstream)
    gain_grad_ref[...] += gain_grad
    share(step, blocks, grad_ref[...] + grad_values, own_ref, other_ref)


def self_back(ids, gain, ours, theirs, came, kept, grad, w):
    rows, width = grad.shape
    blocks = rows // TB
    part = row_spec(blocks, width // 2, 3)
    return call(
        functools.partial(self_back_kernel, blocks), "self_back", SELF_BACK_MB, blocks,
        [held((3, width)), part, part, other_spec(blocks, width), kept_spec(blocks, width),
         row_spec(blocks, width), held(w.shape)],
        [
            (own_spec(blocks, width), (rows // 2, width), F32),
            (other_spec(blocks, width), (rows // 2, width), BF),
            (held((1, width)), (1, width), F32),
        ],
        [],
        6 * rows * width * width, 20 * rows * width + 6 * width * width,
    )(ids, gain, ours, theirs, came, kept, grad, w)


def flip_bit(values, bit):
    size = lax.axis_size("dp")
    return lax.ppermute(values, "dp", [(i, i ^ (1 << bit)) for i in range(size)])


def flip_mp(values):
    return lax.ppermute(values, "mp", [(0, 1), (1, 0)])


class Steps:
    def send(self, *parts):
        self.sent = [part[0] for part in parts]
        self.bits = [part[1] for part in parts]

    def launch(self):
        self.state = [flip_mp(a) if bit is None else flip_bit(a, bit) for a, bit in zip(self.sent, self.bits)]


def begin(value, *steps):
    value, sent = lax.optimization_barrier((value, [s.sent for s in steps]))
    for step, arrays in zip(steps, sent):
        step.sent = arrays
        step.launch()
    return value


def hold(value, *steps):
    value, states = lax.optimization_barrier((value, [s.state for s in steps]))
    for step, state in zip(steps, states):
        step.state = state
    return value


class Swap(Steps):
    def __init__(self, sent):
        self.send((sent, None))


class Gather(Steps):
    def __init__(self, shard):
        self.shard = shard
        self.low_c = None
        self.send((shard, 3))

    def second(self):
        self.low = jnp.stack([self.shard, self.state[0]])
        self.send((self.low, 2))

    def third(self):
        (self.high,) = self.state
        self.send((self.low, None), (self.high, 1))

    def fourth(self):
        self.low_x, self.high_y = self.state
        self.send((jnp.stack([self.low, self.low_x]), 1), (jnp.stack([self.high, self.high_y]), None))

    def over_cores(self):
        self.low_c = flip_bit(self.low, 0)
        self.high_c = flip_bit(self.high, 0)

    def pieces(self):
        low_y, high_x = self.state
        if self.low_c is None:
            self.over_cores()
        return [
            self.low, self.low_x, low_y, self.high, self.high_y, high_x,
            self.low_c, flip_bit(self.low_x, 0), flip_bit(low_y, 0),
            self.high_c, flip_bit(self.high_y, 0), flip_bit(high_x, 0),
        ]


class WideGather(Steps):
    def __init__(self, proj, out):
        self.shard = jnp.concatenate([proj, out])
        self.send((proj, None), (out, None))

    def split(self):
        both = jnp.stack([self.shard, jnp.concatenate(self.state)])
        cut = both.shape[-1] * 5 // 8
        return WidePart(both[..., :cut], 3), WidePart(both[..., cut:], 1)


class WidePart(Steps):
    def __init__(self, near, bit):
        self.near = near
        self.send((near, bit))

    def flip(self, bit):
        self.near = jnp.stack([self.near, self.state[0]])
        self.send((self.near, bit))

    def pieces(self):
        near = [self.near, self.state[0]]
        return near + [flip_bit(piece, 0) for piece in near]


class Scatter(Steps):
    def __init__(self, keep, send):
        self.keep = keep
        self.send((send, 0))

    def own(self, *at):
        return self.keep[at].astype(F32) + self.came[at].astype(F32)

    def second(self):
        (self.came,) = self.state
        every = slice(None)
        self.send((self.own(1, every, 0).astype(BF), 1), (self.own(every, 1, 1).astype(BF), None))

    def third(self):
        low_y, high_x = self.state
        self.kept = (low_y, high_x)
        self.send(
            ((self.own(0, 1, 0) + low_y[1].astype(F32)).astype(BF), None),
            ((self.own(1, 0, 1) + high_x[1].astype(F32)).astype(BF), 1),
        )

    def fourth(self):
        low_y, high_x = self.kept
        low_x, high_y = self.state
        high = self.own(0, 0, 1) + high_x[0].astype(F32) + high_y.astype(F32)
        self.kept = self.own(0, 0, 0) + low_y[0].astype(F32) + low_x.astype(F32)
        self.send((high.astype(BF), 2))

    def fifth(self):
        self.kept = self.kept + self.state[0].astype(F32)
        self.send((self.kept[1].astype(BF), 3))

    def total(self):
        return self.kept[0] + self.state[0].astype(F32)


class SideScatter(Steps):
    def __init__(self, keep, send):
        self.kept = keep
        self.send((send, 0))

    def take(self):
        self.kept = self.kept.astype(F32) + self.state[0].astype(F32)

    def flip(self, bit):
        self.take()
        self.send((self.kept[1].astype(BF), bit))
        self.kept = self.kept[0]

    def across(self):
        self.take()
        self.send((self.kept.astype(BF), None))


def gather_whole(shard):
    n, rows, cols = shard.shape
    dp = lax.axis_size("dp")
    mp = lax.axis_size("mp")
    pieces = lax.all_gather(shard, ("dp", "mp"), axis=0).reshape(dp, mp, n, rows, cols)
    return pieces.transpose(2, 0, 3, 1, 4).reshape(n, dp * rows, mp * cols)


def scatter_whole(grads):
    dp = lax.axis_size("dp")
    mp = lax.axis_size("mp")
    n, rows, cols = grads.shape
    pieces = grads.reshape(n, dp, rows // dp, mp, cols // mp).transpose(1, 3, 0, 2, 4)
    pieces = pieces.reshape((dp * mp,) + pieces.shape[2:])
    return lax.psum_scatter(pieces, ("dp", "mp"), scatter_dimension=0, tiled=True)[0].astype(F32)


class Sum(Steps):
    def __init__(self, values, bit):
        self.values = values
        self.send((values, bit))

    def flip(self, bit):
        self.take()
        self.send((self.values, bit))

    def take(self):
        self.values = self.values + self.state[0]


def other_row(pair_rows, me):
    return lax.dynamic_index_in_dim(pair_rows, 1 - me, 0, False)


def both_halves(own, came, me):
    came = came.astype(F32)
    return jnp.where(me == 0, jnp.stack([own, came]), jnp.stack([came, own]))


def per_device(
    tokens,
    memory,
    doc_lengths,
    mem_lengths,
    norm_gains,
    rel_table,
    self_proj,
    self_out,
    cross_proj,
    cross_out,
    ffn_proj,
    ffn_out,
    cotangent,
):
    me = lax.axis_index("mp")
    dp = lax.axis_size("dp")
    width = tokens.shape[2]
    packed = dp == 1 << BITS and lax.axis_size("mp") == 2
    place = lax.axis_index("dp")
    reverse = sum(((place >> i) & 1) << (BITS - 1 - i) for i in range(BITS))
    ids = jnp.stack([reverse, me, place]).astype(jnp.int32)
    band = bias_band(rel_table)
    pairs = width // LANES
    x_swap = Swap(other_row(tokens, me))
    shard_mid = jnp.concatenate([self_out.T[None], cross_proj, cross_out.T[None]])
    mem_swap = Swap(other_row(memory, me))

    if packed:
        w_one = Gather(self_proj)
        w_ffn = WideGather(ffn_proj, ffn_out.T[None])
        w_one.launch()
        x_swap.launch()
        shard_mid, w_ffn.sent, mem_swap.sent, ids, band, cotangent = hold(
            (shard_mid, w_ffn.sent, mem_swap.sent, ids, band, cotangent), w_one
        )
        w_one.second()
        cot_swap = Swap(other_row(cotangent, me))
        begin((), w_one, w_ffn)
        shard_mid, cot_swap.sent = hold((shard_mid, cot_swap.sent), w_one)
        w_two = Gather(shard_mid)
        w_one.third()
        begin((), w_one, w_two)
        hold((), w_one, x_swap, w_two)
        w_one.fourth()
        w_two.second()
        begin((), w_one, w_two)
        w_one.over_cores()
        hold((), w_one, w_two, w_ffn)
        left, right = w_ffn.split()
        w_self = w_one.pieces()
        w_two.third()
        w_self = begin(w_self, w_two, left, right, mem_swap)
    else:
        cot_swap = Swap(other_row(cotangent, me))
        begin((), x_swap, mem_swap, cot_swap)
        w_self = [gather_whole(self_proj)]
        w_mid = [gather_whole(shard_mid)]
        w_ffn = gather_whole(jnp.concatenate([ffn_proj, ffn_out.T[None]]))
        w_ffn = [w_ffn.reshape(3, width, 2, -1).transpose(2, 0, 1, 3)]
    x = (x_swap.state[0], tokens)
    normed_one, qkv, w_self = project(ids, norm_gains, *x, w_self)
    parts = ((qkv, 0), (qkv, pairs), (qkv, 2 * pairs))
    self_args = (True, ids, doc_lengths, band)
    if packed:
        mixed = attention_forward(*self_args, *parts, width, 0, pairs // 2)
        mixed = hold(mixed, w_two, left, right)
        w_two.fourth()
        left.flip(2)
        mixed = begin(mixed, w_two, left)
        w_two.over_cores()
        mixed_self, qa_self = attention_forward(*self_args, *parts, width, pairs // 2, pairs, mixed)
        mixed_self = hold(mixed_self, mem_swap, w_two, left)
        w_mid = w_two.pieces()
        left.flip(1)
        right.flip(3)
        mixed_self, w_mid = begin((mixed_self, w_mid), left, right, cot_swap)
    else:
        mixed_self, qa_self = attention_forward(*self_args, *parts, width)
    mem = (mem_swap.state[0], memory)
    resid_two, normed_two, q_cross, k_cross, v_cross, w_mid = middle(ids, norm_gains, *x, mixed_self, *mem, w_mid)
    cross_args = (False, ids, mem_lengths, band)
    if packed:
        q_cross = hold(q_cross, right)
        right.flip(2)
        q_cross = begin(q_cross, right)
    parts = ((q_cross, 0), (k_cross, 0), (v_cross, 0))
    if packed:
        mixed = attention_forward(*cross_args, *parts, width, 0, pairs - 1)
        mixed = hold(mixed, left, right, cot_swap)
        w_ffn = left.pieces() + right.pieces()
        mixed_cross, qa_cross = attention_forward(*cross_args, *parts, width, pairs - 1, pairs, mixed)
    else:
        mixed_cross, qa_cross = attention_forward(*cross_args, *parts, width)
    output, output_sent, grad_three, grad_mixed, gain_three, *ffn_grads = feed(
        packed, ids, doc_lengths, norm_gains, resid_two, mixed_cross, cot_swap.state[0], cotangent, w_mid, w_ffn
    )
    out_swap = Swap(output_sent)
    cross_args = cross_args[1:]
    parts = (qa_cross, (k_cross, 0), (v_cross, 0))
    if packed:
        ffn = Scatter(*ffn_grads)
        grad_mixed = begin(grad_mixed, out_swap, ffn)
        grads = cross_backward(*cross_args, *parts, grad_mixed, mixed_cross, 0, 2)
        grads = hold(grads, ffn)
        ffn.second()
        grads, grad_mixed = begin((grads, grad_mixed), ffn)
        grads_cross = cross_backward(*cross_args, *parts, grad_mixed, mixed_cross, 2, pairs, (grads,))
        grads_cross = hold(grads_cross, ffn)
        ffn.third()
        grads_cross = begin(grads_cross, ffn)
    else:
        begin((), out_swap)
        grads_cross = cross_backward(*cross_args, *parts, grad_mixed, mixed_cross, 0, pairs)
    grads_cross = hold(grads_cross, out_swap)
    grad_two, grad_mixed, gmem, gmem_sent, gain_two, *mid_grads = cross_back(
        packed, ids, norm_gains, grads_cross, resid_two, normed_two, *mem, grad_three, mixed_cross, mixed_self, w_mid
    )
    gmem_swap = Swap(gmem_sent)
    parts = (qa_self, (qkv, pairs), (qkv, 2 * pairs))
    more = (mixed_self, normed_one)
    if packed:
        mid = Scatter(*mid_grads)
        hold((), ffn)
        ffn.fourth()
        grad_mixed = begin(grad_mixed, mid, gmem_swap, ffn)
        results = self_backward(1, packed, *self_args[1:], *parts, grad_mixed, *more, 0, 1)
        results = hold(results, mid)
        mid.second()
        results, grad_mixed = begin((results, grad_mixed), mid)
        d_theirs, table_theirs, *grads_theirs = self_backward(
            1, packed, *self_args[1:], *parts, grad_mixed, *more, 1, None, results
        )
        d_theirs, grads_theirs, grad_mixed = hold((d_theirs, grads_theirs, grad_mixed), mid, ffn)
        theirs = SideScatter(*grads_theirs)
        theirs.launch()
        mid.third()
        ffn.fifth()
        mid.sent, ffn.sent = hold((mid.sent, ffn.sent), theirs)
        theirs.flip(1)
        grad_mixed = begin(grad_mixed, mid, theirs, ffn)
        d_ours, table_ours, *grads_ours = self_backward(0, packed, *self_args[1:], *parts, grad_mixed, *more)
        d_ours, grads_ours = hold((d_ours, grads_ours), mid, theirs, gmem_swap, ffn)
        ours = SideScatter(*grads_ours)
        ours.launch()
        theirs.flip(2)
        mid.fourth()
        theirs.sent, mid.sent = hold((theirs.sent, mid.sent), ours)
        ours.flip(1)
        d_ours = begin(d_ours, ours, theirs, mid)
    else:
        begin((), gmem_swap)
        d_theirs, table_theirs, *grads_theirs = self_backward(1, packed, *self_args[1:], *parts, grad_mixed, *more)
        d_ours, table_ours, *grads_ours = self_backward(0, packed, *self_args[1:], *parts, grad_mixed, *more)
    grad_x, grad_x_sent, gain_one = self_back(ids, norm_gains, d_ours, d_theirs, *x, grad_two, w_self)
    grad_x_swap = Swap(grad_x_sent)
    half_of = (jnp.arange(pairs, dtype=jnp.int32) >= pairs // 2).astype(jnp.int32)[:, None, None]
    if packed:
        grad_x_swap.sent, gain_one, table_ours, table_theirs = hold(
            (grad_x_swap.sent, gain_one, table_ours, table_theirs), mid, ours, theirs
        )
        ours.flip(2)
        theirs.flip(3)
        mid.fifth()
        gain_one, table_ours, table_theirs = begin(
            (gain_one, table_ours, table_theirs), grad_x_swap, ours, theirs, mid
        )
    table = jnp.where(half_of == me, table_ours, table_theirs).reshape(-1, width)
    small = jnp.concatenate([gain_one, gain_two, gain_three, table])
    if packed:
        small = Sum(small, 0)
        small.launch()
        small.flip(None)
        small.launch()
        small.flip(1)
        small.launch()
        hold((), mid, ours, theirs, small)
        small.flip(2)
        small.launch()
        ours.flip(3)
        theirs.across()
        begin((), ours, theirs)
        small.flip(3)
        small.launch()
        ffn_grads = ffn.total()
        mid_grads = mid.total()
        ours.take()
        self_grads = ours.kept + theirs.state[0].astype(F32)
        small.take()
        small = small.values
    else:
        begin((), grad_x_swap)
        ffn_grads = scatter_whole(ffn_grads[0].transpose(1, 2, 0, 3).reshape(3, width, -1))
        mid_grads = scatter_whole(mid_grads[0])
        self_grads = scatter_whole(
            jnp.where(
                me == 0,
                jnp.concatenate([grads_ours[0], grads_theirs[0]], axis=2),
                jnp.concatenate([grads_theirs[0], grads_ours[0]], axis=2),
            )
        )
        small = lax.psum(small, ("dp", "mp"))
    table = small[3:].reshape(pairs, -1, LANES)[:, :2, :NB].reshape(2 * pairs, NB).T
    output = both_halves(output, out_swap.state[0], me)
    grad_memory = both_halves(gmem, gmem_swap.state[0], me)
    grad_tokens = both_halves(grad_x, grad_x_swap.state[0], me)
    return (
        output,
        grad_tokens,
        grad_memory,
        small[:3],
        table,
        self_grads,
        mid_grads[0].T,
        mid_grads[1:4],
        mid_grads[4].T,
        ffn_grads[:2],
        ffn_grads[2].T,
    )


def solution(mesh):
    rows = P("dp", "mp", None)
    proj = P(None, "dp", "mp")
    out = P("mp", "dp")
    return jax.shard_map(
        per_device,
        mesh=mesh,
        in_specs=(rows, rows, P("dp", None), P("dp"), P(), P(), proj, out, proj, out, proj, out, rows),
        out_specs=(rows, rows, rows, P(), P(), proj, out, proj, out, proj, out),
        check_vma=False,
    )
```

```python
import functools
import jax
import jax.numpy as jnp
import numpy as np
from jax import lax
from jax.experimental import pallas as pl
from jax.experimental.pallas import tpu as pltpu
from jax.sharding import PartitionSpec as P

DH = 64
NB = 32
REACH = 128
ROW = 1024
LANES = 128
QB = 256
masked_score = -1000000000.0
BF = jnp.bfloat16
F32 = jnp.float32
SELF_FORWARD_MB = 20
CROSS_FORWARD_MB = 56
BACKWARD_MB = 56
PROJECT_MB = 20
MIDDLE_MB = 56
FEED_MB = 60
CROSS_BACK_MB = 56
WEIGHTS_MB = 56
SELF_BACK_MB = 56


def params(megabytes):
    return pltpu.CompilerParams(vmem_limit_bytes=megabytes * 1024 * 1024, dimension_semantics=("arbitrary",))


def dot_t(a, b):
    return lax.dot_general(a, b, (((1,), (1,)), ((), ())), preferred_element_type=F32)


def dot_n(a, b):
    return lax.dot_general(a, b, (((1,), (0,)), ((), ())), preferred_element_type=F32)


def dot_tn(a, b):
    return lax.dot_general(a, b, (((0,), (0,)), ((), ())), preferred_element_type=F32)


def split_three(x):
    top = x.astype(BF)
    rest = x - top.astype(F32)
    mid = rest.astype(BF)
    low = (rest - mid.astype(F32)).astype(BF)
    return top.astype(F32), mid.astype(F32), low.astype(F32)


def place_three(x, slot, other):
    top, mid, low = split_three(x)
    return jnp.where(slot == 4, top, jnp.where(slot == 5, mid, jnp.where(slot == 6, low, other)))


def lane_slots(shape):
    lane = lax.broadcasted_iota(jnp.int32, shape, 1)
    return lane, lane % DH


def make_extras(ids_ref, bounds_ref, causal, extra_q, extra_k):
    me = ids_ref[1]
    shape = extra_q.shape
    _, slot = lane_slots(shape)
    rows = lax.broadcasted_iota(jnp.int32, shape, 0)
    if causal:
        first = bounds_ref[me, 0]
        second = first + bounds_ref[me, 1]
        third = second + bounds_ref[me, 2]
        seg = (
            (rows >= first).astype(jnp.int32)
            + (rows >= second).astype(jnp.int32)
            + (rows >= third).astype(jnp.int32)
        )
        own = jnp.where(slot == seg, 1.0, 0.0)
        barred = jnp.where((slot < 4) & (slot != seg), masked_score, 0.0)
    else:
        own = jnp.where(slot == 0, 1.0, 0.0)
        barred = jnp.where((slot == 0) & (rows >= bounds_ref[me]), masked_score, 0.0)
    extra_q[...] = jnp.where(slot == 7, 1.0, own).astype(BF)
    extra_k[...] = jnp.where((slot >= 4) & (slot <= 6), 1.0, barred).astype(BF)


def band_square(band_ref, head):
    wide = jnp.broadcast_to(band_ref[head : head + 1, :], (LANES, 3 * LANES))
    rolled = pltpu.roll(wide, 0, 1, stride=1, stride_axis=0)
    return rolled[:, LANES : 2 * LANES], rolled[:, :LANES]


def add_band(scores, first, near, side):
    above = jnp.full((LANES, LANES), masked_score, F32)
    corner = jnp.concatenate([side, jnp.zeros((LANES, LANES), F32)], axis=0)
    left = jnp.concatenate([near, side], axis=0)
    right = jnp.concatenate([above, near], axis=0)
    pieces = []
    if first > 0:
        pieces.append(scores[:, : first - LANES])
        pieces.append(scores[:, first - LANES : first] + corner)
    pieces.append(scores[:, first : first + LANES] + left)
    pieces.append(scores[:, first + LANES :] + right)
    return jnp.concatenate(pieces, axis=1)


def forward_kernel(causal, extra, ids_ref, bounds_ref, band_ref, q_ref, k_ref, v_ref, *rest):
    o_ref, qa_ref, extra_q, extra_k = rest[extra:]
    length = q_ref.shape[0]

    @pl.when(pl.program_id(0) == 0)
    def _():
        make_extras(ids_ref, bounds_ref, causal, extra_q, extra_k)

    lane, slot = lane_slots((QB, LANES))
    full_lane, full_slot = lane_slots((length, LANES))
    ones = jnp.where(full_slot == 0, 1.0, 0.0).astype(BF)
    keys, values, bands = [], [], []
    for head in range(2):
        mine = (full_lane < DH) == (head == 0)
        keys.append(jnp.where(mine, k_ref[...], extra_k[...]))
        values.append(jnp.where(mine, v_ref[...], ones))
        if causal:
            bands.append(band_square(band_ref, head))

    def scores_of(block, head):
        first = block * QB
        count = first + QB if causal else length
        mine_block = (lane < DH) == (head == 0)
        queries = jnp.where(mine_block, q_ref[first : first + QB, :], extra_q[first : first + QB, :])
        return queries, dot_t(queries, keys[head][:count])

    todo = [(block, head) for block in range(length // QB) for head in range(2)]
    ahead = [scores_of(*item) for item in todo[:2]]
    for at, (block, head) in enumerate(todo):
        first = block * QB
        span = slice(first, first + QB)
        queries, scores = ahead.pop(0)
        if at + 2 < len(todo):
            ahead.append(scores_of(*todo[at + 2]))
        if causal:
            scores = add_band(scores, first, *bands[head])
        top = jnp.max(scores, axis=1, keepdims=True)
        weights = jnp.exp(scores - top).astype(BF)
        mixed = dot_n(weights, values[head][: weights.shape[1]])
        spare_column = DH if head == 0 else 0
        total = mixed[:, spare_column : spare_column + 1]
        mixed = mixed * (1.0 / total)
        if head == 0:
            kept = mixed
        else:
            o_ref[span, :] = jnp.where(lane < DH, kept, mixed).astype(BF)
        spare = place_three(-(top + jnp.log(total)), slot, queries.astype(F32))
        qa_ref[head, span, :] = jnp.where((lane < DH) == (head == 0), queries, spare.astype(BF))


def backward_kernel(causal, packed, extra, ids_ref, bounds_ref, band_ref, qa_ref, k_ref, v_ref, g_ref, o_ref, *rest):
    if causal:
        rest = rest[:2] + rest[2 + extra :]
        near_ref, normed_ref, grad_ref, bias_ref = rest[:4]
        wgrads = rest[4:-7]
        extra_q, extra_k, dk_acc, dv_acc, near_acc, side_acc, left = rest[-7:]
    else:
        grad_ref, extra_q, extra_k, dk_acc, dv_acc = rest[-5:]
    length = k_ref.shape[0]

    @pl.when(pl.program_id(0) == 0)
    def _():
        make_extras(ids_ref, bounds_ref, causal, extra_q, extra_k)
        if causal:
            put_turned(packed, ids_ref, left, slice(None), normed_ref[...])

    if causal:
        bias_ref[...] = jnp.zeros_like(bias_ref)

    lane, slot = lane_slots((QB, LANES))
    full_lane, full_slot = lane_slots((length, LANES))
    spare_v = jnp.where((full_slot >= 4) & (full_slot <= 6), 1.0, 0.0).astype(BF)
    for head in range(2):
        mine = (full_lane < DH) == (head == 0)
        mine_block = (lane < DH) == (head == 0)
        keys = jnp.where(mine, k_ref[...], extra_k[...])
        values = jnp.where(mine, v_ref[...], spare_v)
        if causal:
            near, side = band_square(band_ref, head)
            near, side = near.T, side.T
            near_only = jnp.full((LANES, LANES), masked_score, F32)
            near_acc[...] = jnp.zeros_like(near_acc)
            side_acc[...] = jnp.zeros_like(side_acc)
        dk_acc[...] = jnp.zeros_like(dk_acc)
        dv_acc[...] = jnp.zeros_like(dv_acc)
        for block in range(length // QB):
            first = block * QB
            count = first + QB if causal else length
            span = slice(first, first + QB)
            queries = qa_ref[head, span, :]
            upstream = g_ref[span, :]
            inner = jnp.sum(
                jnp.where(mine_block, upstream.astype(F32) * o_ref[span, :].astype(F32), 0.0), axis=1, keepdims=True
            )
            spare = place_three(-inner, slot, jnp.zeros((QB, LANES), F32))
            grads = jnp.where(mine_block, upstream, spare.astype(BF))
            scores = dot_t(keys[:count], queries)
            if causal:
                corner = jnp.concatenate([side, jnp.zeros((LANES, LANES), F32)], axis=1)
                upper = jnp.concatenate([near, side], axis=1)
                lower = jnp.concatenate([near_only, near], axis=1)
                pieces = []
                if block > 0:
                    if first > LANES:
                        pieces.append(scores[: first - LANES])
                    pieces.append(scores[first - LANES : first] + corner)
                pieces.append(scores[first : first + LANES] + upper)
                pieces.append(scores[first + LANES :] + lower)
                scores = jnp.concatenate(pieces, axis=0)
            probs = jnp.exp(scores)
            lifted = dot_t(values[:count], grads)
            score_grads = (probs * lifted).astype(BF)
            dv_acc[:count, :] += dot_n(probs.astype(BF), grads)
            dk_acc[:count, :] += dot_n(score_grads, queries)
            dq = dot_tn(score_grads, keys[:count])
            if causal:
                near_acc[...] += score_grads[first : first + LANES, :LANES].astype(F32)
                near_acc[...] += score_grads[first + LANES :, LANES:].astype(F32)
                side_acc[...] += score_grads[first : first + LANES, LANES:].astype(F32)
                if block > 0:
                    side_acc[...] += score_grads[first - LANES : first, :LANES].astype(F32)
            if head == 0:
                grad_ref[0, span, :] = dq.astype(BF)
            else:
                grad_ref[0, span, :] = jnp.where(lane < DH, grad_ref[0, span, :], dq.astype(BF))
        if head == 0:
            grad_ref[1] = dk_acc[...].astype(BF)
            grad_ref[2] = dv_acc[...].astype(BF)
        else:
            grad_ref[1] = jnp.where(full_lane < DH, grad_ref[1], dk_acc[...].astype(BF))
            grad_ref[2] = jnp.where(full_lane < DH, grad_ref[2], dv_acc[...].astype(BF))
        if causal:
            square = jnp.concatenate([side_acc[...], near_acc[...]], axis=0)
            wide = jnp.concatenate([square, jnp.zeros((2 * LANES, 2 * LANES), F32)], axis=1)
            half = LANES
            while half:
                wide = wide[:half] + pltpu.roll(wide[half:], 3 * LANES - half, 1)
                half //= 2
            diag = wide[:, 2 * LANES :]
            ones_column = jnp.where((full_lane % DH == 7) & ~mine, dk_acc[...], 0.0)
            whole = jnp.sum(ones_column, axis=0, keepdims=True)
            table = lax.dot_general(
                diag, near_ref[...], (((1,), (0,)), ((), ())),
                precision=lax.Precision.HIGHEST, preferred_element_type=F32,
            )
            last = jnp.sum(whole, axis=1, keepdims=True) - jnp.sum(table, axis=1, keepdims=True)
            at_last = lax.broadcasted_iota(jnp.int32, table.shape, 1) == NB - 1
            bias_ref[0, head : head + 1, :] = jnp.where(at_last, last, table)
    if causal:
        right = jnp.concatenate([grad_ref[n] for n in range(3)], axis=1)
        grads = dot_n(left[...], right).astype(BF)
        middle_row = grads.shape[0] // 2
        for n in range(3):
            part = grads[:, n * LANES : (n + 1) * LANES]
            if packed:
                shape = wgrads[0].shape[:3] + wgrads[0].shape[4:]
                wgrads[0][:, :, :, n] = part[:middle_row].reshape(shape)
                wgrads[1][:, :, :, n] = part[middle_row:].reshape(shape)
            else:
                wgrads[0][n] = part


def attention_forward(causal, ids, bounds, band, q, k, v, cols, start=0, stop=None, into=()):
    rows = q[0].shape[0]
    pairs = (cols // LANES if stop is None else stop) - start

    def spec(offset):
        return pl.BlockSpec((rows, LANES), lambda p, ids: (0, p + offset + start))

    n = rows * rows * pairs * 2
    return call(
        functools.partial(forward_kernel, causal, len(into)), "attention_forward", SELF_FORWARD_MB if causal else CROSS_FORWARD_MB, pairs,
        [
            pl.BlockSpec(memory_space=pltpu.SMEM),
            pl.BlockSpec((None, 2, 3 * LANES), lambda p, ids: (p + start, 0, 0)),
            spec(q[1]), spec(k[1]), spec(v[1]),
        ] + [anywhere()] * len(into),
        [
            (spec(0), (rows, cols), BF),
            (pl.BlockSpec((2, rows, LANES), lambda p, ids: (p + start, 0, 0)), (2 * cols // LANES, rows, LANES), BF),
        ],
        [pltpu.VMEM((rows, LANES), BF)] * 2,
        n * 256 * 4 // (2 if causal else 1), rows * cols * 16,
        {6: 0, 7: 1} if into else {},
    )(ids, bounds, band, q[0], k[0], v[0], *into)


def cross_backward(ids, bounds, band, qa, k, v, g, o, start, stop, into=()):
    rows, cols = g.shape

    def spec(offset):
        return pl.BlockSpec((rows, LANES), lambda p, ids: (0, p + start + offset))

    n = rows * rows * (stop - start) * 2
    return call(
        functools.partial(backward_kernel, False, False, 0), "cross_backward", BACKWARD_MB, stop - start,
        [
            pl.BlockSpec(memory_space=pltpu.SMEM),
            pl.BlockSpec((None, 2, 3 * LANES), lambda p, ids: (p + start, 0, 0)),
            pl.BlockSpec((2, rows, LANES), lambda p, ids: (p + start, 0, 0)),
            spec(k[1]), spec(v[1]), spec(0), spec(0),
        ] + [anywhere()] * len(into),
        [(pl.BlockSpec((3, rows, LANES), lambda p, ids: (0, 0, p + start)), (3, rows, cols), BF)],
        [pltpu.VMEM((rows, LANES), BF)] * 2 + [pltpu.VMEM((rows, LANES), F32)] * 2,
        n * 256 * 10, rows * cols * 20,
        {8: 0} if into else {},
    )(ids, bounds, band, qa, k[0], v[0], g, o, *into)[0]


def self_backward(side, packed, ids, bounds, band, qa, k, v, g, o, normed, start=0, stop=None, into=()):
    rows, cols = g.shape
    pairs = cols // LANES // 2
    stop = pairs if stop is None else stop
    depth = normed.shape[1] >> BITS

    def at(p, ids):
        return p + start + pairs * jnp.bitwise_xor(ids[1], side)

    def spec(offset):
        return pl.BlockSpec((rows, LANES), lambda p, ids: (0, at(p, ids) + offset))

    n = rows * rows * (stop - start) * 2
    if packed:
        block = pl.BlockSpec((2, 2, 2, 3, depth, LANES), lambda p, ids: (0, 0, 0, 0, 0, p + start))
        wgrads = [(block, (2, 2, 2, 3, depth, cols // 2), BF)] * 2
    else:
        block = pl.BlockSpec((3, normed.shape[1], LANES), lambda p, ids: (0, 0, p + start))
        wgrads = [(block, (3, normed.shape[1], cols // 2), BF)]
    return call(
        functools.partial(backward_kernel, True, packed, len(into)), "self_backward", BACKWARD_MB, stop - start,
        [
            pl.BlockSpec(memory_space=pltpu.SMEM),
            pl.BlockSpec((None, 2, 3 * LANES), lambda p, ids: (at(p, ids), 0, 0)),
            pl.BlockSpec((2, rows, LANES), lambda p, ids: (at(p, ids), 0, 0)),
            spec(k[1]), spec(v[1]), spec(0), spec(0),
            held((LANES, LANES)), held(normed.shape),
        ] + [anywhere()] * len(into),
        [
            (pl.BlockSpec((3, rows, LANES), lambda p, ids: (0, 0, p + start)), (3, rows, cols // 2), BF),
            (pl.BlockSpec((1, 8, LANES), lambda p, ids: (at(p, ids), 0, 0)), (2 * pairs, 8, LANES), F32),
        ] + wgrads,
        [pltpu.VMEM((rows, LANES), BF)] * 2 + [pltpu.VMEM((rows, LANES), F32)] * 2
        + [pltpu.VMEM((LANES, LANES), F32)] * 2 + [pltpu.VMEM((normed.shape[1], rows), BF)],
        n * 256 * 8, rows * cols * 20,
        {10 + i: i for i in range(len(into))},
    )(ids, bounds, band, qa, k[0], v[0], g, o, jnp.asarray(near_buckets()), normed, *into)


def near_buckets():
    buckets = bucket_table(LANES, NB, REACH)
    columns = np.arange(LANES)[None, :]
    return ((buckets[:, None] == columns) & (columns < NB - 1)).astype(np.float32)


def bucket_table(length, buckets, reach):
    offsets = np.arange(length)
    exact_part = buckets // 2
    scaled = np.log(np.maximum(offsets, 1) / exact_part) / np.log(reach / exact_part) * (buckets - exact_part)
    far_bucket = np.minimum(exact_part + np.floor(scaled).astype(np.int64), buckets - 1)
    return np.where(offsets < exact_part, offsets, far_bucket).astype(np.int32)


def bias_band(rel_table):
    distance = LANES - np.arange(3 * LANES)
    buckets = bucket_table(LANES + 1, NB, REACH)
    onehot = np.zeros((3 * LANES, NB), np.float32)
    shift = np.zeros((3 * LANES,), np.float32)
    for at, far in enumerate(distance):
        if 0 <= far < LANES:
            onehot[at, buckets[far]] = 1.0
        elif -LANES < far < 0:
            shift[at] = masked_score
    relative = rel_table - rel_table[NB - 1 :]
    band = jnp.dot(jnp.asarray(onehot), relative, precision=lax.Precision.HIGHEST) + shift[:, None]
    return band.T.reshape(-1, 2, 3 * LANES)


epsilon = 1e-06
TB = 256
BITS = 4


def rms(values, gain):
    inverse = lax.rsqrt(jnp.mean(values * values, axis=-1, keepdims=True) + epsilon)
    return (values * inverse * gain).astype(BF), inverse


def rms_back(values, inverse, gain, upstream):
    weighted = upstream * gain
    inner_mean = jnp.mean(weighted * values, axis=-1, keepdims=True)
    grad_values = inverse * weighted - values * (inverse * inverse * inverse * inner_mean)
    return grad_values, jnp.sum(upstream * values * inverse, axis=0, keepdims=True)


def cost(flops, moved):
    return pl.CostEstimate(flops=flops, bytes_accessed=moved, transcendentals=0)


def turn(s, ids, blocks):
    return ((1 - ids[1]) * (blocks // 2) + jnp.minimum(s, blocks - 1)) % blocks


def row_spec(blocks, width, *lead):
    zeros = (0,) * len(lead)
    return pl.BlockSpec(lead + (TB, width), lambda s, ids: zeros + (turn(s, ids, blocks), 0))


def kept_spec(blocks, width):
    half = blocks // 2
    return pl.BlockSpec((None, TB, width), lambda s, ids: (ids[1], jnp.clip(s - half, 0, half - 1), 0))


def own_spec(blocks, width):
    half = blocks // 2
    return pl.BlockSpec((TB, width), lambda s, ids: (jnp.clip(s - half, 0, half - 1), 0))


def other_spec(blocks, width):
    return pl.BlockSpec((TB, width), lambda s, ids: (jnp.minimum(s, blocks // 2 - 1), 0))


def held(shape):
    zeros = (0,) * len(shape)
    return pl.BlockSpec(shape, lambda s, ids: zeros, pipeline_mode=pl.Buffered(1))


def anywhere():
    return pl.BlockSpec(memory_space=pl.ANY)


def call(kernel, name, megabytes, grid, in_specs, outs, scratch, flops, moved, aliases=None):
    return pl.pallas_call(
        kernel,
        grid_spec=pltpu.PrefetchScalarGridSpec(
            num_scalar_prefetch=1,
            grid=(grid,),
            in_specs=in_specs,
            out_specs=[o[0] for o in outs],
            scratch_shapes=scratch,
        ),
        out_shape=[jax.ShapeDtypeStruct(o[1], o[2]) for o in outs],
        input_output_aliases=aliases or {},
        compiler_params=params(megabytes),
        cost_estimate=cost(flops, moved),
        name=name,
    )


def chosen(step, blocks, came_ref, kept_ref):
    return jnp.where(step < blocks // 2, came_ref[...], kept_ref[...])


def share(step, blocks, values, own_ref, other_ref):
    @pl.when(step < blocks // 2)
    def _():
        other_ref[...] = values.astype(BF)

    @pl.when(step >= blocks // 2)
    def _():
        own_ref[...] = values


def gather_table():
    near = [((0, 0, 0),), ((0, 1, 0),), ((1, 0, 0), (1, 1, 0)), ((0, 0, 1),), ((1, 0, 1),), ((0, 1, 1), (1, 1, 1))]
    table = []
    for c in range(2):
        for places in near:
            entries = []
            for at, (y, x, z0) in enumerate(places):
                for z1 in range(2):
                    entries.append(((at, z1) if len(places) > 1 else (z1,), (y, x, z0, z1, c), 0))
            table.append(entries)
    return table


def wide_table():
    pairs = [(a, b) for a in range(2) for b in range(2)]
    table = []
    for c in range(2):
        for y in range(2):
            table.append([((z0, z1, x), (y, x, z0, z1, c), 0) for x in range(2) for z0, z1 in pairs])
    for c in range(2):
        for z0 in range(2):
            table.append([((z1, y, x), (y, x, z0, z1, c), 1) for x in range(2) for z1, y in pairs])
    return table


def copy_pieces(ids_ref, pieces, table, place, w_ref, sem):
    if len(pieces) == 1:
        for x in range(sem.shape[0]):
            part = pieces[0].at[x] if sem.shape[0] > 1 else pieces[0]
            target = w_ref.at[x] if sem.shape[0] > 1 else w_ref
            pltpu.make_async_copy(part, target, sem.at[x]).start()
        return
    mine = ids_ref[2]
    rows = pieces[0].shape[-2]

    def copy(flip):
        for first in range(2):
            for piece, entries in zip(pieces, table):
                for at, (y, x, z0, z1, c), part in entries:
                    if x ^ flip != first:
                        continue
                    block = jnp.bitwise_xor(mine, 8 * z1 + 4 * z0 + 2 * y + c)
                    span = pl.ds(pl.multiple_of(block * rows, 16), rows)
                    target, done = place(span, x ^ flip, part)
                    pltpu.make_async_copy(piece.at[at], target, done).start()

    @pl.when(ids_ref[1] == 0)
    def _():
        copy(0)

    @pl.when(ids_ref[1] == 1)
    def _():
        copy(1)


def wait_pieces(w_ref, sem):
    pltpu.make_async_copy(w_ref, w_ref, sem).wait()


def natural_place(w_ref, cols, sem):
    return lambda span, x, part: (w_ref.at[:, span, x * cols : (x + 1) * cols], sem.at[0])


def put_turned(packed, ids_ref, target, span, values):
    turned = values.T
    if not packed:
        target[:, span] = turned
        return
    depth = turned.shape[0] >> BITS
    for block in range(1 << BITS):
        reverse = int(format(block, "04b")[::-1], 2)
        at = jnp.bitwise_xor(ids_ref[0], reverse) * depth
        target[pl.ds(pl.multiple_of(at, 16), depth), span] = turned[block * depth : (block + 1) * depth]


def put_grads(packed, ids_ref, n, grads, outs):
    if not packed:
        outs[0][n] = grads
        return
    keep_ref, send_ref = outs
    rows, cols = keep_ref.shape[-2:]
    middle = grads.shape[0] // 2

    def store(flip):
        for x in range(2):
            first = cols * (x ^ flip)
            for target, part in ((keep_ref, grads[:middle]), (send_ref, grads[middle:])):
                block = part[:, first : first + cols].reshape(2, 2, 2, rows, cols)
                target[:, x, :, :, n] = block

    @pl.when(ids_ref[1] == 0)
    def _():
        store(0)

    @pl.when(ids_ref[1] == 1)
    def _():
        store(1)


def grads_out(packed, n, width):
    if not packed:
        shape = (n, width, width)
        return [(held(shape), shape, BF)]
    shape = (2, 2, 2, 2, n, width >> BITS, width // 2)
    return [(held(shape), shape, BF)] * 2


def project_kernel(blocks, pieces, ids_ref, gain_ref, came_ref, kept_ref, *refs):
    w_in = refs[:pieces]
    normed_ref, out_ref, w_ref, sem = refs[pieces:]
    step = pl.program_id(0)

    @pl.when(step == 0)
    def _():
        copy_pieces(ids_ref, w_in, gather_table(), natural_place(w_ref, w_in[0].shape[-1], sem), w_ref, sem)
        wait_pieces(w_ref, sem.at[0])

    normed, _ = rms(chosen(step, blocks, came_ref, kept_ref).astype(F32), gain_ref[0:1, :])
    normed_ref[...] = normed
    width = normed.shape[1]
    for s in range(3):
        out_ref[:, s * width : (s + 1) * width] = dot_n(normed, w_ref[s]).astype(BF)


def project(ids, gain, came, kept, pieces):
    _, half, width = kept.shape
    rows = 2 * half
    blocks = rows // TB
    full = (3, width, width)
    return call(
        functools.partial(project_kernel, blocks, len(pieces)), "project", PROJECT_MB, blocks,
        [held((3, width)), other_spec(blocks, width), kept_spec(blocks, width)] + [anywhere()] * len(pieces),
        [
            (row_spec(blocks, width), (rows, width), BF),
            (row_spec(blocks, 3 * width), (rows, 3 * width), BF),
            (held(full), full, BF),
        ],
        [pltpu.SemaphoreType.DMA((1,))],
        6 * rows * width * width, 10 * rows * width + 6 * width * width,
    )(ids, gain, came, kept, *pieces)


def middle_kernel(blocks, pieces, ids_ref, gain_ref, came_ref, kept_ref, mixed_ref, mem_came_ref, mem_kept_ref, *refs):
    w_in = refs[:pieces]
    resid_ref, normed_ref, q_ref, k_ref, v_ref, w_ref, sem = refs[pieces:]
    step = pl.program_id(0)

    @pl.when(step == 0)
    def _():
        copy_pieces(ids_ref, w_in, gather_table(), natural_place(w_ref, w_in[0].shape[-1], sem), w_ref, sem)
        wait_pieces(w_ref, sem.at[0])

    resid = chosen(step, blocks, came_ref, kept_ref).astype(F32) + dot_t(mixed_ref[...], w_ref[0])
    resid_ref[...] = resid
    normed, _ = rms(resid, gain_ref[1:2, :])
    normed_ref[...] = normed
    q_ref[...] = dot_n(normed, w_ref[1]).astype(BF)
    memory = chosen(step, blocks, mem_came_ref, mem_kept_ref)
    k_ref[...] = dot_n(memory, w_ref[2]).astype(BF)
    v_ref[...] = dot_n(memory, w_ref[3]).astype(BF)


def middle(ids, gain, came, kept, mixed, mem_came, mem_kept, pieces):
    rows, width = mixed.shape
    blocks = rows // TB
    full = (5, width, width)
    spec = row_spec(blocks, width)
    pair = [other_spec(blocks, width), kept_spec(blocks, width)]
    return call(
        functools.partial(middle_kernel, blocks, len(pieces)), "middle", MIDDLE_MB, blocks,
        [held((3, width))] + pair + [spec] + pair + [anywhere()] * len(pieces),
        [(spec, (rows, width), F32)] + [(spec, (rows, width), BF)] * 4 + [(held(full), full, BF)],
        [pltpu.SemaphoreType.DMA((1,))],
        8 * rows * width * width, 20 * rows * width + 10 * width * width,
    )(ids, gain, came, kept, mixed, mem_came, mem_kept, *pieces)


def feed_kernel(blocks, pieces, packed, ids_ref, docs_ref, gain_ref, resid_ref, mixed_ref, cot_came_ref, cot_kept_ref,
                wo_ref, *refs):
    w_in = refs[:pieces]
    refs = refs[pieces:]
    own_ref, other_ref, grad_ref, gmix_ref, gain_grad_ref = refs[:5]
    wgrads = refs[5:-7]
    w_ref, normed_t, branch_t, hidden_s, gate_s, up_s, sem = refs[-7:]
    step = pl.program_id(0)
    me = ids_ref[1]
    width = resid_ref.shape[1]

    def weight(which, x):
        return w_ref[x, which]

    @pl.when(step == 0)
    def _():
        cols = w_in[0].shape[-1]
        copy_pieces(
            ids_ref, w_in, wide_table(),
            lambda span, x, part: (w_ref.at[x, :, span, cols * part : cols if part == 0 else None], sem.at[x]), w_ref, sem,
        )
        gain_grad_ref[...] = jnp.zeros_like(gain_grad_ref)

    @pl.when(step < blocks)
    def _():
        first = pl.multiple_of(turn(step, ids_ref, blocks) * TB, TB)
        span = pl.ds(first, TB)
        resid = resid_ref[...] + dot_t(mixed_ref[...], wo_ref[...])
        normed, inverse = rms(resid, gain_ref[2:3, :])
        slots = first + lax.broadcasted_iota(jnp.int32, (TB, 1), 0)
        padding = slots >= docs_ref[me, 0] + docs_ref[me, 1] + docs_ref[me, 2]
        grad_four = jnp.where(padding, 0.0, chosen(step, blocks, cot_came_ref, cot_kept_ref).astype(F32))
        branch = grad_four.astype(BF)
        put_turned(packed, ids_ref, normed_t, span, normed)
        put_turned(packed, ids_ref, branch_t, span, branch)
        total = resid
        upstream = jnp.zeros((TB, width), F32)
        for x in range(2):

            @pl.when(step == 0)
            def _():
                wait_pieces(w_ref.at[x], sem.at[x])

            gate = dot_n(normed, weight(0, x))
            up = dot_n(normed, weight(1, x))
            lifted = dot_n(branch, weight(2, x))
            square = gate * gate
            inner = jnp.tanh(gate * (0.7978845608028654 + 0.035677408136300125 * square))
            half_up = 0.5 + 0.5 * inner
            activated = gate * half_up
            slope = half_up + (0.5 * gate) * (1.0 - inner * inner) * (
                0.7978845608028654 + 0.10703222440890037 * square
            )
            hidden = (activated * up).astype(BF)
            gate_grad = (lifted * up * slope).astype(BF)
            up_grad = (lifted * activated).astype(BF)
            hidden_s[x, span, :] = hidden
            gate_s[x, span, :] = gate_grad
            up_s[x, span, :] = up_grad
            total = total + dot_t(hidden, weight(2, x))
            upstream = upstream + dot_t(gate_grad, weight(0, x)) + dot_t(up_grad, weight(1, x))
        share(step, blocks, jnp.where(padding, 0.0, total), own_ref, other_ref)
        grad_resid, gain_grad = rms_back(resid, inverse, gain_ref[2:3, :], upstream)
        grad = grad_four + grad_resid
        grad_ref[...] = grad
        gain_grad_ref[...] += gain_grad
        gmix_ref[...] = dot_n(grad.astype(BF), wo_ref[...]).astype(BF)

    for which, (left, right) in enumerate(((normed_t, gate_s), (normed_t, up_s), (branch_t, hidden_s))):
        for x in range(2):

            @pl.when(step == blocks + 2 * which + x)
            def _():
                if packed:
                    grads = dot_n(left[...], right[jnp.bitwise_xor(x, me)]).astype(BF)
                    middle_row = grads.shape[0] // 2
                    wgrads[0][...] = grads[:middle_row].reshape(wgrads[0].shape)
                    wgrads[1][...] = grads[middle_row:].reshape(wgrads[1].shape)
                else:
                    wgrads[0][...] = dot_n(left[...], right[x]).astype(BF)


def feed(packed, ids, docs, gain, resid, mixed, cot_came, cot_kept, w_mid, pieces):
    rows, width = resid.shape
    half = pieces[0].shape[-1] if len(pieces) == 1 else pieces[0].shape[-1] + pieces[-1].shape[-1]
    blocks = rows // TB
    spec = row_spec(blocks, width)

    def at(s):
        late = jnp.maximum(s - blocks, 0)
        return late // 2, late % 2

    if packed:
        depth = width >> BITS
        block = pl.BlockSpec((2, None, 2, 2, None, depth, half), lambda s, ids: (0, at(s)[1], 0, 0, at(s)[0], 0, 0))
        wgrads = [(block, (2, 2, 2, 2, 3, depth, half), BF)] * 2
    else:
        block = pl.BlockSpec((None, None, width, half), lambda s, ids: (at(s)[1], at(s)[0], 0, 0))
        wgrads = [(block, (2, 3, width, half), BF)]
    return call(
        functools.partial(feed_kernel, blocks, len(pieces), packed), "feed", FEED_MB, blocks + 6,
        [pl.BlockSpec(memory_space=pltpu.SMEM), held((3, width)), spec, spec, other_spec(blocks, width),
         kept_spec(blocks, width),
         pl.BlockSpec((None, width, width), lambda s, ids: (4, 0, 0), pipeline_mode=pl.Buffered(1))]
        + [anywhere()] * len(pieces),
        [
            (own_spec(blocks, width), (rows // 2, width), F32),
            (other_spec(blocks, width), (rows // 2, width), BF),
            (spec, (rows, width), F32),
            (spec, (rows, width), BF),
            (held((1, width)), (1, width), F32),
        ] + wgrads,
        [pltpu.VMEM((2, 3, width, half), BF)] + [pltpu.VMEM((width, rows), BF)] * 2
        + [pltpu.VMEM((2, rows, half), BF)] * 3 + [pltpu.SemaphoreType.DMA((2,))],
        36 * rows * width * half, 24 * rows * width + 24 * width * half,
    )(ids, docs, gain, resid, mixed, cot_came, cot_kept, w_mid, *pieces)


def cross_back_kernel(blocks, packed, ids_ref, gain_ref, d_ref, resid_ref, normed_ref, mem_came_ref, mem_kept_ref,
                      grad_ref, mixed_cross_ref, mixed_self_ref, w_ref, *outs):
    grad_two_ref, gmix_ref, gmem_own_ref, gmem_other_ref, gain_grad_ref = outs[:5]
    wgrads = outs[5:-2]
    lefts, rights = outs[-2:]
    step = pl.program_id(0)

    @pl.when(step == 0)
    def _():
        gain_grad_ref[...] = jnp.zeros_like(gain_grad_ref)

    @pl.when(step < blocks)
    def _():
        span = pl.ds(pl.multiple_of(turn(step, ids_ref, blocks) * TB, TB), TB)
        resid = resid_ref[...]
        inverse = lax.rsqrt(jnp.mean(resid * resid, axis=-1, keepdims=True) + epsilon)
        grad_resid, gain_grad = rms_back(resid, inverse, gain_ref[1:2, :], dot_t(d_ref[0], w_ref[1]))
        gain_grad_ref[...] += gain_grad
        grad_three = grad_ref[...]
        grad_two = grad_three + grad_resid
        grad_two_ref[...] = grad_two
        branch = grad_two.astype(BF)
        gmix_ref[...] = dot_n(branch, w_ref[0]).astype(BF)
        gmem = dot_t(d_ref[1], w_ref[2]) + dot_t(d_ref[2], w_ref[3])
        share(step, blocks, gmem, gmem_own_ref, gmem_other_ref)
        memory = chosen(step, blocks, mem_came_ref, mem_kept_ref)
        for n, values in enumerate((branch, normed_ref[...], memory, grad_three.astype(BF))):
            put_turned(packed, ids_ref, lefts.at[n], span, values)
        rights[0, span, :] = mixed_self_ref[...]
        rights[1, span, :] = d_ref[0]
        rights[2, span, :] = d_ref[1]
        rights[3, span, :] = d_ref[2]
        rights[4, span, :] = mixed_cross_ref[...]

    for n, left in enumerate((0, 1, 2, 2, 3)):

        @pl.when(step == blocks + n)
        def _():
            put_grads(packed, ids_ref, n, dot_n(lefts[left], rights[n]).astype(BF), wgrads)


def cross_back(packed, ids, gain, d, resid, normed, mem_came, mem_kept, grad, mixed_cross, mixed_self, w):
    rows, width = resid.shape
    blocks = rows // TB
    spec = row_spec(blocks, width)
    return call(
        functools.partial(cross_back_kernel, blocks, packed), "cross_back", CROSS_BACK_MB, blocks + 5,
        [held((3, width)), row_spec(blocks, width, 3), spec, spec, other_spec(blocks, width), kept_spec(blocks, width),
         spec, spec, spec, held(w.shape)],
        [
            (spec, (rows, width), F32),
            (spec, (rows, width), BF),
            (own_spec(blocks, width), (rows // 2, width), F32),
            (other_spec(blocks, width), (rows // 2, width), BF),
            (held((1, width)), (1, width), F32),
        ] + grads_out(packed, 5, width),
        [pltpu.VMEM((4, width, rows), BF), pltpu.VMEM((5, rows, width), BF)],
        18 * rows * width * width, 36 * rows * width + 20 * width * width,
    )(ids, gain, d, resid, normed, mem_came, mem_kept, grad, mixed_cross, mixed_self, w)


def self_back_kernel(blocks, ids_ref, gain_ref, ours_ref, theirs_ref, came_ref, kept_ref, grad_ref, w_ref,
                     own_ref, other_ref, gain_grad_ref):
    step = pl.program_id(0)

    @pl.when(step == 0)
    def _():
        gain_grad_ref[...] = jnp.zeros_like(gain_grad_ref)

    values = chosen(step, blocks, came_ref, kept_ref).astype(F32)
    inverse = lax.rsqrt(jnp.mean(values * values, axis=-1, keepdims=True) + epsilon)
    upstream = jnp.zeros(values.shape, F32)
    for n in range(3):
        ours, theirs = ours_ref[n], theirs_ref[n]
        first = jnp.where(ids_ref[1] == 0, ours, theirs)
        second = jnp.where(ids_ref[1] == 0, theirs, ours)
        upstream = upstream + dot_t(jnp.concatenate([first, second], axis=1), w_ref[n])
    grad_values, gain_grad = rms_back(values, inverse, gain_ref[0:1, :], upstream)
    gain_grad_ref[...] += gain_grad
    share(step, blocks, grad_ref[...] + grad_values, own_ref, other_ref)


def self_back(ids, gain, ours, theirs, came, kept, grad, w):
    rows, width = grad.shape
    blocks = rows // TB
    part = row_spec(blocks, width // 2, 3)
    return call(
        functools.partial(self_back_kernel, blocks), "self_back", SELF_BACK_MB, blocks,
        [held((3, width)), part, part, other_spec(blocks, width), kept_spec(blocks, width),
         row_spec(blocks, width), held(w.shape)],
        [
            (own_spec(blocks, width), (rows // 2, width), F32),
            (other_spec(blocks, width), (rows // 2, width), BF),
            (held((1, width)), (1, width), F32),
        ],
        [],
        6 * rows * width * width, 20 * rows * width + 6 * width * width,
    )(ids, gain, ours, theirs, came, kept, grad, w)


def flip_bit(values, bit):
    size = lax.axis_size("dp")
    return lax.ppermute(values, "dp", [(i, i ^ (1 << bit)) for i in range(size)])


def flip_mp(values):
    return lax.ppermute(values, "mp", [(0, 1), (1, 0)])


class Steps:
    def send(self, *parts):
        self.sent = [part[0] for part in parts]
        self.bits = [part[1] for part in parts]

    def launch(self):
        self.state = [flip_mp(a) if bit is None else flip_bit(a, bit) for a, bit in zip(self.sent, self.bits)]


def begin(value, *steps):
    value, sent = lax.optimization_barrier((value, [s.sent for s in steps]))
    for step, arrays in zip(steps, sent):
        step.sent = arrays
        step.launch()
    return value


def hold(value, *steps):
    value, states = lax.optimization_barrier((value, [s.state for s in steps]))
    for step, state in zip(steps, states):
        step.state = state
    return value


class Swap(Steps):
    def __init__(self, sent):
        self.send((sent, None))


class Gather(Steps):
    def __init__(self, shard):
        self.shard = shard
        self.low_c = None
        self.send((shard, 3))

    def second(self):
        self.low = jnp.stack([self.shard, self.state[0]])
        self.send((self.low, 2))

    def third(self):
        (self.high,) = self.state
        self.send((self.low, None), (self.high, 1))

    def fourth(self):
        self.low_x, self.high_y = self.state
        self.send((jnp.stack([self.low, self.low_x]), 1), (jnp.stack([self.high, self.high_y]), None))

    def over_cores(self):
        self.low_c = flip_bit(self.low, 0)
        self.high_c = flip_bit(self.high, 0)

    def pieces(self):
        low_y, high_x = self.state
        if self.low_c is None:
            self.over_cores()
        return [
            self.low, self.low_x, low_y, self.high, self.high_y, high_x,
            self.low_c, flip_bit(self.low_x, 0), flip_bit(low_y, 0),
            self.high_c, flip_bit(self.high_y, 0), flip_bit(high_x, 0),
        ]


class WideGather(Steps):
    def __init__(self, proj, out):
        self.shard = jnp.concatenate([proj, out])
        self.send((proj, None), (out, None))

    def split(self):
        both = jnp.stack([self.shard, jnp.concatenate(self.state)])
        cut = both.shape[-1] * 5 // 8
        return WidePart(both[..., :cut], 3), WidePart(both[..., cut:], 1)


class WidePart(Steps):
    def __init__(self, near, bit):
        self.near = near
        self.send((near, bit))

    def flip(self, bit):
        self.near = jnp.stack([self.near, self.state[0]])
        self.send((self.near, bit))

    def pieces(self):
        near = [self.near, self.state[0]]
        return near + [flip_bit(piece, 0) for piece in near]


class Scatter(Steps):
    def __init__(self, keep, send):
        self.keep = keep
        self.send((send, 0))

    def own(self, *at):
        return self.keep[at].astype(F32) + self.came[at].astype(F32)

    def second(self):
        (self.came,) = self.state
        every = slice(None)
        self.send((self.own(1, every, 0).astype(BF), 1), (self.own(every, 1, 1).astype(BF), None))

    def third(self):
        low_y, high_x = self.state
        self.kept = (low_y, high_x)
        self.send(
            ((self.own(0, 1, 0) + low_y[1].astype(F32)).astype(BF), None),
            ((self.own(1, 0, 1) + high_x[1].astype(F32)).astype(BF), 1),
        )

    def fourth(self):
        low_y, high_x = self.kept
        low_x, high_y = self.state
        high = self.own(0, 0, 1) + high_x[0].astype(F32) + high_y.astype(F32)
        self.kept = self.own(0, 0, 0) + low_y[0].astype(F32) + low_x.astype(F32)
        self.send((high.astype(BF), 2))

    def fifth(self):
        self.kept = self.kept + self.state[0].astype(F32)
        self.send((self.kept[1].astype(BF), 3))

    def total(self):
        return self.kept[0] + self.state[0].astype(F32)


class SideScatter(Steps):
    def __init__(self, keep, send):
        self.kept = keep
        self.send((send, 0))

    def take(self):
        self.kept = self.kept.astype(F32) + self.state[0].astype(F32)

    def flip(self, bit, more=None):
        self.take()
        if more is not None:
            self.kept = self.kept + more.astype(F32)
        self.send((self.kept[1].astype(BF), bit))
        self.kept = self.kept[0]

    def across(self):
        self.take()
        self.send((self.kept.astype(BF), None))


def gather_whole(shard):
    n, rows, cols = shard.shape
    dp = lax.axis_size("dp")
    mp = lax.axis_size("mp")
    pieces = lax.all_gather(shard, ("dp", "mp"), axis=0).reshape(dp, mp, n, rows, cols)
    return pieces.transpose(2, 0, 3, 1, 4).reshape(n, dp * rows, mp * cols)


def scatter_whole(grads):
    dp = lax.axis_size("dp")
    mp = lax.axis_size("mp")
    n, rows, cols = grads.shape
    pieces = grads.reshape(n, dp, rows // dp, mp, cols // mp).transpose(1, 3, 0, 2, 4)
    pieces = pieces.reshape((dp * mp,) + pieces.shape[2:])
    return lax.psum_scatter(pieces, ("dp", "mp"), scatter_dimension=0, tiled=True)[0].astype(F32)


class Sum(Steps):
    def __init__(self, values, bit):
        self.values = values
        self.send((values, bit))

    def flip(self, bit):
        self.take()
        self.send((self.values, bit))

    def take(self):
        self.values = self.values + self.state[0]


def other_row(pair_rows, me):
    return lax.dynamic_index_in_dim(pair_rows, 1 - me, 0, False)


def both_halves(own, came, me):
    came = came.astype(F32)
    return jnp.where(me == 0, jnp.stack([own, came]), jnp.stack([came, own]))


def per_device(
    tokens,
    memory,
    doc_lengths,
    mem_lengths,
    norm_gains,
    rel_table,
    self_proj,
    self_out,
    cross_proj,
    cross_out,
    ffn_proj,
    ffn_out,
    cotangent,
):
    me = lax.axis_index("mp")
    dp = lax.axis_size("dp")
    width = tokens.shape[2]
    packed = dp == 1 << BITS and lax.axis_size("mp") == 2
    place = lax.axis_index("dp")
    reverse = sum(((place >> i) & 1) << (BITS - 1 - i) for i in range(BITS))
    ids = jnp.stack([reverse, me, place]).astype(jnp.int32)
    band = bias_band(rel_table)
    pairs = width // LANES
    x_swap = Swap(other_row(tokens, me))
    shard_mid = jnp.concatenate([self_out.T[None], cross_proj, cross_out.T[None]])
    mem_swap = Swap(other_row(memory, me))

    if packed:
        w_one = Gather(self_proj)
        w_ffn = WideGather(ffn_proj, ffn_out.T[None])
        w_one.launch()
        x_swap.launch()
        shard_mid, w_ffn.sent, mem_swap.sent, ids, band, cotangent = hold(
            (shard_mid, w_ffn.sent, mem_swap.sent, ids, band, cotangent), w_one
        )
        w_one.second()
        cot_swap = Swap(other_row(cotangent, me))
        begin((), w_one)
        shard_mid, cot_swap.sent = hold((shard_mid, cot_swap.sent), w_one)
        w_two = Gather(shard_mid)
        w_one.third()
        begin((), w_one, w_two)
        hold((), w_one, x_swap)
        w_one.fourth()
        begin((), w_one)
        w_one.over_cores()
        hold((), w_one, w_two)
        w_self = w_one.pieces()
        w_two.second()
        w_self = begin(w_self, w_two, w_ffn)
    else:
        cot_swap = Swap(other_row(cotangent, me))
        begin((), x_swap, mem_swap, cot_swap)
        w_self = [gather_whole(self_proj)]
        w_mid = [gather_whole(shard_mid)]
        w_ffn = gather_whole(jnp.concatenate([ffn_proj, ffn_out.T[None]]))
        w_ffn = [w_ffn.reshape(3, width, 2, -1).transpose(2, 0, 1, 3)]
    x = (x_swap.state[0], tokens)
    normed_one, qkv, w_self = project(ids, norm_gains, *x, w_self)
    if packed:
        qkv = hold(qkv, w_two, w_ffn)
        w_two.third()
        left, right = w_ffn.split()
        qkv = begin(qkv, w_two, left, right, mem_swap)
    parts = ((qkv, 0), (qkv, pairs), (qkv, 2 * pairs))
    self_args = (True, ids, doc_lengths, band)
    if packed:
        mixed = attention_forward(*self_args, *parts, width, 0, pairs // 2)
        mixed = hold(mixed, w_two, left, right)
        w_two.fourth()
        left.flip(2)
        mixed = begin(mixed, w_two, left)
        w_two.over_cores()
        mixed_self, qa_self = attention_forward(*self_args, *parts, width, pairs // 2, pairs, mixed)
        mixed_self = hold(mixed_self, mem_swap, w_two, left)
        w_mid = w_two.pieces()
        left.flip(1)
        right.flip(3)
        mixed_self, w_mid = begin((mixed_self, w_mid), left, right, cot_swap)
    else:
        mixed_self, qa_self = attention_forward(*self_args, *parts, width)
    mem = (mem_swap.state[0], memory)
    resid_two, normed_two, q_cross, k_cross, v_cross, w_mid = middle(ids, norm_gains, *x, mixed_self, *mem, w_mid)
    cross_args = (False, ids, mem_lengths, band)
    if packed:
        q_cross = hold(q_cross, right)
        right.flip(2)
        q_cross = begin(q_cross, right)
    parts = ((q_cross, 0), (k_cross, 0), (v_cross, 0))
    if packed:
        mixed = attention_forward(*cross_args, *parts, width, 0, pairs - 1)
        mixed = hold(mixed, left, right, cot_swap)
        w_ffn = left.pieces() + right.pieces()
        mixed_cross, qa_cross = attention_forward(*cross_args, *parts, width, pairs - 1, pairs, mixed)
    else:
        mixed_cross, qa_cross = attention_forward(*cross_args, *parts, width)
    output, output_sent, grad_three, grad_mixed, gain_three, *ffn_grads = feed(
        packed, ids, doc_lengths, norm_gains, resid_two, mixed_cross, cot_swap.state[0], cotangent, w_mid, w_ffn
    )
    out_swap = Swap(output_sent)
    cross_args = cross_args[1:]
    parts = (qa_cross, (k_cross, 0), (v_cross, 0))
    if packed:
        ffn = Scatter(*ffn_grads)
        grad_mixed = begin(grad_mixed, out_swap, ffn)
        grads = cross_backward(*cross_args, *parts, grad_mixed, mixed_cross, 0, 2)
        grads = hold(grads, ffn)
        ffn.second()
        grads, grad_mixed = begin((grads, grad_mixed), ffn)
        grads_cross = cross_backward(*cross_args, *parts, grad_mixed, mixed_cross, 2, pairs, (grads,))
        grads_cross = hold(grads_cross, ffn)
        ffn.third()
        grads_cross = begin(grads_cross, ffn)
    else:
        begin((), out_swap)
        grads_cross = cross_backward(*cross_args, *parts, grad_mixed, mixed_cross, 0, pairs)
    grads_cross = hold(grads_cross, out_swap)
    grad_two, grad_mixed, gmem, gmem_sent, gain_two, *mid_grads = cross_back(
        packed, ids, norm_gains, grads_cross, resid_two, normed_two, *mem, grad_three, mixed_cross, mixed_self, w_mid
    )
    gmem_swap = Swap(gmem_sent)
    parts = (qa_self, (qkv, pairs), (qkv, 2 * pairs))
    more = (mixed_self, normed_one)
    if packed:
        mid = Scatter(*mid_grads)
        hold((), ffn)
        ffn.fourth()
        grad_mixed = begin(grad_mixed, mid, gmem_swap, ffn)
        results = self_backward(1, packed, *self_args[1:], *parts, grad_mixed, *more, 0, 1)
        results = hold(results, mid)
        mid.second()
        results, grad_mixed = begin((results, grad_mixed), mid)
        d_theirs, table_theirs, *grads_theirs = self_backward(
            1, packed, *self_args[1:], *parts, grad_mixed, *more, 1, None, results
        )
        d_theirs, grads_theirs, grad_mixed = hold((d_theirs, grads_theirs, grad_mixed), mid, ffn)
        theirs = SideScatter(*grads_theirs)
        theirs.launch()
        mid.third()
        ffn.fifth()
        mid.sent, ffn.sent = hold((mid.sent, ffn.sent), theirs)
        theirs.flip(1)
        grad_mixed = begin(grad_mixed, mid, theirs, ffn)
        d_ours, table_ours, *grads_ours = self_backward(0, packed, *self_args[1:], *parts, grad_mixed, *more)
        d_ours, grads_ours = hold((d_ours, grads_ours), mid, theirs, gmem_swap, ffn)
        ours = SideScatter(*grads_ours)
        ours.launch()
        theirs.across()
        mid.fourth()
        theirs.sent, mid.sent = hold((theirs.sent, mid.sent), ours)
        ours.flip(1)
        d_ours = begin(d_ours, ours, theirs, mid)
    else:
        begin((), gmem_swap)
        d_theirs, table_theirs, *grads_theirs = self_backward(1, packed, *self_args[1:], *parts, grad_mixed, *more)
        d_ours, table_ours, *grads_ours = self_backward(0, packed, *self_args[1:], *parts, grad_mixed, *more)
    grad_x, grad_x_sent, gain_one = self_back(ids, norm_gains, d_ours, d_theirs, *x, grad_two, w_self)
    grad_x_swap = Swap(grad_x_sent)
    half_of = (jnp.arange(pairs, dtype=jnp.int32) >= pairs // 2).astype(jnp.int32)[:, None, None]
    if packed:
        grad_x_swap.sent, gain_one, table_ours, table_theirs = hold(
            (grad_x_swap.sent, gain_one, table_ours, table_theirs), mid, ours, theirs
        )
        ours.flip(2, theirs.state[0])
        mid.fifth()
        gain_one, table_ours, table_theirs = begin(
            (gain_one, table_ours, table_theirs), grad_x_swap, ours, mid
        )
    table = jnp.where(half_of == me, table_ours, table_theirs).reshape(-1, width)
    small = jnp.concatenate([gain_one, gain_two, gain_three, table])
    if packed:
        small = Sum(small, 0)
        small.launch()
        output, out_swap.state, gmem, gmem_swap.state, ffn.state = hold(
            (output, out_swap.state, gmem, gmem_swap.state, ffn.state), small
        )
        small.flip(1)
        small.launch()
        hold((), ours, small)
        small.flip(2)
        ours.flip(3)
        begin((), small, ours)
        hold((), small, mid)
        small.flip(3)
        small.launch()
        hold((), small, grad_x_swap)
        small.flip(None)
        small.launch()
        ffn_grads = ffn.total()
        mid_grads = mid.total()
        ours.take()
        self_grads = ours.kept
        small.take()
        small = small.values
    else:
        begin((), grad_x_swap)
        ffn_grads = scatter_whole(ffn_grads[0].transpose(1, 2, 0, 3).reshape(3, width, -1))
        mid_grads = scatter_whole(mid_grads[0])
        self_grads = scatter_whole(
            jnp.where(
                me == 0,
                jnp.concatenate([grads_ours[0], grads_theirs[0]], axis=2),
                jnp.concatenate([grads_theirs[0], grads_ours[0]], axis=2),
            )
        )
        small = lax.psum(small, ("dp", "mp"))
    table = small[3:].reshape(pairs, -1, LANES)[:, :2, :NB].reshape(2 * pairs, NB).T
    output = both_halves(output, out_swap.state[0], me)
    grad_memory = both_halves(gmem, gmem_swap.state[0], me)
    grad_tokens = both_halves(grad_x, grad_x_swap.state[0], me)
    return (
        output,
        grad_tokens,
        grad_memory,
        small[:3],
        table,
        self_grads,
        mid_grads[0].T,
        mid_grads[1:4],
        mid_grads[4].T,
        ffn_grads[:2],
        ffn_grads[2].T,
    )


def solution(mesh):
    rows = P("dp", "mp", None)
    proj = P(None, "dp", "mp")
    out = P("mp", "dp")
    return jax.shard_map(
        per_device,
        mesh=mesh,
        in_specs=(rows, rows, P("dp", None), P("dp"), P(), P(), proj, out, proj, out, proj, out, rows),
        out_specs=(rows, rows, rows, P(), P(), proj, out, proj, out, proj, out),
        check_vma=False,
    )
```

```python
import functools
import jax
import jax.numpy as jnp
import numpy as np
from jax import lax
from jax.experimental import pallas as pl
from jax.experimental.pallas import tpu as pltpu
from jax.sharding import PartitionSpec as P

DH = 64
NB = 32
REACH = 128
ROW = 1024
LANES = 128
QB = 256
masked_score = -1000000000.0
BF = jnp.bfloat16
F32 = jnp.float32
SELF_FORWARD_MB = 20
CROSS_FORWARD_MB = 56
BACKWARD_MB = 56
PROJECT_MB = 20
MIDDLE_MB = 56
FEED_MB = 60
CROSS_BACK_MB = 56
WEIGHTS_MB = 56
SELF_BACK_MB = 56


def params(megabytes):
    return pltpu.CompilerParams(vmem_limit_bytes=megabytes * 1024 * 1024, dimension_semantics=("arbitrary",))


def dot_t(a, b):
    return lax.dot_general(a, b, (((1,), (1,)), ((), ())), preferred_element_type=F32)


def dot_n(a, b):
    return lax.dot_general(a, b, (((1,), (0,)), ((), ())), preferred_element_type=F32)


def dot_tn(a, b):
    return lax.dot_general(a, b, (((0,), (0,)), ((), ())), preferred_element_type=F32)


def split_three(x):
    top = x.astype(BF)
    rest = x - top.astype(F32)
    mid = rest.astype(BF)
    low = (rest - mid.astype(F32)).astype(BF)
    return top.astype(F32), mid.astype(F32), low.astype(F32)


def place_three(x, slot, other):
    top, mid, low = split_three(x)
    return jnp.where(slot == 4, top, jnp.where(slot == 5, mid, jnp.where(slot == 6, low, other)))


def lane_slots(shape):
    lane = lax.broadcasted_iota(jnp.int32, shape, 1)
    return lane, lane % DH


def make_extras(ids_ref, bounds_ref, causal, extra_q, extra_k):
    me = ids_ref[1]
    shape = extra_q.shape
    _, slot = lane_slots(shape)
    rows = lax.broadcasted_iota(jnp.int32, shape, 0)
    if causal:
        first = bounds_ref[me, 0]
        second = first + bounds_ref[me, 1]
        third = second + bounds_ref[me, 2]
        seg = (
            (rows >= first).astype(jnp.int32)
            + (rows >= second).astype(jnp.int32)
            + (rows >= third).astype(jnp.int32)
        )
        own = jnp.where(slot == seg, 1.0, 0.0)
        barred = jnp.where((slot < 4) & (slot != seg), masked_score, 0.0)
    else:
        own = jnp.where(slot == 0, 1.0, 0.0)
        barred = jnp.where((slot == 0) & (rows >= bounds_ref[me]), masked_score, 0.0)
    extra_q[...] = jnp.where(slot == 7, 1.0, own).astype(BF)
    extra_k[...] = jnp.where((slot >= 4) & (slot <= 6), 1.0, barred).astype(BF)


def band_square(band_ref, head):
    wide = jnp.broadcast_to(band_ref[head : head + 1, :], (LANES, 3 * LANES))
    rolled = pltpu.roll(wide, 0, 1, stride=1, stride_axis=0)
    return rolled[:, LANES : 2 * LANES], rolled[:, :LANES]


def add_band(scores, first, near, side):
    above = jnp.full((LANES, LANES), masked_score, F32)
    corner = jnp.concatenate([side, jnp.zeros((LANES, LANES), F32)], axis=0)
    left = jnp.concatenate([near, side], axis=0)
    right = jnp.concatenate([above, near], axis=0)
    pieces = []
    if first > 0:
        pieces.append(scores[:, : first - LANES])
        pieces.append(scores[:, first - LANES : first] + corner)
    pieces.append(scores[:, first : first + LANES] + left)
    pieces.append(scores[:, first + LANES :] + right)
    return jnp.concatenate(pieces, axis=1)


def forward_kernel(causal, extra, ids_ref, bounds_ref, band_ref, q_ref, k_ref, v_ref, *rest):
    o_ref, qa_ref, extra_q, extra_k = rest[extra:]
    length = q_ref.shape[0]

    @pl.when(pl.program_id(0) == 0)
    def _():
        make_extras(ids_ref, bounds_ref, causal, extra_q, extra_k)

    lane, slot = lane_slots((QB, LANES))
    full_lane, full_slot = lane_slots((length, LANES))
    ones = jnp.where(full_slot == 0, 1.0, 0.0).astype(BF)
    keys, values, bands = [], [], []
    for head in range(2):
        mine = (full_lane < DH) == (head == 0)
        keys.append(jnp.where(mine, k_ref[...], extra_k[...]))
        values.append(jnp.where(mine, v_ref[...], ones))
        if causal:
            bands.append(band_square(band_ref, head))

    def scores_of(block, head):
        first = block * QB
        count = first + QB if causal else length
        mine_block = (lane < DH) == (head == 0)
        queries = jnp.where(mine_block, q_ref[first : first + QB, :], extra_q[first : first + QB, :])
        return queries, dot_t(queries, keys[head][:count])

    todo = [(block, head) for block in range(length // QB) for head in range(2)]
    ahead = [scores_of(*item) for item in todo[:2]]
    for at, (block, head) in enumerate(todo):
        first = block * QB
        span = slice(first, first + QB)
        queries, scores = ahead.pop(0)
        if at + 2 < len(todo):
            ahead.append(scores_of(*todo[at + 2]))
        if causal:
            scores = add_band(scores, first, *bands[head])
        top = jnp.max(scores, axis=1, keepdims=True)
        weights = jnp.exp(scores - top).astype(BF)
        mixed = dot_n(weights, values[head][: weights.shape[1]])
        spare_column = DH if head == 0 else 0
        total = mixed[:, spare_column : spare_column + 1]
        mixed = mixed * (1.0 / total)
        if head == 0:
            kept = mixed
        else:
            o_ref[span, :] = jnp.where(lane < DH, kept, mixed).astype(BF)
        spare = place_three(-(top + jnp.log(total)), slot, queries.astype(F32))
        qa_ref[head, span, :] = jnp.where((lane < DH) == (head == 0), queries, spare.astype(BF))


def backward_kernel(causal, packed, extra, ids_ref, bounds_ref, band_ref, qa_ref, k_ref, v_ref, g_ref, o_ref, *rest):
    if causal:
        rest = rest[:2] + rest[2 + extra :]
        near_ref, left, grad_ref, bias_ref = rest[:4]
        wgrads = rest[4:-6]
        extra_q, extra_k, dk_acc, dv_acc, near_acc, side_acc = rest[-6:]
    else:
        grad_ref, extra_q, extra_k, dk_acc, dv_acc = rest[-5:]
    length = k_ref.shape[0]

    @pl.when(pl.program_id(0) == 0)
    def _():
        make_extras(ids_ref, bounds_ref, causal, extra_q, extra_k)

    lane, slot = lane_slots((QB, LANES))
    full_lane, full_slot = lane_slots((length, LANES))
    spare_v = jnp.where((full_slot >= 4) & (full_slot <= 6), 1.0, 0.0).astype(BF)
    squares, wholes = [], []
    for head in range(2):
        mine = (full_lane < DH) == (head == 0)
        mine_block = (lane < DH) == (head == 0)
        keys = jnp.where(mine, k_ref[...], extra_k[...])
        values = jnp.where(mine, v_ref[...], spare_v)
        if causal:
            near, side = band_square(band_ref, head)
            near_acc[...] = jnp.zeros_like(near_acc)
            side_acc[...] = jnp.zeros_like(side_acc)
        dk_acc[head] = jnp.zeros(dk_acc.shape[1:], F32)
        dv_acc[head] = jnp.zeros(dv_acc.shape[1:], F32)
        for block in range(length // QB):
            first = block * QB
            count = first + QB if causal else length
            span = slice(first, first + QB)
            queries = qa_ref[head, span, :]
            upstream = g_ref[span, :]
            inner = jnp.sum(
                jnp.where(mine_block, upstream.astype(F32) * o_ref[span, :].astype(F32), 0.0), axis=1, keepdims=True
            )
            spare = place_three(-inner, slot, jnp.zeros((QB, LANES), F32))
            grads = jnp.where(mine_block, upstream, spare.astype(BF))
            scores = dot_t(queries, keys[:count])
            if causal:
                scores = add_band(scores, first, near, side)
            probs = jnp.exp(scores)
            lifted = dot_t(grads, values[:count])
            score_grads = (probs * lifted).astype(BF)
            dv_acc[head, :, :count] += dot_n(grads.T, probs.astype(BF))
            dk_acc[head, :, :count] += dot_n(queries.T, score_grads)
            dq = dot_n(score_grads, keys[:count]).astype(BF)
            if causal:
                near_acc[...] += score_grads[:LANES, first : first + LANES].astype(F32)
                near_acc[...] += score_grads[LANES:, first + LANES :].astype(F32)
                side_acc[...] += score_grads[LANES:, first : first + LANES].astype(F32)
                if block > 0:
                    side_acc[...] += score_grads[:LANES, first - LANES : first].astype(F32)
            if head == 0:
                grad_ref[0, span, :] = dq
            else:
                grad_ref[0, span, :] = jnp.where(lane < DH, grad_ref[0, span, :], dq)
        if causal:
            squares.append(jnp.concatenate([side_acc[...], near_acc[...]], axis=1))
            ones_row = DH + 7 if head == 0 else 7
            wholes.append(jnp.sum(dk_acc[head, ones_row : ones_row + 1, :], axis=1, keepdims=True))
    upper = lax.broadcasted_iota(jnp.int32, (LANES, length), 0) < DH
    grad_ref[1] = jnp.where(upper, dk_acc[0], dk_acc[1]).astype(BF).T
    grad_ref[2] = jnp.where(upper, dv_acc[0], dv_acc[1]).astype(BF).T
    if causal:
        wide = jnp.concatenate([jnp.stack(squares), jnp.zeros((2, LANES, LANES), F32)], axis=2)
        half = LANES // 2
        while half:
            wide = wide[:, :half] + pltpu.roll(wide[:, half:], 3 * LANES - half, 2)
            half //= 2
        diag = jnp.concatenate([wide[0], wide[1], jnp.zeros((6, 3 * LANES), F32)], axis=0)[:, : 2 * LANES]
        table = lax.dot_general(
            diag, near_ref[...], (((1,), (0,)), ((), ())),
            precision=lax.Precision.HIGHEST, preferred_element_type=F32,
        )
        whole = jnp.concatenate(wholes + [jnp.zeros((6, 1), F32)], axis=0)
        last = whole - jnp.sum(table, axis=1, keepdims=True)
        at_last = lax.broadcasted_iota(jnp.int32, table.shape, 1) == NB - 1
        bias_ref[0] = jnp.where(at_last, last, table)
    if causal:
        right = jnp.concatenate([grad_ref[n] for n in range(3)], axis=1)
        grads = dot_n(left[...], right).astype(BF)
        middle_row = grads.shape[0] // 2
        for n in range(3):
            part = grads[:, n * LANES : (n + 1) * LANES]
            if packed:
                shape = wgrads[0].shape[:3] + wgrads[0].shape[4:]
                wgrads[0][:, :, :, n] = part[:middle_row].reshape(shape)
                wgrads[1][:, :, :, n] = part[middle_row:].reshape(shape)
            else:
                wgrads[0][n] = part


def attention_forward(causal, ids, bounds, band, q, k, v, cols, start=0, stop=None, into=()):
    rows = q[0].shape[0]
    pairs = (cols // LANES if stop is None else stop) - start

    def spec(offset):
        return pl.BlockSpec((rows, LANES), lambda p, ids: (0, p + offset + start))

    n = rows * rows * pairs * 2
    return call(
        functools.partial(forward_kernel, causal, len(into)), "attention_forward", SELF_FORWARD_MB if causal else CROSS_FORWARD_MB, pairs,
        [
            pl.BlockSpec(memory_space=pltpu.SMEM),
            pl.BlockSpec((None, 2, 3 * LANES), lambda p, ids: (p + start, 0, 0)),
            spec(q[1]), spec(k[1]), spec(v[1]),
        ] + [anywhere()] * len(into),
        [
            (spec(0), (rows, cols), BF),
            (pl.BlockSpec((2, rows, LANES), lambda p, ids: (p + start, 0, 0)), (2 * cols // LANES, rows, LANES), BF),
        ],
        [pltpu.VMEM((rows, LANES), BF)] * 2,
        n * 256 * 4 // (2 if causal else 1), rows * cols * 16,
        {6: 0, 7: 1} if into else {},
    )(ids, bounds, band, q[0], k[0], v[0], *into)


def cross_backward(ids, bounds, band, qa, k, v, g, o, start, stop, into=()):
    rows, cols = g.shape

    def spec(offset):
        return pl.BlockSpec((rows, LANES), lambda p, ids: (0, p + start + offset))

    n = rows * rows * (stop - start) * 2
    return call(
        functools.partial(backward_kernel, False, False, 0), "cross_backward", BACKWARD_MB, stop - start,
        [
            pl.BlockSpec(memory_space=pltpu.SMEM),
            pl.BlockSpec((None, 2, 3 * LANES), lambda p, ids: (p + start, 0, 0)),
            pl.BlockSpec((2, rows, LANES), lambda p, ids: (p + start, 0, 0)),
            spec(k[1]), spec(v[1]), spec(0), spec(0),
        ] + [anywhere()] * len(into),
        [(pl.BlockSpec((3, rows, LANES), lambda p, ids: (0, 0, p + start)), (3, rows, cols), BF)],
        [pltpu.VMEM((rows, LANES), BF)] * 2 + [pltpu.VMEM((2, LANES, rows), F32)] * 2,
        n * 256 * 10, rows * cols * 20,
        {8: 0} if into else {},
    )(ids, bounds, band, qa, k[0], v[0], g, o, *into)[0]


def self_backward(side, packed, ids, bounds, band, qa, k, v, g, o, normed_t, start=0, stop=None, into=()):
    rows, cols = g.shape
    pairs = cols // LANES // 2
    stop = pairs if stop is None else stop
    depth = normed_t.shape[0] >> BITS

    def at(p, ids):
        return p + start + pairs * jnp.bitwise_xor(ids[1], side)

    def spec(offset):
        return pl.BlockSpec((rows, LANES), lambda p, ids: (0, at(p, ids) + offset))

    n = rows * rows * (stop - start) * 2
    if packed:
        block = pl.BlockSpec((2, 2, 2, 3, depth, LANES), lambda p, ids: (0, 0, 0, 0, 0, p + start))
        wgrads = [(block, (2, 2, 2, 3, depth, cols // 2), BF)] * 2
    else:
        block = pl.BlockSpec((3, normed_t.shape[0], LANES), lambda p, ids: (0, 0, p + start))
        wgrads = [(block, (3, normed_t.shape[0], cols // 2), BF)]
    return call(
        functools.partial(backward_kernel, True, packed, len(into)), "self_backward", BACKWARD_MB, stop - start,
        [
            pl.BlockSpec(memory_space=pltpu.SMEM),
            pl.BlockSpec((None, 2, 3 * LANES), lambda p, ids: (at(p, ids), 0, 0)),
            pl.BlockSpec((2, rows, LANES), lambda p, ids: (at(p, ids), 0, 0)),
            spec(k[1]), spec(v[1]), spec(0), spec(0),
            held((2 * LANES, LANES)), held(normed_t.shape),
        ] + [anywhere()] * len(into),
        [
            (pl.BlockSpec((3, rows, LANES), lambda p, ids: (0, 0, p + start)), (3, rows, cols // 2), BF),
            (pl.BlockSpec((1, 8, LANES), lambda p, ids: (at(p, ids), 0, 0)), (2 * pairs, 8, LANES), F32),
        ] + wgrads,
        [pltpu.VMEM((rows, LANES), BF)] * 2 + [pltpu.VMEM((2, LANES, rows), F32)] * 2
        + [pltpu.VMEM((LANES, LANES), F32)] * 2,
        n * 256 * 8, rows * cols * 20,
        {10 + i: i for i in range(len(into))},
    )(ids, bounds, band, qa, k[0], v[0], g, o, jnp.asarray(near_buckets()), normed_t, *into)


def near_buckets():
    buckets = bucket_table(LANES, NB, REACH)
    table = np.zeros((2 * LANES, LANES), np.float32)
    for distance in range(LANES):
        if buckets[distance] < NB - 1:
            table[LANES - distance, buckets[distance]] = 1.0
    return table


def bucket_table(length, buckets, reach):
    offsets = np.arange(length)
    exact_part = buckets // 2
    scaled = np.log(np.maximum(offsets, 1) / exact_part) / np.log(reach / exact_part) * (buckets - exact_part)
    far_bucket = np.minimum(exact_part + np.floor(scaled).astype(np.int64), buckets - 1)
    return np.where(offsets < exact_part, offsets, far_bucket).astype(np.int32)


def bias_band(rel_table):
    distance = LANES - np.arange(3 * LANES)
    buckets = bucket_table(LANES + 1, NB, REACH)
    onehot = np.zeros((3 * LANES, NB), np.float32)
    shift = np.zeros((3 * LANES,), np.float32)
    for at, far in enumerate(distance):
        if 0 <= far < LANES:
            onehot[at, buckets[far]] = 1.0
        elif -LANES < far < 0:
            shift[at] = masked_score
    relative = rel_table - rel_table[NB - 1 :]
    band = jnp.dot(jnp.asarray(onehot), relative, precision=lax.Precision.HIGHEST) + shift[:, None]
    return band.T.reshape(-1, 2, 3 * LANES)


epsilon = 1e-06
TB = 256
BITS = 4


def rms(values, gain):
    inverse = lax.rsqrt(jnp.mean(values * values, axis=-1, keepdims=True) + epsilon)
    return (values * inverse * gain).astype(BF), inverse


def rms_back(values, inverse, gain, upstream):
    weighted = upstream * gain
    inner_mean = jnp.mean(weighted * values, axis=-1, keepdims=True)
    grad_values = inverse * weighted - values * (inverse * inverse * inverse * inner_mean)
    return grad_values, jnp.sum(upstream * values * inverse, axis=0, keepdims=True)


def cost(flops, moved):
    return pl.CostEstimate(flops=flops, bytes_accessed=moved, transcendentals=0)


def turn(s, ids, blocks):
    return ((1 - ids[1]) * (blocks // 2) + jnp.minimum(s, blocks - 1)) % blocks


def row_span(s, ids, blocks):
    return pl.ds(pl.multiple_of(turn(s, ids, blocks) * TB, TB), TB)


def row_spec(blocks, width, *lead):
    zeros = (0,) * len(lead)
    return pl.BlockSpec(lead + (TB, width), lambda s, ids: zeros + (turn(s, ids, blocks), 0))


def kept_spec(blocks, width):
    half = blocks // 2
    return pl.BlockSpec((None, TB, width), lambda s, ids: (ids[1], jnp.clip(s - half, 0, half - 1), 0))


def own_spec(blocks, width):
    half = blocks // 2
    return pl.BlockSpec((TB, width), lambda s, ids: (jnp.clip(s - half, 0, half - 1), 0))


def other_spec(blocks, width):
    return pl.BlockSpec((TB, width), lambda s, ids: (jnp.minimum(s, blocks // 2 - 1), 0))


def held(shape):
    zeros = (0,) * len(shape)
    return pl.BlockSpec(shape, lambda s, ids: zeros, pipeline_mode=pl.Buffered(1))


def anywhere():
    return pl.BlockSpec(memory_space=pl.ANY)


def call(kernel, name, megabytes, grid, in_specs, outs, scratch, flops, moved, aliases=None):
    return pl.pallas_call(
        kernel,
        grid_spec=pltpu.PrefetchScalarGridSpec(
            num_scalar_prefetch=1,
            grid=(grid,),
            in_specs=in_specs,
            out_specs=[o[0] for o in outs],
            scratch_shapes=scratch,
        ),
        out_shape=[jax.ShapeDtypeStruct(o[1], o[2]) for o in outs],
        input_output_aliases=aliases or {},
        compiler_params=params(megabytes),
        cost_estimate=cost(flops, moved),
        name=name,
    )


def chosen(step, blocks, came_ref, kept_ref):
    return jnp.where(step < blocks // 2, came_ref[...], kept_ref[...])


def share(step, blocks, values, own_ref, other_ref):
    @pl.when(step < blocks // 2)
    def _():
        other_ref[...] = values.astype(BF)

    @pl.when(step >= blocks // 2)
    def _():
        own_ref[...] = values


def gather_table():
    near = [((0, 0, 0),), ((0, 1, 0),), ((1, 0, 0), (1, 1, 0)), ((0, 0, 1),), ((1, 0, 1),), ((0, 1, 1), (1, 1, 1))]
    table = []
    for c in range(2):
        for places in near:
            entries = []
            for at, (y, x, z0) in enumerate(places):
                for z1 in range(2):
                    entries.append(((at, z1) if len(places) > 1 else (z1,), (y, x, z0, z1, c), 0))
            table.append(entries)
    return table


def wide_table():
    pairs = [(a, b) for a in range(2) for b in range(2)]
    table = []
    for c in range(2):
        for y in range(2):
            table.append([((z0, z1, x), (y, x, z0, z1, c), 0) for x in range(2) for z0, z1 in pairs])
    for c in range(2):
        for z0 in range(2):
            table.append([((z1, y, x), (y, x, z0, z1, c), 1) for x in range(2) for z1, y in pairs])
    return table


def copy_pieces(ids_ref, pieces, table, place, w_ref, sem):
    if len(pieces) == 1:
        for x in range(sem.shape[0]):
            part = pieces[0].at[x] if sem.shape[0] > 1 else pieces[0]
            target = w_ref.at[x] if sem.shape[0] > 1 else w_ref
            pltpu.make_async_copy(part, target, sem.at[x]).start()
        return
    mine = ids_ref[2]
    rows = pieces[0].shape[-2]

    def copy(flip):
        for first in range(2):
            for piece, entries in zip(pieces, table):
                for at, (y, x, z0, z1, c), part in entries:
                    if x ^ flip != first:
                        continue
                    block = jnp.bitwise_xor(mine, 8 * z1 + 4 * z0 + 2 * y + c)
                    span = pl.ds(pl.multiple_of(block * rows, 16), rows)
                    target, done = place(span, x ^ flip, part)
                    pltpu.make_async_copy(piece.at[at], target, done).start()

    @pl.when(ids_ref[1] == 0)
    def _():
        copy(0)

    @pl.when(ids_ref[1] == 1)
    def _():
        copy(1)


def wait_pieces(w_ref, sem):
    pltpu.make_async_copy(w_ref, w_ref, sem).wait()


def natural_place(w_ref, cols, sem):
    return lambda span, x, part: (w_ref.at[:, span, x * cols : (x + 1) * cols], sem.at[0])


def put_turned(packed, ids_ref, target, span, values):
    turned = values.T
    if not packed:
        target[:, span] = turned
        return
    depth = turned.shape[0] >> BITS
    for block in range(1 << BITS):
        reverse = int(format(block, "04b")[::-1], 2)
        at = jnp.bitwise_xor(ids_ref[0], reverse) * depth
        target[pl.ds(pl.multiple_of(at, 16), depth), span] = turned[block * depth : (block + 1) * depth]


def put_grads(packed, ids_ref, grads, outs):
    if not packed:
        outs[0][...] = grads
        return
    keep_ref, send_ref = outs
    rows, cols = keep_ref.shape[-2:]
    middle = grads.shape[0] // 2

    def store(flip):
        for x in range(2):
            first = cols * (x ^ flip)
            for target, part in ((keep_ref, grads[:middle]), (send_ref, grads[middle:])):
                target[:, x] = part[:, first : first + cols].reshape(2, 2, 2, rows, cols)

    @pl.when(ids_ref[1] == 0)
    def _():
        store(0)

    @pl.when(ids_ref[1] == 1)
    def _():
        store(1)


def grads_out(packed, n, width, first):
    def at(s):
        return jnp.maximum(s - first, 0)

    if not packed:
        return [(pl.BlockSpec((None, width, width), lambda s, ids: (at(s), 0, 0)), (n, width, width), BF)]
    rows, cols = width >> BITS, width // 2
    block = pl.BlockSpec((2, 2, 2, 2, None, rows, cols), lambda s, ids: (0, 0, 0, 0, at(s), 0, 0))
    return [(block, (2, 2, 2, 2, n, rows, cols), BF)] * 2


def project_kernel(blocks, pieces, packed, ids_ref, gain_ref, came_ref, kept_ref, *refs):
    w_in = refs[:pieces]
    turned_ref, out_ref, w_ref, sem = refs[pieces:]
    step = pl.program_id(0)

    @pl.when(step == 0)
    def _():
        copy_pieces(ids_ref, w_in, gather_table(), natural_place(w_ref, w_in[0].shape[-1], sem), w_ref, sem)
        wait_pieces(w_ref, sem.at[0])

    normed, _ = rms(chosen(step, blocks, came_ref, kept_ref).astype(F32), gain_ref[0:1, :])
    put_turned(packed, ids_ref, turned_ref, row_span(step, ids_ref, blocks), normed)
    width = normed.shape[1]
    for s in range(3):
        out_ref[:, s * width : (s + 1) * width] = dot_n(normed, w_ref[s]).astype(BF)


def project(packed, ids, gain, came, kept, pieces):
    _, half, width = kept.shape
    rows = 2 * half
    blocks = rows // TB
    full = (3, width, width)
    return call(
        functools.partial(project_kernel, blocks, len(pieces), packed), "project", PROJECT_MB, blocks,
        [held((3, width)), other_spec(blocks, width), kept_spec(blocks, width)] + [anywhere()] * len(pieces),
        [
            (held((width, rows)), (width, rows), BF),
            (row_spec(blocks, 3 * width), (rows, 3 * width), BF),
            (held(full), full, BF),
        ],
        [pltpu.SemaphoreType.DMA((1,))],
        6 * rows * width * width, 10 * rows * width + 6 * width * width,
    )(ids, gain, came, kept, *pieces)


def middle_kernel(blocks, pieces, packed, ids_ref, gain_ref, came_ref, kept_ref, mixed_ref, mem_came_ref, mem_kept_ref, *refs):
    w_in = refs[:pieces]
    resid_ref, turned_ref, mem_turned_ref, q_ref, k_ref, v_ref, w_ref, sem = refs[pieces:]
    step = pl.program_id(0)

    @pl.when(step == 0)
    def _():
        copy_pieces(ids_ref, w_in, gather_table(), natural_place(w_ref, w_in[0].shape[-1], sem), w_ref, sem)
        wait_pieces(w_ref, sem.at[0])

    resid = chosen(step, blocks, came_ref, kept_ref).astype(F32) + dot_t(mixed_ref[...], w_ref[0])
    resid_ref[...] = resid
    normed, _ = rms(resid, gain_ref[1:2, :])
    span = row_span(step, ids_ref, blocks)
    put_turned(packed, ids_ref, turned_ref, span, normed)
    q_ref[...] = dot_n(normed, w_ref[1]).astype(BF)
    memory = chosen(step, blocks, mem_came_ref, mem_kept_ref)
    put_turned(packed, ids_ref, mem_turned_ref, span, memory)
    k_ref[...] = dot_n(memory, w_ref[2]).astype(BF)
    v_ref[...] = dot_n(memory, w_ref[3]).astype(BF)


def middle(packed, ids, gain, came, kept, mixed, mem_came, mem_kept, pieces):
    rows, width = mixed.shape
    blocks = rows // TB
    full = (5, width, width)
    spec = row_spec(blocks, width)
    pair = [other_spec(blocks, width), kept_spec(blocks, width)]
    return call(
        functools.partial(middle_kernel, blocks, len(pieces), packed), "middle", MIDDLE_MB, blocks,
        [held((3, width))] + pair + [spec] + pair + [anywhere()] * len(pieces),
        [(spec, (rows, width), F32)] + [(held((width, rows)), (width, rows), BF)] * 2
        + [(spec, (rows, width), BF)] * 3 + [(held(full), full, BF)],
        [pltpu.SemaphoreType.DMA((1,))],
        8 * rows * width * width, 20 * rows * width + 10 * width * width,
    )(ids, gain, came, kept, mixed, mem_came, mem_kept, *pieces)


def feed_kernel(blocks, pieces, packed, ids_ref, docs_ref, gain_ref, resid_ref, mixed_ref, cot_came_ref, cot_kept_ref,
                wo_ref, *refs):
    w_in = refs[:pieces]
    refs = refs[pieces:]
    own_ref, other_ref, grad_ref, gmix_ref, gain_grad_ref = refs[:5]
    wgrads = refs[5:-7]
    w_ref, normed_t, branch_t, hidden_s, gate_s, up_s, sem = refs[-7:]
    step = pl.program_id(0)
    me = ids_ref[1]
    width = resid_ref.shape[1]

    def weight(which, x):
        return w_ref[x, which]

    @pl.when(step == 0)
    def _():
        cols = w_in[0].shape[-1]
        copy_pieces(
            ids_ref, w_in, wide_table(),
            lambda span, x, part: (w_ref.at[x, :, span, cols * part : cols if part == 0 else None], sem.at[x]), w_ref, sem,
        )
        gain_grad_ref[...] = jnp.zeros_like(gain_grad_ref)

    @pl.when(step < blocks)
    def _():
        first = pl.multiple_of(turn(step, ids_ref, blocks) * TB, TB)
        span = pl.ds(first, TB)
        resid = resid_ref[...] + dot_t(mixed_ref[...], wo_ref[...])
        normed, inverse = rms(resid, gain_ref[2:3, :])
        slots = first + lax.broadcasted_iota(jnp.int32, (TB, 1), 0)
        padding = slots >= docs_ref[me, 0] + docs_ref[me, 1] + docs_ref[me, 2]
        grad_four = jnp.where(padding, 0.0, chosen(step, blocks, cot_came_ref, cot_kept_ref).astype(F32))
        branch = grad_four.astype(BF)
        put_turned(packed, ids_ref, normed_t, span, normed)
        put_turned(packed, ids_ref, branch_t, span, branch)
        total = resid
        upstream = jnp.zeros((TB, width), F32)
        for x in range(2):

            @pl.when(step == 0)
            def _():
                wait_pieces(w_ref.at[x], sem.at[x])

            gate = dot_n(normed, weight(0, x))
            up = dot_n(normed, weight(1, x))
            lifted = dot_n(branch, weight(2, x))
            square = gate * gate
            inner = jnp.tanh(gate * (0.7978845608028654 + 0.035677408136300125 * square))
            half_up = 0.5 + 0.5 * inner
            activated = gate * half_up
            slope = half_up + (0.5 * gate) * (1.0 - inner * inner) * (
                0.7978845608028654 + 0.10703222440890037 * square
            )
            hidden = (activated * up).astype(BF)
            gate_grad = (lifted * up * slope).astype(BF)
            up_grad = (lifted * activated).astype(BF)
            hidden_s[x, span, :] = hidden
            gate_s[x, span, :] = gate_grad
            up_s[x, span, :] = up_grad
            total = total + dot_t(hidden, weight(2, x))
            upstream = upstream + dot_t(gate_grad, weight(0, x)) + dot_t(up_grad, weight(1, x))
        share(step, blocks, jnp.where(padding, 0.0, total), own_ref, other_ref)
        grad_resid, gain_grad = rms_back(resid, inverse, gain_ref[2:3, :], upstream)
        grad = grad_four + grad_resid
        grad_ref[...] = grad
        gain_grad_ref[...] += gain_grad
        gmix_ref[...] = dot_n(grad.astype(BF), wo_ref[...]).astype(BF)

    for which, (left, right) in enumerate(((normed_t, gate_s), (normed_t, up_s), (branch_t, hidden_s))):
        for x in range(2):

            @pl.when(step == blocks + 2 * which + x)
            def _():
                if packed:
                    grads = dot_n(left[...], right[jnp.bitwise_xor(x, me)]).astype(BF)
                    middle_row = grads.shape[0] // 2
                    wgrads[0][...] = grads[:middle_row].reshape(wgrads[0].shape)
                    wgrads[1][...] = grads[middle_row:].reshape(wgrads[1].shape)
                else:
                    wgrads[0][...] = dot_n(left[...], right[x]).astype(BF)


def feed(packed, ids, docs, gain, resid, mixed, cot_came, cot_kept, w_mid, pieces):
    rows, width = resid.shape
    half = pieces[0].shape[-1] if len(pieces) == 1 else pieces[0].shape[-1] + pieces[-1].shape[-1]
    blocks = rows // TB
    spec = row_spec(blocks, width)

    def at(s):
        late = jnp.maximum(s - blocks, 0)
        return late // 2, late % 2

    if packed:
        depth = width >> BITS
        block = pl.BlockSpec((2, None, 2, 2, None, depth, half), lambda s, ids: (0, at(s)[1], 0, 0, at(s)[0], 0, 0))
        wgrads = [(block, (2, 2, 2, 2, 3, depth, half), BF)] * 2
    else:
        block = pl.BlockSpec((None, None, width, half), lambda s, ids: (at(s)[1], at(s)[0], 0, 0))
        wgrads = [(block, (2, 3, width, half), BF)]
    return call(
        functools.partial(feed_kernel, blocks, len(pieces), packed), "feed", FEED_MB, blocks + 6,
        [pl.BlockSpec(memory_space=pltpu.SMEM), held((3, width)), spec, spec, other_spec(blocks, width),
         kept_spec(blocks, width),
         pl.BlockSpec((None, width, width), lambda s, ids: (4, 0, 0), pipeline_mode=pl.Buffered(1))]
        + [anywhere()] * len(pieces),
        [
            (own_spec(blocks, width), (rows // 2, width), F32),
            (other_spec(blocks, width), (rows // 2, width), BF),
            (spec, (rows, width), F32),
            (spec, (rows, width), BF),
            (held((1, width)), (1, width), F32),
        ] + wgrads,
        [pltpu.VMEM((2, 3, width, half), BF)] + [pltpu.VMEM((width, rows), BF)] * 2
        + [pltpu.VMEM((2, rows, half), BF)] * 3 + [pltpu.SemaphoreType.DMA((2,))],
        36 * rows * width * half, 24 * rows * width + 24 * width * half,
    )(ids, docs, gain, resid, mixed, cot_came, cot_kept, w_mid, *pieces)


def cross_back_kernel(blocks, packed, ids_ref, gain_ref, d_ref, resid_ref, normed_t, mem_t, grad_ref,
                       mixed_cross_ref, mixed_self_ref, w_ref, *outs):
    grad_two_ref, gmix_ref, gmem_own_ref, gmem_other_ref, gain_grad_ref = outs[:5]
    wgrads = outs[5:-2]
    lefts, rights = outs[-2:]
    step = pl.program_id(0)

    @pl.when(step == 0)
    def _():
        gain_grad_ref[...] = jnp.zeros_like(gain_grad_ref)

    @pl.when(step < blocks)
    def _():
        span = pl.ds(pl.multiple_of(turn(step, ids_ref, blocks) * TB, TB), TB)
        resid = resid_ref[...]
        inverse = lax.rsqrt(jnp.mean(resid * resid, axis=-1, keepdims=True) + epsilon)
        grad_resid, gain_grad = rms_back(resid, inverse, gain_ref[1:2, :], dot_t(d_ref[0], w_ref[1]))
        gain_grad_ref[...] += gain_grad
        grad_three = grad_ref[...]
        grad_two = grad_three + grad_resid
        grad_two_ref[...] = grad_two
        branch = grad_two.astype(BF)
        gmix_ref[...] = dot_n(branch, w_ref[0]).astype(BF)
        gmem = dot_t(d_ref[1], w_ref[2]) + dot_t(d_ref[2], w_ref[3])
        share(step, blocks, gmem, gmem_own_ref, gmem_other_ref)
        put_turned(packed, ids_ref, lefts.at[0], span, branch)
        put_turned(packed, ids_ref, lefts.at[1], span, grad_three.astype(BF))
        rights[0, span, :] = mixed_self_ref[...]
        rights[1, span, :] = d_ref[0]
        rights[2, span, :] = d_ref[1]
        rights[3, span, :] = d_ref[2]
        rights[4, span, :] = mixed_cross_ref[...]

    for n, left in enumerate((lefts.at[0], normed_t, mem_t, mem_t, lefts.at[1])):

        @pl.when(step == blocks + n)
        def _():
            put_grads(packed, ids_ref, dot_n(left[...], rights[n]).astype(BF), wgrads)


def cross_back(packed, ids, gain, d, resid, normed_t, mem_t, grad, mixed_cross, mixed_self, w):
    rows, width = resid.shape
    blocks = rows // TB
    spec = row_spec(blocks, width)
    return call(
        functools.partial(cross_back_kernel, blocks, packed), "cross_back", CROSS_BACK_MB, blocks + 5,
        [held((3, width)), row_spec(blocks, width, 3), spec, held((width, rows)), held((width, rows)),
         spec, spec, spec, held(w.shape)],
        [
            (spec, (rows, width), F32),
            (spec, (rows, width), BF),
            (own_spec(blocks, width), (rows // 2, width), F32),
            (other_spec(blocks, width), (rows // 2, width), BF),
            (held((1, width)), (1, width), F32),
        ] + grads_out(packed, 5, width, blocks),
        [pltpu.VMEM((2, width, rows), BF), pltpu.VMEM((5, rows, width), BF)],
        18 * rows * width * width, 36 * rows * width + 20 * width * width,
    )(ids, gain, d, resid, normed_t, mem_t, grad, mixed_cross, mixed_self, w)


def self_back_kernel(blocks, ids_ref, gain_ref, ours_ref, theirs_ref, came_ref, kept_ref, grad_ref, w_ref,
                     own_ref, other_ref, gain_grad_ref):
    step = pl.program_id(0)

    @pl.when(step == 0)
    def _():
        gain_grad_ref[...] = jnp.zeros_like(gain_grad_ref)

    values = chosen(step, blocks, came_ref, kept_ref).astype(F32)
    inverse = lax.rsqrt(jnp.mean(values * values, axis=-1, keepdims=True) + epsilon)
    upstream = jnp.zeros(values.shape, F32)
    for n in range(3):
        ours, theirs = ours_ref[n], theirs_ref[n]
        first = jnp.where(ids_ref[1] == 0, ours, theirs)
        second = jnp.where(ids_ref[1] == 0, theirs, ours)
        upstream = upstream + dot_t(jnp.concatenate([first, second], axis=1), w_ref[n])
    grad_values, gain_grad = rms_back(values, inverse, gain_ref[0:1, :], upstream)
    gain_grad_ref[...] += gain_grad
    share(step, blocks, grad_ref[...] + grad_values, own_ref, other_ref)


def self_back(ids, gain, ours, theirs, came, kept, grad, w):
    rows, width = grad.shape
    blocks = rows // TB
    part = row_spec(blocks, width // 2, 3)
    return call(
        functools.partial(self_back_kernel, blocks), "self_back", SELF_BACK_MB, blocks,
        [held((3, width)), part, part, other_spec(blocks, width), kept_spec(blocks, width),
         row_spec(blocks, width), held(w.shape)],
        [
            (own_spec(blocks, width), (rows // 2, width), F32),
            (other_spec(blocks, width), (rows // 2, width), BF),
            (held((1, width)), (1, width), F32),
        ],
        [],
        6 * rows * width * width, 20 * rows * width + 6 * width * width,
    )(ids, gain, ours, theirs, came, kept, grad, w)


def flip_bit(values, bit):
    size = lax.axis_size("dp")
    return lax.ppermute(values, "dp", [(i, i ^ (1 << bit)) for i in range(size)])


def flip_mp(values):
    return lax.ppermute(values, "mp", [(0, 1), (1, 0)])


class Steps:
    def send(self, *parts):
        self.sent = [part[0] for part in parts]
        self.bits = [part[1] for part in parts]

    def launch(self):
        self.state = [flip_mp(a) if bit is None else flip_bit(a, bit) for a, bit in zip(self.sent, self.bits)]


def begin(value, *steps):
    value, sent = lax.optimization_barrier((value, [s.sent for s in steps]))
    for step, arrays in zip(steps, sent):
        step.sent = arrays
        step.launch()
    return value


def hold(value, *steps):
    value, states = lax.optimization_barrier((value, [s.state for s in steps]))
    for step, state in zip(steps, states):
        step.state = state
    return value


class Swap(Steps):
    def __init__(self, sent):
        self.send((sent, None))


class Gather(Steps):
    def __init__(self, shard):
        self.shard = shard
        self.low_c = None
        self.send((shard, 3))

    def second(self):
        self.low = jnp.stack([self.shard, self.state[0]])
        self.send((self.low, 2))

    def third(self):
        (self.high,) = self.state
        self.send((self.low, None), (self.high, 1))

    def fourth(self):
        self.low_x, self.high_y = self.state
        self.send((jnp.stack([self.low, self.low_x]), 1), (jnp.stack([self.high, self.high_y]), None))

    def over_cores(self):
        self.low_c = flip_bit(self.low, 0)
        self.high_c = flip_bit(self.high, 0)

    def pieces(self):
        low_y, high_x = self.state
        if self.low_c is None:
            self.over_cores()
        return [
            self.low, self.low_x, low_y, self.high, self.high_y, high_x,
            self.low_c, flip_bit(self.low_x, 0), flip_bit(low_y, 0),
            self.high_c, flip_bit(self.high_y, 0), flip_bit(high_x, 0),
        ]


class WideGather(Steps):
    def __init__(self, proj, out):
        self.shard = jnp.concatenate([proj, out])
        self.send((proj, None), (out, None))

    def split(self):
        both = jnp.stack([self.shard, jnp.concatenate(self.state)])
        cut = both.shape[-1] * 5 // 8
        return WidePart(both[..., :cut], 3), WidePart(both[..., cut:], 1)


class WidePart(Steps):
    def __init__(self, near, bit):
        self.near = near
        self.send((near, bit))

    def flip(self, bit):
        self.near = jnp.stack([self.near, self.state[0]])
        self.send((self.near, bit))

    def pieces(self):
        near = [self.near, self.state[0]]
        return near + [flip_bit(piece, 0) for piece in near]


class Scatter(Steps):
    def __init__(self, keep, send):
        self.keep = keep
        self.send((send, 0))

    def own(self, *at):
        return self.keep[at].astype(F32) + self.came[at].astype(F32)

    def second(self):
        (self.came,) = self.state
        low = self.keep[1, :, 0] + self.came[1, :, 0]
        high = self.keep[:, 1, 1] + self.came[:, 1, 1]
        self.send((low, 1), (high, None))

    def third(self):
        low_y, high_x = self.state
        self.kept = (low_y, high_x)
        self.send(
            ((self.own(0, 1, 0) + low_y[1].astype(F32)).astype(BF), None),
            ((self.own(1, 0, 1) + high_x[1].astype(F32)).astype(BF), 1),
        )

    def fourth(self):
        low_y, high_x = self.kept
        low_x, high_y = self.state
        high = self.own(0, 0, 1) + high_x[0].astype(F32) + high_y.astype(F32)
        self.kept = self.own(0, 0, 0) + low_y[0].astype(F32) + low_x.astype(F32)
        self.send((high.astype(BF), 2))

    def fifth(self):
        self.kept = self.kept + self.state[0].astype(F32)
        self.send((self.kept[1].astype(BF), 3))

    def total(self):
        return self.kept[0] + self.state[0].astype(F32)


class SideScatter(Steps):
    def __init__(self, keep, send):
        self.kept = keep
        self.send((send, 0))

    def take(self):
        self.kept = self.kept.astype(F32) + self.state[0].astype(F32)

    def flip(self, bit, more=None):
        self.take()
        if more is not None:
            self.kept = self.kept + more.astype(F32)
        self.send((self.kept[1].astype(BF), bit))
        self.kept = self.kept[0]

    def across(self):
        self.take()
        self.send((self.kept.astype(BF), None))


def gather_whole(shard):
    n, rows, cols = shard.shape
    dp = lax.axis_size("dp")
    mp = lax.axis_size("mp")
    pieces = lax.all_gather(shard, ("dp", "mp"), axis=0).reshape(dp, mp, n, rows, cols)
    return pieces.transpose(2, 0, 3, 1, 4).reshape(n, dp * rows, mp * cols)


def scatter_whole(grads):
    dp = lax.axis_size("dp")
    mp = lax.axis_size("mp")
    n, rows, cols = grads.shape
    pieces = grads.reshape(n, dp, rows // dp, mp, cols // mp).transpose(1, 3, 0, 2, 4)
    pieces = pieces.reshape((dp * mp,) + pieces.shape[2:])
    return lax.psum_scatter(pieces, ("dp", "mp"), scatter_dimension=0, tiled=True)[0].astype(F32)


class Sum(Steps):
    def __init__(self, values, bit):
        self.values = values
        self.send((values, bit))

    def flip(self, bit):
        self.take()
        self.send((self.values, bit))

    def take(self):
        self.values = self.values + self.state[0]


def other_row(pair_rows, me):
    return lax.dynamic_index_in_dim(pair_rows, 1 - me, 0, False)


def both_halves(own, came, me):
    came = came.astype(F32)
    return jnp.where(me == 0, jnp.stack([own, came]), jnp.stack([came, own]))


def per_device(
    tokens,
    memory,
    doc_lengths,
    mem_lengths,
    norm_gains,
    rel_table,
    self_proj,
    self_out,
    cross_proj,
    cross_out,
    ffn_proj,
    ffn_out,
    cotangent,
):
    me = lax.axis_index("mp")
    dp = lax.axis_size("dp")
    width = tokens.shape[2]
    packed = dp == 1 << BITS and lax.axis_size("mp") == 2
    place = lax.axis_index("dp")
    reverse = sum(((place >> i) & 1) << (BITS - 1 - i) for i in range(BITS))
    ids = jnp.stack([reverse, me, place]).astype(jnp.int32)
    band = bias_band(rel_table)
    pairs = width // LANES
    x_swap = Swap(other_row(tokens, me))
    shard_mid = jnp.concatenate([self_out.T[None], cross_proj, cross_out.T[None]])
    mem_swap = Swap(other_row(memory, me))

    if packed:
        w_one = Gather(self_proj)
        w_ffn = WideGather(ffn_proj, ffn_out.T[None])
        w_one.launch()
        x_swap.launch()
        shard_mid, w_ffn.sent, mem_swap.sent, ids, band, cotangent = hold(
            (shard_mid, w_ffn.sent, mem_swap.sent, ids, band, cotangent), w_one
        )
        w_one.second()
        cot_swap = Swap(other_row(cotangent, me))
        begin((), w_one)
        shard_mid, cot_swap.sent = hold((shard_mid, cot_swap.sent), w_one)
        w_two = Gather(shard_mid)
        w_one.third()
        begin((), w_one, w_two)
        hold((), w_one, x_swap)
        w_one.fourth()
        begin((), w_one)
        w_one.over_cores()
        hold((), w_one, w_two)
        w_self = w_one.pieces()
        w_two.second()
        w_self = begin(w_self, w_two, w_ffn)
    else:
        cot_swap = Swap(other_row(cotangent, me))
        begin((), x_swap, mem_swap, cot_swap)
        w_self = [gather_whole(self_proj)]
        w_mid = [gather_whole(shard_mid)]
        w_ffn = gather_whole(jnp.concatenate([ffn_proj, ffn_out.T[None]]))
        w_ffn = [w_ffn.reshape(3, width, 2, -1).transpose(2, 0, 1, 3)]
    x = (x_swap.state[0], tokens)
    normed_one_t, qkv, w_self = project(packed, ids, norm_gains, *x, w_self)
    if packed:
        qkv = hold(qkv, w_two, w_ffn)
        w_two.third()
        left, right = w_ffn.split()
        qkv = begin(qkv, w_two, left, right, mem_swap)
    parts = ((qkv, 0), (qkv, pairs), (qkv, 2 * pairs))
    self_args = (True, ids, doc_lengths, band)
    if packed:
        mixed = attention_forward(*self_args, *parts, width, 0, pairs // 2)
        mixed = hold(mixed, w_two, left, right)
        w_two.fourth()
        left.flip(2)
        mixed = begin(mixed, w_two, left)
        w_two.over_cores()
        mixed_self, qa_self = attention_forward(*self_args, *parts, width, pairs // 2, pairs, mixed)
        mixed_self = hold(mixed_self, mem_swap, w_two, left)
        w_mid = w_two.pieces()
        left.flip(1)
        right.flip(3)
        mixed_self, w_mid = begin((mixed_self, w_mid), left, right, cot_swap)
    else:
        mixed_self, qa_self = attention_forward(*self_args, *parts, width)
    mem = (mem_swap.state[0], memory)
    resid_two, normed_two_t, mem_t, q_cross, k_cross, v_cross, w_mid = middle(
        packed, ids, norm_gains, *x, mixed_self, *mem, w_mid
    )
    cross_args = (False, ids, mem_lengths, band)
    if packed:
        q_cross = hold(q_cross, right)
        right.flip(2)
        q_cross = begin(q_cross, right)
    parts = ((q_cross, 0), (k_cross, 0), (v_cross, 0))
    if packed:
        mixed = attention_forward(*cross_args, *parts, width, 0, pairs - 1)
        mixed = hold(mixed, left, right, cot_swap)
        w_ffn = left.pieces() + right.pieces()
        mixed_cross, qa_cross = attention_forward(*cross_args, *parts, width, pairs - 1, pairs, mixed)
    else:
        mixed_cross, qa_cross = attention_forward(*cross_args, *parts, width)
    output, output_sent, grad_three, grad_mixed, gain_three, *ffn_grads = feed(
        packed, ids, doc_lengths, norm_gains, resid_two, mixed_cross, cot_swap.state[0], cotangent, w_mid, w_ffn
    )
    out_swap = Swap(output_sent)
    cross_args = cross_args[1:]
    parts = (qa_cross, (k_cross, 0), (v_cross, 0))
    if packed:
        ffn = Scatter(*ffn_grads)
        grad_mixed = begin(grad_mixed, out_swap, ffn)
        grads = cross_backward(*cross_args, *parts, grad_mixed, mixed_cross, 0, 1)
        grads = hold(grads, ffn)
        ffn.second()
        grads, grad_mixed = begin((grads, grad_mixed), ffn)
        grads_cross = cross_backward(*cross_args, *parts, grad_mixed, mixed_cross, 1, pairs, (grads,))
        grads_cross = hold(grads_cross, ffn)
        ffn.third()
        grads_cross = begin(grads_cross, ffn)
    else:
        begin((), out_swap)
        grads_cross = cross_backward(*cross_args, *parts, grad_mixed, mixed_cross, 0, pairs)
    grads_cross = hold(grads_cross, out_swap)
    grad_two, grad_mixed, gmem, gmem_sent, gain_two, *mid_grads = cross_back(
        packed, ids, norm_gains, grads_cross, resid_two, normed_two_t, mem_t, grad_three, mixed_cross, mixed_self, w_mid
    )
    gmem_swap = Swap(gmem_sent)
    parts = (qa_self, (qkv, pairs), (qkv, 2 * pairs))
    more = (mixed_self, normed_one_t)
    if packed:
        mid = Scatter(*mid_grads)
        hold((), ffn)
        ffn.fourth()
        grad_mixed = begin(grad_mixed, mid, gmem_swap, ffn)
        results = self_backward(1, packed, *self_args[1:], *parts, grad_mixed, *more, 0, 1)
        results = hold(results, mid)
        mid.second()
        results, grad_mixed = begin((results, grad_mixed), mid)
        d_theirs, table_theirs, *grads_theirs = self_backward(
            1, packed, *self_args[1:], *parts, grad_mixed, *more, 1, None, results
        )
        d_theirs, grads_theirs, grad_mixed = hold((d_theirs, grads_theirs, grad_mixed), mid, ffn)
        theirs = SideScatter(*grads_theirs)
        theirs.launch()
        mid.third()
        ffn.fifth()
        mid.sent, ffn.sent = hold((mid.sent, ffn.sent), theirs)
        theirs.flip(1)
        grad_mixed = begin(grad_mixed, mid, theirs, ffn)
        d_ours, table_ours, *grads_ours = self_backward(0, packed, *self_args[1:], *parts, grad_mixed, *more)
        d_ours, grads_ours = hold((d_ours, grads_ours), mid, theirs, gmem_swap, ffn)
        ours = SideScatter(*grads_ours)
        ours.launch()
        theirs.across()
        mid.fourth()
        theirs.sent, mid.sent = hold((theirs.sent, mid.sent), ours)
        ours.flip(1)
        d_ours = begin(d_ours, ours, theirs, mid)
    else:
        begin((), gmem_swap)
        d_theirs, table_theirs, *grads_theirs = self_backward(1, packed, *self_args[1:], *parts, grad_mixed, *more)
        d_ours, table_ours, *grads_ours = self_backward(0, packed, *self_args[1:], *parts, grad_mixed, *more)
    grad_x, grad_x_sent, gain_one = self_back(ids, norm_gains, d_ours, d_theirs, *x, grad_two, w_self)
    grad_x_swap = Swap(grad_x_sent)
    half_of = (jnp.arange(pairs, dtype=jnp.int32) >= pairs // 2).astype(jnp.int32)[:, None, None]
    if packed:
        grad_x_swap.sent, gain_one, table_ours, table_theirs = hold(
            (grad_x_swap.sent, gain_one, table_ours, table_theirs), mid, ours, theirs
        )
        ours.flip(2, theirs.state[0])
        mid.fifth()
        gain_one, table_ours, table_theirs = begin(
            (gain_one, table_ours, table_theirs), grad_x_swap, ours, mid
        )
    table = jnp.where(half_of == me, table_ours, table_theirs).reshape(-1, width)
    small = jnp.concatenate([gain_one, gain_two, gain_three, table])
    if packed:
        small = Sum(small, 0)
        small.launch()
        output, out_swap.state, gmem, gmem_swap.state, ffn.state = hold(
            (output, out_swap.state, gmem, gmem_swap.state, ffn.state), small
        )
        output = both_halves(output, out_swap.state[0], me)
        grad_memory = both_halves(gmem, gmem_swap.state[0], me)
        ffn_grads = ffn.total()
        ffn_grads = (ffn_grads[:2], ffn_grads[2].T)
        small.flip(1)
        small.launch()
        output, grad_memory, ffn_grads = hold((output, grad_memory, ffn_grads), ours, small)
        small.flip(2)
        ours.flip(3)
        begin((), small, ours)
        hold((), small, mid)
        small.flip(3)
        small.launch()
        hold((), small, grad_x_swap)
        small.flip(None)
        small.launch()
        mid_grads = mid.total()
        ours.take()
        self_grads = ours.kept
        small.take()
        small = small.values
    else:
        begin((), grad_x_swap)
        output = both_halves(output, out_swap.state[0], me)
        grad_memory = both_halves(gmem, gmem_swap.state[0], me)
        ffn_grads = scatter_whole(ffn_grads[0].transpose(1, 2, 0, 3).reshape(3, width, -1))
        ffn_grads = (ffn_grads[:2], ffn_grads[2].T)
        mid_grads = scatter_whole(mid_grads[0])
        self_grads = scatter_whole(
            jnp.where(
                me == 0,
                jnp.concatenate([grads_ours[0], grads_theirs[0]], axis=2),
                jnp.concatenate([grads_theirs[0], grads_ours[0]], axis=2),
            )
        )
        small = lax.psum(small, ("dp", "mp"))
    table = small[3:].reshape(pairs, -1, LANES)[:, :2, :NB].reshape(2 * pairs, NB).T
    grad_tokens = both_halves(grad_x, grad_x_swap.state[0], me)
    return (
        output,
        grad_tokens,
        grad_memory,
        small[:3],
        table,
        self_grads,
        mid_grads[0].T,
        mid_grads[1:4],
        mid_grads[4].T,
        *ffn_grads,
    )


def solution(mesh):
    rows = P("dp", "mp", None)
    proj = P(None, "dp", "mp")
    out = P("mp", "dp")
    return jax.shard_map(
        per_device,
        mesh=mesh,
        in_specs=(rows, rows, P("dp", None), P("dp"), P(), P(), proj, out, proj, out, proj, out, rows),
        out_specs=(rows, rows, rows, P(), P(), proj, out, proj, out, proj, out),
        check_vma=False,
    )
```

```python
import functools
import jax
import jax.numpy as jnp
import numpy as np
from jax import lax
from jax.experimental import pallas as pl
from jax.experimental.pallas import tpu as pltpu
from jax.sharding import PartitionSpec as P

DH = 64
NB = 32
REACH = 128
ROW = 1024
LANES = 128
QB = 256
masked_score = -1000000000.0
BF = jnp.bfloat16
F32 = jnp.float32
SELF_FORWARD_MB = 20
CROSS_FORWARD_MB = 48
BACKWARD_MB = 48
PROJECT_MB = 20
MIDDLE_MB = 56
FEED_MB = 60
CROSS_BACK_MB = 56
WEIGHTS_MB = 56
SELF_BACK_MB = 56


def params(megabytes):
    return pltpu.CompilerParams(vmem_limit_bytes=megabytes * 1024 * 1024, dimension_semantics=("arbitrary",))


def dot_t(a, b):
    return lax.dot_general(a, b, (((1,), (1,)), ((), ())), preferred_element_type=F32)


def dot_n(a, b):
    return lax.dot_general(a, b, (((1,), (0,)), ((), ())), preferred_element_type=F32)


def dot_tn(a, b):
    return lax.dot_general(a, b, (((0,), (0,)), ((), ())), preferred_element_type=F32)


def split_three(x):
    top = x.astype(BF)
    rest = x - top.astype(F32)
    mid = rest.astype(BF)
    low = (rest - mid.astype(F32)).astype(BF)
    return top.astype(F32), mid.astype(F32), low.astype(F32)


def place_three(x, slot, other):
    top, mid, low = split_three(x)
    return jnp.where(slot == 4, top, jnp.where(slot == 5, mid, jnp.where(slot == 6, low, other)))


def lane_slots(shape):
    lane = lax.broadcasted_iota(jnp.int32, shape, 1)
    return lane, lane % DH


def make_extras(ids_ref, bounds_ref, causal, extra_q, extra_k):
    me = ids_ref[1]
    shape = extra_q.shape
    _, slot = lane_slots(shape)
    rows = lax.broadcasted_iota(jnp.int32, shape, 0)
    if causal:
        first = bounds_ref[me, 0]
        second = first + bounds_ref[me, 1]
        third = second + bounds_ref[me, 2]
        seg = (
            (rows >= first).astype(jnp.int32)
            + (rows >= second).astype(jnp.int32)
            + (rows >= third).astype(jnp.int32)
        )
        own = jnp.where(slot == seg, 1.0, 0.0)
        barred = jnp.where((slot < 4) & (slot != seg), masked_score, 0.0)
    else:
        own = jnp.where(slot == 0, 1.0, 0.0)
        barred = jnp.where((slot == 0) & (rows >= bounds_ref[me]), masked_score, 0.0)
    extra_q[...] = jnp.where(slot == 7, 1.0, own).astype(BF)
    extra_k[...] = jnp.where((slot >= 4) & (slot <= 6), 1.0, barred).astype(BF)


def band_square(band_ref, head):
    wide = jnp.broadcast_to(band_ref[head : head + 1, :], (LANES, 3 * LANES))
    rolled = pltpu.roll(wide, 0, 1, stride=1, stride_axis=0)
    return rolled[:, LANES : 2 * LANES], rolled[:, :LANES]


def add_band(scores, first, near, side):
    above = jnp.full((LANES, LANES), masked_score, F32)
    corner = jnp.concatenate([side, jnp.zeros((LANES, LANES), F32)], axis=0)
    left = jnp.concatenate([near, side], axis=0)
    right = jnp.concatenate([above, near], axis=0)
    pieces = []
    if first > 0:
        pieces.append(scores[:, : first - LANES])
        pieces.append(scores[:, first - LANES : first] + corner)
    pieces.append(scores[:, first : first + LANES] + left)
    pieces.append(scores[:, first + LANES :] + right)
    return jnp.concatenate(pieces, axis=1)


def forward_kernel(causal, extra, ids_ref, bounds_ref, band_ref, q_ref, k_ref, v_ref, *rest):
    o_ref, qa_ref, extra_q, extra_k = rest[extra:]
    length = q_ref.shape[0]

    @pl.when(pl.program_id(0) == 0)
    def _():
        make_extras(ids_ref, bounds_ref, causal, extra_q, extra_k)

    lane, slot = lane_slots((QB, LANES))
    full_lane, full_slot = lane_slots((length, LANES))
    ones = jnp.where(full_slot == 0, 1.0, 0.0).astype(BF)
    keys, values, bands = [], [], []
    for head in range(2):
        mine = (full_lane < DH) == (head == 0)
        keys.append(jnp.where(mine, k_ref[...], extra_k[...]))
        values.append(jnp.where(mine, v_ref[...], ones))
        if causal:
            bands.append(band_square(band_ref, head))

    def scores_of(block, head):
        first = block * QB
        count = first + QB if causal else length
        mine_block = (lane < DH) == (head == 0)
        queries = jnp.where(mine_block, q_ref[first : first + QB, :], extra_q[first : first + QB, :])
        return queries, dot_t(queries, keys[head][:count])

    todo = [(block, head) for block in range(length // QB) for head in range(2)]
    ahead = [scores_of(*item) for item in todo[:2]]
    for at, (block, head) in enumerate(todo):
        first = block * QB
        span = slice(first, first + QB)
        queries, scores = ahead.pop(0)
        if at + 2 < len(todo):
            ahead.append(scores_of(*todo[at + 2]))
        if causal:
            scores = add_band(scores, first, *bands[head])
        top = jnp.max(scores, axis=1, keepdims=True)
        weights = jnp.exp(scores - top).astype(BF)
        mixed = dot_n(weights, values[head][: weights.shape[1]])
        spare_column = DH if head == 0 else 0
        total = mixed[:, spare_column : spare_column + 1]
        mixed = mixed * (1.0 / total)
        if head == 0:
            kept = mixed
        else:
            o_ref[span, :] = jnp.where(lane < DH, kept, mixed).astype(BF)
        spare = place_three(-(top + jnp.log(total)), slot, queries.astype(F32))
        qa_ref[head, span, :] = jnp.where((lane < DH) == (head == 0), queries, spare.astype(BF))


def backward_kernel(causal, packed, extra, ids_ref, bounds_ref, band_ref, qa_ref, k_ref, v_ref, g_ref, o_ref, *rest):
    if causal:
        rest = rest[:2] + rest[2 + extra :]
        near_ref, left, grad_ref, bias_ref = rest[:4]
        wgrads = rest[4:-6]
        extra_q, extra_k, dk_acc, dv_acc, near_acc, side_acc = rest[-6:]
    else:
        grad_ref, extra_q, extra_k, dk_acc, dv_acc = rest[-5:]
    length = k_ref.shape[0]

    @pl.when(pl.program_id(0) == 0)
    def _():
        make_extras(ids_ref, bounds_ref, causal, extra_q, extra_k)

    lane, slot = lane_slots((QB, LANES))
    full_lane, full_slot = lane_slots((length, LANES))
    spare_v = jnp.where((full_slot >= 4) & (full_slot <= 6), 1.0, 0.0).astype(BF)
    squares, wholes = [], []
    for head in range(2):
        mine = (full_lane < DH) == (head == 0)
        mine_block = (lane < DH) == (head == 0)
        keys = jnp.where(mine, k_ref[...], extra_k[...])
        values = jnp.where(mine, v_ref[...], spare_v)
        if causal:
            near, side = band_square(band_ref, head)
            near_acc[...] = jnp.zeros_like(near_acc)
            side_acc[...] = jnp.zeros_like(side_acc)
        dk_acc[head] = jnp.zeros(dk_acc.shape[1:], F32)
        dv_acc[head] = jnp.zeros(dv_acc.shape[1:], F32)
        for block in range(length // QB):
            first = block * QB
            count = first + QB if causal else length
            span = slice(first, first + QB)
            queries = qa_ref[head, span, :]
            upstream = g_ref[span, :]
            inner = jnp.sum(
                jnp.where(mine_block, upstream.astype(F32) * o_ref[span, :].astype(F32), 0.0), axis=1, keepdims=True
            )
            spare = place_three(-inner, slot, jnp.zeros((QB, LANES), F32))
            grads = jnp.where(mine_block, upstream, spare.astype(BF))
            scores = dot_t(queries, keys[:count])
            if causal:
                scores = add_band(scores, first, near, side)
            probs = jnp.exp(scores)
            lifted = dot_t(grads, values[:count])
            score_grads = (probs * lifted).astype(BF)
            dv_acc[head, :, :count] += dot_n(grads.T, probs.astype(BF))
            dk_acc[head, :, :count] += dot_n(queries.T, score_grads)
            dq = dot_n(score_grads, keys[:count]).astype(BF)
            if causal:
                near_acc[...] += score_grads[:LANES, first : first + LANES].astype(F32)
                near_acc[...] += score_grads[LANES:, first + LANES :].astype(F32)
                side_acc[...] += score_grads[LANES:, first : first + LANES].astype(F32)
                if block > 0:
                    side_acc[...] += score_grads[:LANES, first - LANES : first].astype(F32)
            if head == 0:
                grad_ref[0, span, :] = dq
            else:
                grad_ref[0, span, :] = jnp.where(lane < DH, grad_ref[0, span, :], dq)
        if causal:
            squares.append(jnp.concatenate([side_acc[...], near_acc[...]], axis=1))
            ones_row = DH + 7 if head == 0 else 7
            wholes.append(jnp.sum(dk_acc[head, ones_row : ones_row + 1, :], axis=1, keepdims=True))
    upper = lax.broadcasted_iota(jnp.int32, (LANES, length), 0) < DH
    grad_ref[1] = jnp.where(upper, dk_acc[0], dk_acc[1]).astype(BF).T
    grad_ref[2] = jnp.where(upper, dv_acc[0], dv_acc[1]).astype(BF).T
    if causal:
        wide = jnp.concatenate([jnp.stack(squares), jnp.zeros((2, LANES, LANES), F32)], axis=2)
        half = LANES // 2
        while half:
            wide = wide[:, :half] + pltpu.roll(wide[:, half:], 3 * LANES - half, 2)
            half //= 2
        diag = jnp.concatenate([wide[0], wide[1], jnp.zeros((6, 3 * LANES), F32)], axis=0)[:, : 2 * LANES]
        table = lax.dot_general(
            diag, near_ref[...], (((1,), (0,)), ((), ())),
            precision=lax.Precision.HIGHEST, preferred_element_type=F32,
        )
        whole = jnp.concatenate(wholes + [jnp.zeros((6, 1), F32)], axis=0)
        last = whole - jnp.sum(table, axis=1, keepdims=True)
        at_last = lax.broadcasted_iota(jnp.int32, table.shape, 1) == NB - 1
        bias_ref[0] = jnp.where(at_last, last, table)
    if causal:
        right = jnp.concatenate([grad_ref[n] for n in range(3)], axis=1)
        grads = dot_n(left[...], right).astype(BF)
        middle_row = grads.shape[0] // 2
        for n in range(3):
            part = grads[:, n * LANES : (n + 1) * LANES]
            if packed:
                shape = wgrads[0].shape[:3] + wgrads[0].shape[4:]
                wgrads[0][:, :, :, n] = part[:middle_row].reshape(shape)
                wgrads[1][:, :, :, n] = part[middle_row:].reshape(shape)
            else:
                wgrads[0][n] = part


def attention_forward(causal, ids, bounds, band, q, k, v, cols, start=0, stop=None, into=()):
    rows = q[0].shape[0]
    pairs = (cols // LANES if stop is None else stop) - start

    def spec(offset):
        return pl.BlockSpec((rows, LANES), lambda p, ids: (0, p + offset + start))

    n = rows * rows * pairs * 2
    return call(
        functools.partial(forward_kernel, causal, len(into)), "attention_forward", SELF_FORWARD_MB if causal else CROSS_FORWARD_MB, pairs,
        [
            pl.BlockSpec(memory_space=pltpu.SMEM),
            pl.BlockSpec((None, 2, 3 * LANES), lambda p, ids: (p + start, 0, 0)),
            spec(q[1]), spec(k[1]), spec(v[1]),
        ] + [anywhere()] * len(into),
        [
            (spec(0), (rows, cols), BF),
            (pl.BlockSpec((2, rows, LANES), lambda p, ids: (p + start, 0, 0)), (2 * cols // LANES, rows, LANES), BF),
        ],
        [pltpu.VMEM((rows, LANES), BF)] * 2,
        n * 256 * 4 // (2 if causal else 1), rows * cols * 16,
        {6: 0, 7: 1} if into else {},
    )(ids, bounds, band, q[0], k[0], v[0], *into)


def cross_backward(ids, bounds, band, qa, k, v, g, o, start, stop, into=()):
    rows, cols = g.shape

    def spec(offset):
        return pl.BlockSpec((rows, LANES), lambda p, ids: (0, p + start + offset))

    n = rows * rows * (stop - start) * 2
    return call(
        functools.partial(backward_kernel, False, False, 0), "cross_backward", BACKWARD_MB, stop - start,
        [
            pl.BlockSpec(memory_space=pltpu.SMEM),
            pl.BlockSpec((None, 2, 3 * LANES), lambda p, ids: (p + start, 0, 0)),
            pl.BlockSpec((2, rows, LANES), lambda p, ids: (p + start, 0, 0)),
            spec(k[1]), spec(v[1]), spec(0), spec(0),
        ] + [anywhere()] * len(into),
        [(pl.BlockSpec((3, rows, LANES), lambda p, ids: (0, 0, p + start)), (3, rows, cols), BF)],
        [pltpu.VMEM((rows, LANES), BF)] * 2 + [pltpu.VMEM((2, LANES, rows), F32)] * 2,
        n * 256 * 10, rows * cols * 20,
        {8: 0} if into else {},
    )(ids, bounds, band, qa, k[0], v[0], g, o, *into)[0]


def self_backward(side, packed, ids, bounds, band, qa, k, v, g, o, normed_t, start=0, stop=None, into=()):
    rows, cols = g.shape
    pairs = cols // LANES // 2
    stop = pairs if stop is None else stop
    depth = normed_t.shape[0] >> BITS

    def at(p, ids):
        return p + start + pairs * jnp.bitwise_xor(ids[1], side)

    def spec(offset):
        return pl.BlockSpec((rows, LANES), lambda p, ids: (0, at(p, ids) + offset))

    n = rows * rows * (stop - start) * 2
    if packed:
        block = pl.BlockSpec((2, 2, 2, 3, depth, LANES), lambda p, ids: (0, 0, 0, 0, 0, p + start))
        wgrads = [(block, (2, 2, 2, 3, depth, cols // 2), BF)] * 2
    else:
        block = pl.BlockSpec((3, normed_t.shape[0], LANES), lambda p, ids: (0, 0, p + start))
        wgrads = [(block, (3, normed_t.shape[0], cols // 2), BF)]
    return call(
        functools.partial(backward_kernel, True, packed, len(into)), "self_backward", BACKWARD_MB, stop - start,
        [
            pl.BlockSpec(memory_space=pltpu.SMEM),
            pl.BlockSpec((None, 2, 3 * LANES), lambda p, ids: (at(p, ids), 0, 0)),
            pl.BlockSpec((2, rows, LANES), lambda p, ids: (at(p, ids), 0, 0)),
            spec(k[1]), spec(v[1]), spec(0), spec(0),
            held((2 * LANES, LANES)), held(normed_t.shape),
        ] + [anywhere()] * len(into),
        [
            (pl.BlockSpec((3, rows, LANES), lambda p, ids: (0, 0, p + start)), (3, rows, cols // 2), BF),
            (pl.BlockSpec((1, 8, LANES), lambda p, ids: (at(p, ids), 0, 0)), (2 * pairs, 8, LANES), F32),
        ] + wgrads,
        [pltpu.VMEM((rows, LANES), BF)] * 2 + [pltpu.VMEM((2, LANES, rows), F32)] * 2
        + [pltpu.VMEM((LANES, LANES), F32)] * 2,
        n * 256 * 8, rows * cols * 20,
        {10 + i: i for i in range(len(into))},
    )(ids, bounds, band, qa, k[0], v[0], g, o, jnp.asarray(near_buckets()), normed_t, *into)


def near_buckets():
    buckets = bucket_table(LANES, NB, REACH)
    table = np.zeros((2 * LANES, LANES), np.float32)
    for distance in range(LANES):
        if buckets[distance] < NB - 1:
            table[LANES - distance, buckets[distance]] = 1.0
    return table


def bucket_table(length, buckets, reach):
    offsets = np.arange(length)
    exact_part = buckets // 2
    scaled = np.log(np.maximum(offsets, 1) / exact_part) / np.log(reach / exact_part) * (buckets - exact_part)
    far_bucket = np.minimum(exact_part + np.floor(scaled).astype(np.int64), buckets - 1)
    return np.where(offsets < exact_part, offsets, far_bucket).astype(np.int32)


def bias_band(rel_table):
    distance = LANES - np.arange(3 * LANES)
    buckets = bucket_table(LANES + 1, NB, REACH)
    onehot = np.zeros((3 * LANES, NB), np.float32)
    shift = np.zeros((3 * LANES,), np.float32)
    for at, far in enumerate(distance):
        if 0 <= far < LANES:
            onehot[at, buckets[far]] = 1.0
        elif -LANES < far < 0:
            shift[at] = masked_score
    relative = rel_table - rel_table[NB - 1 :]
    band = jnp.dot(jnp.asarray(onehot), relative, precision=lax.Precision.HIGHEST) + shift[:, None]
    return band.T.reshape(-1, 2, 3 * LANES)


epsilon = 1e-06
TB = 256
BITS = 4


def rms(values, gain):
    inverse = lax.rsqrt(jnp.mean(values * values, axis=-1, keepdims=True) + epsilon)
    return (values * inverse * gain).astype(BF), inverse


def rms_back(values, inverse, gain, upstream):
    weighted = upstream * gain
    inner_mean = jnp.mean(weighted * values, axis=-1, keepdims=True)
    grad_values = inverse * weighted - values * (inverse * inverse * inverse * inner_mean)
    return grad_values, jnp.sum(upstream * values * inverse, axis=0, keepdims=True)


def cost(flops, moved):
    return pl.CostEstimate(flops=flops, bytes_accessed=moved, transcendentals=0)


def turn(s, ids, blocks):
    return ((1 - ids[1]) * (blocks // 2) + jnp.minimum(s, blocks - 1)) % blocks


def row_span(s, ids, blocks):
    return pl.ds(pl.multiple_of(turn(s, ids, blocks) * TB, TB), TB)


def row_spec(blocks, width, *lead):
    zeros = (0,) * len(lead)
    return pl.BlockSpec(lead + (TB, width), lambda s, ids: zeros + (turn(s, ids, blocks), 0))


def kept_spec(blocks, width):
    half = blocks // 2
    return pl.BlockSpec((None, TB, width), lambda s, ids: (ids[1], jnp.clip(s - half, 0, half - 1), 0))


def own_spec(blocks, width):
    half = blocks // 2
    return pl.BlockSpec((TB, width), lambda s, ids: (jnp.clip(s - half, 0, half - 1), 0))


def other_spec(blocks, width):
    return pl.BlockSpec((TB, width), lambda s, ids: (jnp.minimum(s, blocks // 2 - 1), 0))


def held(shape):
    zeros = (0,) * len(shape)
    return pl.BlockSpec(shape, lambda s, ids: zeros, pipeline_mode=pl.Buffered(1))


def anywhere():
    return pl.BlockSpec(memory_space=pl.ANY)


def call(kernel, name, megabytes, grid, in_specs, outs, scratch, flops, moved, aliases=None):
    return pl.pallas_call(
        kernel,
        grid_spec=pltpu.PrefetchScalarGridSpec(
            num_scalar_prefetch=1,
            grid=(grid,),
            in_specs=in_specs,
            out_specs=[o[0] for o in outs],
            scratch_shapes=scratch,
        ),
        out_shape=[jax.ShapeDtypeStruct(o[1], o[2]) for o in outs],
        input_output_aliases=aliases or {},
        compiler_params=params(megabytes),
        cost_estimate=cost(flops, moved),
        name=name,
    )


def chosen(step, blocks, came_ref, kept_ref):
    return jnp.where(step < blocks // 2, came_ref[...], kept_ref[...])


def share(step, blocks, values, own_ref, other_ref):
    @pl.when(step < blocks // 2)
    def _():
        other_ref[...] = values.astype(BF)

    @pl.when(step >= blocks // 2)
    def _():
        own_ref[...] = values


def gather_table():
    near = [((0, 0, 0),), ((0, 1, 0),), ((1, 0, 0), (1, 1, 0)), ((0, 0, 1),), ((1, 0, 1),), ((0, 1, 1), (1, 1, 1))]
    table = []
    for c in range(2):
        for places in near:
            entries = []
            for at, (y, x, z0) in enumerate(places):
                for z1 in range(2):
                    entries.append(((at, z1) if len(places) > 1 else (z1,), (y, x, z0, z1, c), 0))
            table.append(entries)
    return table


def wide_table():
    pairs = [(a, b) for a in range(2) for b in range(2)]
    table = []
    for c in range(2):
        for y in range(2):
            table.append([((z0, z1, x), (y, x, z0, z1, c), 0) for x in range(2) for z0, z1 in pairs])
    for c in range(2):
        for z0 in range(2):
            table.append([((z1, y, x), (y, x, z0, z1, c), 1) for x in range(2) for z1, y in pairs])
    return table


def copy_pieces(ids_ref, pieces, table, place, w_ref, sem):
    if len(pieces) == 1:
        for x in range(sem.shape[0]):
            part = pieces[0].at[x] if sem.shape[0] > 1 else pieces[0]
            target = w_ref.at[x] if sem.shape[0] > 1 else w_ref
            pltpu.make_async_copy(part, target, sem.at[x]).start()
        return
    mine = ids_ref[2]
    rows = pieces[0].shape[-2]

    def copy(flip):
        for first in range(2):
            for piece, entries in zip(pieces, table):
                for at, (y, x, z0, z1, c), part in entries:
                    if x ^ flip != first:
                        continue
                    block = jnp.bitwise_xor(mine, 8 * z1 + 4 * z0 + 2 * y + c)
                    span = pl.ds(pl.multiple_of(block * rows, 16), rows)
                    target, done = place(span, x ^ flip, part)
                    pltpu.make_async_copy(piece.at[at], target, done).start()

    @pl.when(ids_ref[1] == 0)
    def _():
        copy(0)

    @pl.when(ids_ref[1] == 1)
    def _():
        copy(1)


def wait_pieces(w_ref, sem):
    pltpu.make_async_copy(w_ref, w_ref, sem).wait()


def natural_place(w_ref, cols, sem):
    return lambda span, x, part: (w_ref.at[:, span, x * cols : (x + 1) * cols], sem.at[0])


def put_turned(packed, ids_ref, target, span, values):
    turned = values.T
    if not packed:
        target[:, span] = turned
        return
    depth = turned.shape[0] >> BITS
    for block in range(1 << BITS):
        reverse = int(format(block, "04b")[::-1], 2)
        at = jnp.bitwise_xor(ids_ref[0], reverse) * depth
        target[pl.ds(pl.multiple_of(at, 16), depth), span] = turned[block * depth : (block + 1) * depth]


def put_grads(packed, ids_ref, grads, outs):
    if not packed:
        outs[0][...] = grads
        return
    keep_ref, send_ref = outs
    rows, cols = keep_ref.shape[-2:]
    middle = grads.shape[0] // 2

    def store(flip):
        for x in range(2):
            first = cols * (x ^ flip)
            for target, part in ((keep_ref, grads[:middle]), (send_ref, grads[middle:])):
                target[:, x] = part[:, first : first + cols].reshape(2, 2, 2, rows, cols)

    @pl.when(ids_ref[1] == 0)
    def _():
        store(0)

    @pl.when(ids_ref[1] == 1)
    def _():
        store(1)


def grads_out(packed, n, width, first):
    def at(s):
        return jnp.maximum(s - first, 0)

    if not packed:
        return [(pl.BlockSpec((None, width, width), lambda s, ids: (at(s), 0, 0)), (n, width, width), BF)]
    rows, cols = width >> BITS, width // 2
    block = pl.BlockSpec((2, 2, 2, 2, None, rows, cols), lambda s, ids: (0, 0, 0, 0, at(s), 0, 0))
    return [(block, (2, 2, 2, 2, n, rows, cols), BF)] * 2


def project_kernel(blocks, pieces, packed, ids_ref, gain_ref, came_ref, kept_ref, *refs):
    w_in = refs[:pieces]
    turned_ref, out_ref, w_ref, sem = refs[pieces:]
    step = pl.program_id(0)

    @pl.when(step == 0)
    def _():
        copy_pieces(ids_ref, w_in, gather_table(), natural_place(w_ref, w_in[0].shape[-1], sem), w_ref, sem)
        wait_pieces(w_ref, sem.at[0])

    normed, _ = rms(chosen(step, blocks, came_ref, kept_ref).astype(F32), gain_ref[0:1, :])
    put_turned(packed, ids_ref, turned_ref, row_span(step, ids_ref, blocks), normed)
    width = normed.shape[1]
    for s in range(3):
        out_ref[:, s * width : (s + 1) * width] = dot_n(normed, w_ref[s]).astype(BF)


def project(packed, ids, gain, came, kept, pieces):
    _, half, width = kept.shape
    rows = 2 * half
    blocks = rows // TB
    full = (3, width, width)
    return call(
        functools.partial(project_kernel, blocks, len(pieces), packed), "project", PROJECT_MB, blocks,
        [held((3, width)), other_spec(blocks, width), kept_spec(blocks, width)] + [anywhere()] * len(pieces),
        [
            (held((width, rows)), (width, rows), BF),
            (row_spec(blocks, 3 * width), (rows, 3 * width), BF),
            (held(full), full, BF),
        ],
        [pltpu.SemaphoreType.DMA((1,))],
        6 * rows * width * width, 10 * rows * width + 6 * width * width,
    )(ids, gain, came, kept, *pieces)


def middle_kernel(blocks, pieces, packed, ids_ref, gain_ref, came_ref, kept_ref, mixed_ref, mem_came_ref, mem_kept_ref, *refs):
    w_in = refs[:pieces]
    resid_ref, turned_ref, mem_turned_ref, q_ref, k_ref, v_ref, w_ref, sem = refs[pieces:]
    step = pl.program_id(0)

    @pl.when(step == 0)
    def _():
        copy_pieces(ids_ref, w_in, gather_table(), natural_place(w_ref, w_in[0].shape[-1], sem), w_ref, sem)
        wait_pieces(w_ref, sem.at[0])

    resid = chosen(step, blocks, came_ref, kept_ref).astype(F32) + dot_t(mixed_ref[...], w_ref[0])
    resid_ref[...] = resid
    normed, _ = rms(resid, gain_ref[1:2, :])
    span = row_span(step, ids_ref, blocks)
    put_turned(packed, ids_ref, turned_ref, span, normed)
    q_ref[...] = dot_n(normed, w_ref[1]).astype(BF)
    memory = chosen(step, blocks, mem_came_ref, mem_kept_ref)
    put_turned(packed, ids_ref, mem_turned_ref, span, memory)
    k_ref[...] = dot_n(memory, w_ref[2]).astype(BF)
    v_ref[...] = dot_n(memory, w_ref[3]).astype(BF)


def middle(packed, ids, gain, came, kept, mixed, mem_came, mem_kept, pieces):
    rows, width = mixed.shape
    blocks = rows // TB
    full = (5, width, width)
    spec = row_spec(blocks, width)
    pair = [other_spec(blocks, width), kept_spec(blocks, width)]
    return call(
        functools.partial(middle_kernel, blocks, len(pieces), packed), "middle", MIDDLE_MB, blocks,
        [held((3, width))] + pair + [spec] + pair + [anywhere()] * len(pieces),
        [(spec, (rows, width), F32)] + [(held((width, rows)), (width, rows), BF)] * 2
        + [(spec, (rows, width), BF)] * 3 + [(held(full), full, BF)],
        [pltpu.SemaphoreType.DMA((1,))],
        8 * rows * width * width, 20 * rows * width + 10 * width * width,
    )(ids, gain, came, kept, mixed, mem_came, mem_kept, *pieces)


def feed_kernel(blocks, pieces, packed, ids_ref, docs_ref, gain_ref, resid_ref, mixed_ref, cot_came_ref, cot_kept_ref,
                wo_ref, *refs):
    w_in = refs[:pieces]
    refs = refs[pieces:]
    own_ref, other_ref, grad_ref, gmix_ref, gain_grad_ref = refs[:5]
    wgrads = refs[5:-7]
    w_ref, normed_t, branch_t, hidden_s, gate_s, up_s, sem = refs[-7:]
    step = pl.program_id(0)
    me = ids_ref[1]
    width = resid_ref.shape[1]

    def weight(which, x):
        return w_ref[x, which]

    @pl.when(step == 0)
    def _():
        cols = w_in[0].shape[-1]
        copy_pieces(
            ids_ref, w_in, wide_table(),
            lambda span, x, part: (w_ref.at[x, :, span, cols * part : cols if part == 0 else None], sem.at[x]), w_ref, sem,
        )
        gain_grad_ref[...] = jnp.zeros_like(gain_grad_ref)

    @pl.when(step < blocks)
    def _():
        first = pl.multiple_of(turn(step, ids_ref, blocks) * TB, TB)
        span = pl.ds(first, TB)
        resid = resid_ref[...] + dot_t(mixed_ref[...], wo_ref[...])
        normed, inverse = rms(resid, gain_ref[2:3, :])
        slots = first + lax.broadcasted_iota(jnp.int32, (TB, 1), 0)
        padding = slots >= docs_ref[me, 0] + docs_ref[me, 1] + docs_ref[me, 2]
        grad_four = jnp.where(padding, 0.0, chosen(step, blocks, cot_came_ref, cot_kept_ref).astype(F32))
        branch = grad_four.astype(BF)
        put_turned(packed, ids_ref, normed_t, span, normed)
        put_turned(packed, ids_ref, branch_t, span, branch)
        total = resid
        upstream = jnp.zeros((TB, width), F32)
        for x in range(2):

            @pl.when(step == 0)
            def _():
                wait_pieces(w_ref.at[x], sem.at[x])

            gate = dot_n(normed, weight(0, x))
            up = dot_n(normed, weight(1, x))
            lifted = dot_n(branch, weight(2, x))
            square = gate * gate
            inner = jnp.tanh(gate * (0.7978845608028654 + 0.035677408136300125 * square))
            half_up = 0.5 + 0.5 * inner
            activated = gate * half_up
            slope = half_up + (0.5 * gate) * (1.0 - inner * inner) * (
                0.7978845608028654 + 0.10703222440890037 * square
            )
            hidden = (activated * up).astype(BF)
            gate_grad = (lifted * up * slope).astype(BF)
            up_grad = (lifted * activated).astype(BF)
            hidden_s[x, span, :] = hidden
            gate_s[x, span, :] = gate_grad
            up_s[x, span, :] = up_grad
            total = total + dot_t(hidden, weight(2, x))
            upstream = upstream + dot_t(gate_grad, weight(0, x)) + dot_t(up_grad, weight(1, x))
        share(step, blocks, jnp.where(padding, 0.0, total), own_ref, other_ref)
        grad_resid, gain_grad = rms_back(resid, inverse, gain_ref[2:3, :], upstream)
        grad = grad_four + grad_resid
        grad_ref[...] = grad
        gain_grad_ref[...] += gain_grad
        gmix_ref[...] = dot_n(grad.astype(BF), wo_ref[...]).astype(BF)

    for which, (left, right) in enumerate(((normed_t, gate_s), (normed_t, up_s), (branch_t, hidden_s))):
        for x in range(2):

            @pl.when(step == blocks + 2 * which + x)
            def _():
                if packed:
                    grads = dot_n(left[...], right[jnp.bitwise_xor(x, me)]).astype(BF)
                    middle_row = grads.shape[0] // 2
                    wgrads[0][...] = grads[:middle_row].reshape(wgrads[0].shape)
                    wgrads[1][...] = grads[middle_row:].reshape(wgrads[1].shape)
                else:
                    wgrads[0][...] = dot_n(left[...], right[x]).astype(BF)


def feed(packed, ids, docs, gain, resid, mixed, cot_came, cot_kept, w_mid, pieces):
    rows, width = resid.shape
    half = pieces[0].shape[-1] if len(pieces) == 1 else pieces[0].shape[-1] + pieces[-1].shape[-1]
    blocks = rows // TB
    spec = row_spec(blocks, width)

    def at(s):
        late = jnp.maximum(s - blocks, 0)
        return late // 2, late % 2

    if packed:
        depth = width >> BITS
        block = pl.BlockSpec((2, None, 2, 2, None, depth, half), lambda s, ids: (0, at(s)[1], 0, 0, at(s)[0], 0, 0))
        wgrads = [(block, (2, 2, 2, 2, 3, depth, half), BF)] * 2
    else:
        block = pl.BlockSpec((None, None, width, half), lambda s, ids: (at(s)[1], at(s)[0], 0, 0))
        wgrads = [(block, (2, 3, width, half), BF)]
    return call(
        functools.partial(feed_kernel, blocks, len(pieces), packed), "feed", FEED_MB, blocks + 6,
        [pl.BlockSpec(memory_space=pltpu.SMEM), held((3, width)), spec, spec, other_spec(blocks, width),
         kept_spec(blocks, width),
         pl.BlockSpec((None, width, width), lambda s, ids: (4, 0, 0), pipeline_mode=pl.Buffered(1))]
        + [anywhere()] * len(pieces),
        [
            (own_spec(blocks, width), (rows // 2, width), F32),
            (other_spec(blocks, width), (rows // 2, width), BF),
            (spec, (rows, width), F32),
            (spec, (rows, width), BF),
            (held((1, width)), (1, width), F32),
        ] + wgrads,
        [pltpu.VMEM((2, 3, width, half), BF)] + [pltpu.VMEM((width, rows), BF)] * 2
        + [pltpu.VMEM((2, rows, half), BF)] * 3 + [pltpu.SemaphoreType.DMA((2,))],
        36 * rows * width * half, 24 * rows * width + 24 * width * half,
    )(ids, docs, gain, resid, mixed, cot_came, cot_kept, w_mid, *pieces)


def cross_back_kernel(blocks, packed, ids_ref, gain_ref, d_ref, resid_ref, normed_t, mem_t, grad_ref,
                       mixed_cross_ref, mixed_self_ref, w_ref, *outs):
    grad_two_ref, gmix_ref, gmem_own_ref, gmem_other_ref, gain_grad_ref = outs[:5]
    wgrads = outs[5:-2]
    lefts, rights = outs[-2:]
    step = pl.program_id(0)

    @pl.when(step == 0)
    def _():
        gain_grad_ref[...] = jnp.zeros_like(gain_grad_ref)

    @pl.when(step < blocks)
    def _():
        span = pl.ds(pl.multiple_of(turn(step, ids_ref, blocks) * TB, TB), TB)
        resid = resid_ref[...]
        inverse = lax.rsqrt(jnp.mean(resid * resid, axis=-1, keepdims=True) + epsilon)
        grad_resid, gain_grad = rms_back(resid, inverse, gain_ref[1:2, :], dot_t(d_ref[0], w_ref[1]))
        gain_grad_ref[...] += gain_grad
        grad_three = grad_ref[...]
        grad_two = grad_three + grad_resid
        grad_two_ref[...] = grad_two
        branch = grad_two.astype(BF)
        gmix_ref[...] = dot_n(branch, w_ref[0]).astype(BF)
        gmem = dot_t(d_ref[1], w_ref[2]) + dot_t(d_ref[2], w_ref[3])
        share(step, blocks, gmem, gmem_own_ref, gmem_other_ref)
        put_turned(packed, ids_ref, lefts.at[0], span, branch)
        put_turned(packed, ids_ref, lefts.at[1], span, grad_three.astype(BF))
        rights[0, span, :] = mixed_self_ref[...]
        rights[1, span, :] = d_ref[0]
        rights[2, span, :] = d_ref[1]
        rights[3, span, :] = d_ref[2]
        rights[4, span, :] = mixed_cross_ref[...]

    for n, left in enumerate((lefts.at[0], normed_t, mem_t, mem_t, lefts.at[1])):

        @pl.when(step == blocks + n)
        def _():
            put_grads(packed, ids_ref, dot_n(left[...], rights[n]).astype(BF), wgrads)


def cross_back(packed, ids, gain, d, resid, normed_t, mem_t, grad, mixed_cross, mixed_self, w):
    rows, width = resid.shape
    blocks = rows // TB
    spec = row_spec(blocks, width)
    return call(
        functools.partial(cross_back_kernel, blocks, packed), "cross_back", CROSS_BACK_MB, blocks + 5,
        [held((3, width)), row_spec(blocks, width, 3), spec, held((width, rows)), held((width, rows)),
         spec, spec, spec, held(w.shape)],
        [
            (spec, (rows, width), F32),
            (spec, (rows, width), BF),
            (own_spec(blocks, width), (rows // 2, width), F32),
            (other_spec(blocks, width), (rows // 2, width), BF),
            (held((1, width)), (1, width), F32),
        ] + grads_out(packed, 5, width, blocks),
        [pltpu.VMEM((2, width, rows), BF), pltpu.VMEM((5, rows, width), BF)],
        18 * rows * width * width, 36 * rows * width + 20 * width * width,
    )(ids, gain, d, resid, normed_t, mem_t, grad, mixed_cross, mixed_self, w)


def self_back_kernel(blocks, ids_ref, gain_ref, ours_ref, theirs_ref, came_ref, kept_ref, grad_ref, w_ref,
                     own_ref, other_ref, gain_grad_ref):
    step = pl.program_id(0)

    @pl.when(step == 0)
    def _():
        gain_grad_ref[...] = jnp.zeros_like(gain_grad_ref)

    values = chosen(step, blocks, came_ref, kept_ref).astype(F32)
    inverse = lax.rsqrt(jnp.mean(values * values, axis=-1, keepdims=True) + epsilon)
    upstream = jnp.zeros(values.shape, F32)
    for n in range(3):
        ours, theirs = ours_ref[n], theirs_ref[n]
        first = jnp.where(ids_ref[1] == 0, ours, theirs)
        second = jnp.where(ids_ref[1] == 0, theirs, ours)
        upstream = upstream + dot_t(jnp.concatenate([first, second], axis=1), w_ref[n])
    grad_values, gain_grad = rms_back(values, inverse, gain_ref[0:1, :], upstream)
    gain_grad_ref[...] += gain_grad
    share(step, blocks, grad_ref[...] + grad_values, own_ref, other_ref)


def self_back(ids, gain, ours, theirs, came, kept, grad, w):
    rows, width = grad.shape
    blocks = rows // TB
    part = row_spec(blocks, width // 2, 3)
    return call(
        functools.partial(self_back_kernel, blocks), "self_back", SELF_BACK_MB, blocks,
        [held((3, width)), part, part, other_spec(blocks, width), kept_spec(blocks, width),
         row_spec(blocks, width), held(w.shape)],
        [
            (own_spec(blocks, width), (rows // 2, width), F32),
            (other_spec(blocks, width), (rows // 2, width), BF),
            (held((1, width)), (1, width), F32),
        ],
        [],
        6 * rows * width * width, 20 * rows * width + 6 * width * width,
    )(ids, gain, ours, theirs, came, kept, grad, w)


def flip_bit(values, bit):
    size = lax.axis_size("dp")
    return lax.ppermute(values, "dp", [(i, i ^ (1 << bit)) for i in range(size)])


def flip_mp(values):
    return lax.ppermute(values, "mp", [(0, 1), (1, 0)])


class Steps:
    def send(self, *parts):
        self.sent = [part[0] for part in parts]
        self.bits = [part[1] for part in parts]

    def launch(self):
        self.state = [flip_mp(a) if bit is None else flip_bit(a, bit) for a, bit in zip(self.sent, self.bits)]


def begin(value, *steps):
    value, sent = lax.optimization_barrier((value, [s.sent for s in steps]))
    for step, arrays in zip(steps, sent):
        step.sent = arrays
        step.launch()
    return value


def hold(value, *steps):
    value, states = lax.optimization_barrier((value, [s.state for s in steps]))
    for step, state in zip(steps, states):
        step.state = state
    return value


class Swap(Steps):
    def __init__(self, sent):
        self.send((sent, None))


class Gather(Steps):
    def __init__(self, shard):
        self.shard = shard
        self.low_c = None
        self.send((shard, 3))

    def second(self):
        self.low = jnp.stack([self.shard, self.state[0]])
        self.send((self.low, 2))

    def third(self):
        (self.high,) = self.state
        self.send((self.low, None), (self.high, 1))

    def fourth(self):
        self.low_x, self.high_y = self.state
        self.send((jnp.stack([self.low, self.low_x]), 1), (jnp.stack([self.high, self.high_y]), None))

    def over_cores(self):
        self.low_c = flip_bit(self.low, 0)
        self.high_c = flip_bit(self.high, 0)

    def pieces(self):
        low_y, high_x = self.state
        if self.low_c is None:
            self.over_cores()
        return [
            self.low, self.low_x, low_y, self.high, self.high_y, high_x,
            self.low_c, flip_bit(self.low_x, 0), flip_bit(low_y, 0),
            self.high_c, flip_bit(self.high_y, 0), flip_bit(high_x, 0),
        ]


class WideGather(Steps):
    def __init__(self, proj, out):
        self.shard = jnp.concatenate([proj, out])
        self.send((proj, None), (out, None))

    def split(self):
        both = jnp.stack([self.shard, jnp.concatenate(self.state)])
        cut = both.shape[-1] * 5 // 8
        return WidePart(both[..., :cut], 3), WidePart(both[..., cut:], 1)


class WidePart(Steps):
    def __init__(self, near, bit):
        self.near = near
        self.send((near, bit))

    def flip(self, bit):
        self.near = jnp.stack([self.near, self.state[0]])
        self.send((self.near, bit))

    def pieces(self):
        near = [self.near, self.state[0]]
        return near + [flip_bit(piece, 0) for piece in near]


class Scatter(Steps):
    def __init__(self, keep, send):
        self.keep = keep
        self.send((send, 0))

    def own(self, *at):
        return self.keep[at].astype(F32) + self.came[at].astype(F32)

    def second(self):
        (self.came,) = self.state
        low = self.keep[1, :, 0] + self.came[1, :, 0]
        high = self.keep[:, 1, 1] + self.came[:, 1, 1]
        self.send((low, 1), (high, None))

    def third(self):
        low_y, high_x = self.state
        self.kept = (low_y, high_x)
        self.send(
            ((self.own(0, 1, 0) + low_y[1].astype(F32)).astype(BF), None),
            ((self.own(1, 0, 1) + high_x[1].astype(F32)).astype(BF), 1),
        )

    def fourth(self):
        low_y, high_x = self.kept
        low_x, high_y = self.state
        high = self.own(0, 0, 1) + high_x[0].astype(F32) + high_y.astype(F32)
        self.kept = self.own(0, 0, 0) + low_y[0].astype(F32) + low_x.astype(F32)
        self.send((high.astype(BF), 2))

    def fifth(self):
        self.kept = self.kept + self.state[0].astype(F32)
        self.send((self.kept[1].astype(BF), 3))

    def total(self):
        return self.kept[0] + self.state[0].astype(F32)


class SideScatter(Steps):
    def __init__(self, keep, send):
        self.kept = keep
        self.send((send, 0))

    def take(self):
        self.kept = self.kept.astype(F32) + self.state[0].astype(F32)

    def flip(self, bit, more=None):
        self.take()
        if more is not None:
            self.kept = self.kept + more.astype(F32)
        self.send((self.kept[1].astype(BF), bit))
        self.kept = self.kept[0]

    def across(self):
        self.take()
        self.send((self.kept.astype(BF), None))


def gather_whole(shard):
    n, rows, cols = shard.shape
    dp = lax.axis_size("dp")
    mp = lax.axis_size("mp")
    pieces = lax.all_gather(shard, ("dp", "mp"), axis=0).reshape(dp, mp, n, rows, cols)
    return pieces.transpose(2, 0, 3, 1, 4).reshape(n, dp * rows, mp * cols)


def scatter_whole(grads):
    dp = lax.axis_size("dp")
    mp = lax.axis_size("mp")
    n, rows, cols = grads.shape
    pieces = grads.reshape(n, dp, rows // dp, mp, cols // mp).transpose(1, 3, 0, 2, 4)
    pieces = pieces.reshape((dp * mp,) + pieces.shape[2:])
    return lax.psum_scatter(pieces, ("dp", "mp"), scatter_dimension=0, tiled=True)[0].astype(F32)


class Sum(Steps):
    def __init__(self, values, bit):
        self.values = values
        self.send((values, bit))

    def flip(self, bit):
        self.take()
        self.send((self.values, bit))

    def take(self):
        self.values = self.values + self.state[0]


def other_row(pair_rows, me):
    return lax.dynamic_index_in_dim(pair_rows, 1 - me, 0, False)


def both_halves(own, came, me):
    came = came.astype(F32)
    return jnp.where(me == 0, jnp.stack([own, came]), jnp.stack([came, own]))


def per_device(
    tokens,
    memory,
    doc_lengths,
    mem_lengths,
    norm_gains,
    rel_table,
    self_proj,
    self_out,
    cross_proj,
    cross_out,
    ffn_proj,
    ffn_out,
    cotangent,
):
    me = lax.axis_index("mp")
    dp = lax.axis_size("dp")
    width = tokens.shape[2]
    packed = dp == 1 << BITS and lax.axis_size("mp") == 2
    place = lax.axis_index("dp")
    reverse = sum(((place >> i) & 1) << (BITS - 1 - i) for i in range(BITS))
    ids = jnp.stack([reverse, me, place]).astype(jnp.int32)
    band = bias_band(rel_table)
    pairs = width // LANES
    x_swap = Swap(other_row(tokens, me))
    shard_mid = jnp.concatenate([self_out.T[None], cross_proj, cross_out.T[None]])
    mem_swap = Swap(other_row(memory, me))

    if packed:
        w_one = Gather(self_proj)
        w_ffn = WideGather(ffn_proj, ffn_out.T[None])
        w_one.launch()
        x_swap.launch()
        shard_mid, w_ffn.sent, mem_swap.sent, ids, band, cotangent = hold(
            (shard_mid, w_ffn.sent, mem_swap.sent, ids, band, cotangent), w_one
        )
        w_one.second()
        cot_swap = Swap(other_row(cotangent, me))
        begin((), w_one)
        shard_mid, cot_swap.sent = hold((shard_mid, cot_swap.sent), w_one)
        w_two = Gather(shard_mid)
        w_one.third()
        begin((), w_one, w_two)
        hold((), w_one, x_swap)
        w_one.fourth()
        begin((), w_one)
        w_one.over_cores()
        hold((), w_one, w_two)
        w_self = w_one.pieces()
        w_two.second()
        w_self = begin(w_self, w_two, w_ffn)
    else:
        cot_swap = Swap(other_row(cotangent, me))
        begin((), x_swap, mem_swap, cot_swap)
        w_self = [gather_whole(self_proj)]
        w_mid = [gather_whole(shard_mid)]
        w_ffn = gather_whole(jnp.concatenate([ffn_proj, ffn_out.T[None]]))
        w_ffn = [w_ffn.reshape(3, width, 2, -1).transpose(2, 0, 1, 3)]
    x = (x_swap.state[0], tokens)
    normed_one_t, qkv, w_self = project(packed, ids, norm_gains, *x, w_self)
    if packed:
        qkv = hold(qkv, w_two, w_ffn)
        w_two.third()
        left, right = w_ffn.split()
        qkv = begin(qkv, w_two, left, right, mem_swap)
    parts = ((qkv, 0), (qkv, pairs), (qkv, 2 * pairs))
    self_args = (True, ids, doc_lengths, band)
    if packed:
        mixed = attention_forward(*self_args, *parts, width, 0, pairs // 2)
        mixed = hold(mixed, w_two, left, right)
        w_two.fourth()
        left.flip(2)
        mixed = begin(mixed, w_two, left)
        w_two.over_cores()
        mixed_self, qa_self = attention_forward(*self_args, *parts, width, pairs // 2, pairs, mixed)
        mixed_self = hold(mixed_self, mem_swap, w_two, left)
        w_mid = w_two.pieces()
        left.flip(1)
        right.flip(3)
        mixed_self, w_mid = begin((mixed_self, w_mid), left, right, cot_swap)
    else:
        mixed_self, qa_self = attention_forward(*self_args, *parts, width)
    mem = (mem_swap.state[0], memory)
    resid_two, normed_two_t, mem_t, q_cross, k_cross, v_cross, w_mid = middle(
        packed, ids, norm_gains, *x, mixed_self, *mem, w_mid
    )
    cross_args = (False, ids, mem_lengths, band)
    if packed:
        q_cross = hold(q_cross, right)
        right.flip(2)
        q_cross = begin(q_cross, right)
    parts = ((q_cross, 0), (k_cross, 0), (v_cross, 0))
    if packed:
        mixed = attention_forward(*cross_args, *parts, width, 0, pairs - 1)
        mixed = hold(mixed, left, right, cot_swap)
        w_ffn = left.pieces() + right.pieces()
        mixed_cross, qa_cross = attention_forward(*cross_args, *parts, width, pairs - 1, pairs, mixed)
    else:
        mixed_cross, qa_cross = attention_forward(*cross_args, *parts, width)
    output, output_sent, grad_three, grad_mixed, gain_three, *ffn_grads = feed(
        packed, ids, doc_lengths, norm_gains, resid_two, mixed_cross, cot_swap.state[0], cotangent, w_mid, w_ffn
    )
    out_swap = Swap(output_sent)
    cross_args = cross_args[1:]
    parts = (qa_cross, (k_cross, 0), (v_cross, 0))
    if packed:
        ffn = Scatter(*ffn_grads)
        grad_mixed = begin(grad_mixed, out_swap, ffn)
        grads = cross_backward(*cross_args, *parts, grad_mixed, mixed_cross, 0, 1)
        grads = hold(grads, ffn)
        ffn.second()
        grads, grad_mixed = begin((grads, grad_mixed), ffn)
        grads_cross = cross_backward(*cross_args, *parts, grad_mixed, mixed_cross, 1, pairs, (grads,))
        grads_cross = hold(grads_cross, ffn)
        ffn.third()
        grads_cross = begin(grads_cross, ffn)
    else:
        begin((), out_swap)
        grads_cross = cross_backward(*cross_args, *parts, grad_mixed, mixed_cross, 0, pairs)
    grads_cross = hold(grads_cross, out_swap)
    grad_two, grad_mixed, gmem, gmem_sent, gain_two, *mid_grads = cross_back(
        packed, ids, norm_gains, grads_cross, resid_two, normed_two_t, mem_t, grad_three, mixed_cross, mixed_self, w_mid
    )
    gmem_swap = Swap(gmem_sent)
    parts = (qa_self, (qkv, pairs), (qkv, 2 * pairs))
    more = (mixed_self, normed_one_t)
    if packed:
        mid = Scatter(*mid_grads)
        hold((), ffn)
        ffn.fourth()
        grad_mixed = begin(grad_mixed, mid, gmem_swap, ffn)
        results = self_backward(1, packed, *self_args[1:], *parts, grad_mixed, *more, 0, 1)
        results = hold(results, mid)
        mid.second()
        results, grad_mixed = begin((results, grad_mixed), mid)
        d_theirs, table_theirs, *grads_theirs = self_backward(
            1, packed, *self_args[1:], *parts, grad_mixed, *more, 1, None, results
        )
        d_theirs, grads_theirs, grad_mixed = hold((d_theirs, grads_theirs, grad_mixed), mid, ffn)
        theirs = SideScatter(*grads_theirs)
        theirs.launch()
        mid.third()
        ffn.fifth()
        mid.sent, ffn.sent = hold((mid.sent, ffn.sent), theirs)
        theirs.flip(1)
        grad_mixed = begin(grad_mixed, mid, theirs, ffn)
        d_ours, table_ours, *grads_ours = self_backward(0, packed, *self_args[1:], *parts, grad_mixed, *more)
        d_ours, grads_ours = hold((d_ours, grads_ours), mid, theirs, gmem_swap, ffn)
        ours = SideScatter(*grads_ours)
        ours.launch()
        theirs.across()
        mid.fourth()
        theirs.sent, mid.sent = hold((theirs.sent, mid.sent), ours)
        ours.flip(1)
        d_ours = begin(d_ours, ours, theirs, mid)
    else:
        begin((), gmem_swap)
        d_theirs, table_theirs, *grads_theirs = self_backward(1, packed, *self_args[1:], *parts, grad_mixed, *more)
        d_ours, table_ours, *grads_ours = self_backward(0, packed, *self_args[1:], *parts, grad_mixed, *more)
    grad_x, grad_x_sent, gain_one = self_back(ids, norm_gains, d_ours, d_theirs, *x, grad_two, w_self)
    grad_x_swap = Swap(grad_x_sent)
    half_of = (jnp.arange(pairs, dtype=jnp.int32) >= pairs // 2).astype(jnp.int32)[:, None, None]
    if packed:
        grad_x_swap.sent, gain_one, table_ours, table_theirs = hold(
            (grad_x_swap.sent, gain_one, table_ours, table_theirs), mid, ours, theirs
        )
        ours.flip(2, theirs.state[0])
        mid.fifth()
        gain_one, table_ours, table_theirs = begin(
            (gain_one, table_ours, table_theirs), grad_x_swap, ours, mid
        )
    table = jnp.where(half_of == me, table_ours, table_theirs).reshape(-1, width)
    small = jnp.concatenate([gain_one, gain_two, gain_three, table])
    if packed:
        small = Sum(small, 0)
        small.launch()
        output, out_swap.state, gmem, gmem_swap.state, ffn.state = hold(
            (output, out_swap.state, gmem, gmem_swap.state, ffn.state), small
        )
        output = both_halves(output, out_swap.state[0], me)
        grad_memory = both_halves(gmem, gmem_swap.state[0], me)
        ffn_grads = ffn.total()
        ffn_grads = (ffn_grads[:2], ffn_grads[2].T)
        small.flip(1)
        small.launch()
        output, grad_memory, ffn_grads = hold((output, grad_memory, ffn_grads), ours, small)
        small.flip(2)
        ours.flip(3)
        begin((), small, ours)
        hold((), small, mid)
        small.flip(3)
        small.launch()
        hold((), small, grad_x_swap)
        small.flip(None)
        small.launch()
        mid_grads = mid.total()
        ours.take()
        self_grads = ours.kept
        small.take()
        small = small.values
    else:
        begin((), grad_x_swap)
        output = both_halves(output, out_swap.state[0], me)
        grad_memory = both_halves(gmem, gmem_swap.state[0], me)
        ffn_grads = scatter_whole(ffn_grads[0].transpose(1, 2, 0, 3).reshape(3, width, -1))
        ffn_grads = (ffn_grads[:2], ffn_grads[2].T)
        mid_grads = scatter_whole(mid_grads[0])
        self_grads = scatter_whole(
            jnp.where(
                me == 0,
                jnp.concatenate([grads_ours[0], grads_theirs[0]], axis=2),
                jnp.concatenate([grads_theirs[0], grads_ours[0]], axis=2),
            )
        )
        small = lax.psum(small, ("dp", "mp"))
    table = small[3:].reshape(pairs, -1, LANES)[:, :2, :NB].reshape(2 * pairs, NB).T
    grad_tokens = both_halves(grad_x, grad_x_swap.state[0], me)
    return (
        output,
        grad_tokens,
        grad_memory,
        small[:3],
        table,
        self_grads,
        mid_grads[0].T,
        mid_grads[1:4],
        mid_grads[4].T,
        *ffn_grads,
    )


def solution(mesh):
    rows = P("dp", "mp", None)
    proj = P(None, "dp", "mp")
    out = P("mp", "dp")
    return jax.shard_map(
        per_device,
        mesh=mesh,
        in_specs=(rows, rows, P("dp", None), P("dp"), P(), P(), proj, out, proj, out, proj, out, rows),
        out_specs=(rows, rows, rows, P(), P(), proj, out, proj, out, proj, out),
        check_vma=False,
    )
```
